32 devices in a mesh: ctx: 4 (over y, x), fsdp: 8 (over z, core).
Axes of the slice: x: 2, y: 2, z: 4, core: 2. Of those that a mesh axis runs over, the one named last changes fastest.
Arguments:
- hidden_in: bfloat16 [8, 1024, 1536], P('fsdp', 'ctx'), may hold values from -6 to 6
- cotangent: bfloat16 [8, 1024, 1536], P('fsdp', 'ctx'), may hold values from -6 to 6
- norm_mix: bfloat16 [1536], P('fsdp'), may hold values from 0.25 to 1.75
- in_proj: bfloat16 [4608, 1536], P('fsdp'), may hold values from -0.15625 to 0.15625
- conv_kernel: bfloat16 [1536, 3], P('fsdp'), may hold values from -3.5 to 3.5
- out_proj: bfloat16 [1536, 1536], P('fsdp'), may hold values from -0.15625 to 0.15625
- norm_ff1: bfloat16 [1536], P('fsdp'), may hold values from 0.25 to 1.75
- gate1: bfloat16 [6912, 1536], P('fsdp'), may hold values from -0.15625 to 0.15625
- up1: bfloat16 [6912, 1536], P('fsdp'), may hold values from -0.15625 to 0.15625
- down1: bfloat16 [6912, 1536], P('fsdp'), may hold values from -0.078125 to 0.078125
- norm_attn: bfloat16 [1536], P('fsdp'), may hold values from 0.25 to 1.75
- q_proj: bfloat16 [1536, 1536], P('fsdp'), may hold values from -0.15625 to 0.15625
- key_projection: bfloat16 [512, 1536], P('fsdp'), may hold values from -0.15625 to 0.15625
- value_projection: bfloat16 [512, 1536], P('fsdp'), may hold values from -0.15625 to 0.15625
- q_norm: bfloat16 [64], P('fsdp'), may hold values from 0.25 to 1.75
- k_norm: bfloat16 [64], P('fsdp'), may hold values from 0.25 to 1.75
- o_proj: bfloat16 [1536, 1536], P('fsdp'), may hold values from -0.4375 to 0.4375
- norm_ff2: bfloat16 [1536], P('fsdp'), may hold values from 0.25 to 1.75
- gate2: bfloat16 [6912, 1536], P('fsdp'), may hold values from -0.15625 to 0.15625
- up2: bfloat16 [6912, 1536], P('fsdp'), may hold values from -0.15625 to 0.15625
- down2: bfloat16 [6912, 1536], P('fsdp'), may hold values from -0.078125 to 0.078125
Outputs:
- hidden_out: bfloat16 [8, 1024, 1536], P('fsdp', 'ctx')
- grad_in: float32 [8, 1024, 1536], P('fsdp', 'ctx')
- grad_norm_mix: float32 [1536], P('fsdp')
- grad_in_proj: float32 [4608, 1536], P('fsdp')
- grad_conv_kernel: float32 [1536, 3], P('fsdp')
- grad_out_proj: float32 [1536, 1536], P('fsdp')
- grad_norm_ff1: float32 [1536], P('fsdp')
- grad_gate1: float32 [6912, 1536], P('fsdp')
- grad_up1: float32 [6912, 1536], P('fsdp')
- grad_down1: float32 [6912, 1536], P('fsdp')
- grad_norm_attn: float32 [1536], P('fsdp')
- grad_q_proj: float32 [1536, 1536], P('fsdp')
- grad_k_proj: float32 [512, 1536], P('fsdp')
- grad_v_proj: float32 [512, 1536], P('fsdp')
- grad_q_norm: float32 [64], P('fsdp')
- grad_k_norm: float32 [64], P('fsdp')
- grad_o_proj: float32 [1536, 1536], P('fsdp')
- grad_norm_ff2: float32 [1536], P('fsdp')
- grad_gate2: float32 [6912, 1536], P('fsdp')
- grad_up2: float32 [6912, 1536], P('fsdp')
- grad_down2: float32 [6912, 1536], P('fsdp')
The draws below stay inside these ranges and needn't reach their ends.
All inputs are finite; a program needn't handle non-finite values.
Results may differ from the reference program's by a relative error of at most 0.028.
Values may be sent and summed in bfloat16 or wider, within the bound.
A program may use at most 640 MiB of HBM per device.

```python
import jax
import jax.numpy as jnp
from jax import lax

MODEL_WIDTH = 1536
FF = 6912
QUERY_HEADS = 24
KEY_VALUE_HEADS = 8
HEAD_SIZE = 64
KW = 3
SEQ_LEN = 1024
NSEQ = 8
N_CTX = 4


def steps_of(stream_key, dims, cuts, smallest, largest):
    loudness = 1.0
    for axis_at, blocks in cuts:
        draws = jax.random.uniform(jax.random.fold_in(jax.random.fold_in(stream_key, 6), axis_at), (blocks,), jnp.float32, smallest / len(cuts), largest / len(cuts))
        loudness = loudness * jnp.repeat(jnp.exp(draws), dims[axis_at] // blocks).reshape((-1,) + (1,) * (len(dims) - 1 - axis_at))
    return loudness


def centred(key, shape, deviation, most, pieces=(), kind=jnp.bfloat16):
    values = deviation * jax.random.normal(key, shape, jnp.float32)
    if pieces:
        values = values * steps_of(key, shape, pieces, -0.22, 0.18)
    return jnp.clip(values, -most, most).astype(kind)


def setup_inputs(seed: int = 0) -> dict:
    arg_keys = jax.random.split(jax.random.key(seed), 22)
    return {
        "hidden_in": centred(arg_keys[0], (NSEQ, SEQ_LEN, MODEL_WIDTH), 1.0, 6.0, ((0, 8), (1, 4))),
        "cotangent": centred(arg_keys[1], (NSEQ, SEQ_LEN, MODEL_WIDTH), 1.0, 6.0, ((0, 8), (1, 4))),
        "norm_mix": jnp.clip(1.0 + 0.15 * jax.random.normal(arg_keys[2], (MODEL_WIDTH,), jnp.float32), 0.25, 1.75).astype(jnp.bfloat16),
        "in_proj": centred(arg_keys[3], (3 * MODEL_WIDTH, MODEL_WIDTH), MODEL_WIDTH ** -0.5, 0.15625, ((0, 8),)),
        "conv_kernel": centred(arg_keys[4], (MODEL_WIDTH, KW), KW ** -0.5, 3.5, ((0, 8),)),
        "out_proj": centred(arg_keys[5], (MODEL_WIDTH, MODEL_WIDTH), MODEL_WIDTH ** -0.5, 0.15625, ((0, 8),)),
        "norm_ff1": jnp.clip(1.0 + 0.15 * jax.random.normal(arg_keys[6], (MODEL_WIDTH,), jnp.float32), 0.25, 1.75).astype(jnp.bfloat16),
        "gate1": centred(arg_keys[7], (FF, MODEL_WIDTH), MODEL_WIDTH ** -0.5, 0.15625, ((0, 8),)),
        "up1": centred(arg_keys[8], (FF, MODEL_WIDTH), MODEL_WIDTH ** -0.5, 0.15625, ((0, 8),)),
        "down1": centred(arg_keys[9], (FF, MODEL_WIDTH), FF ** -0.5, 0.078125, ((0, 8),)),
        "norm_attn": jnp.clip(1.0 + 0.15 * jax.random.normal(arg_keys[10], (MODEL_WIDTH,), jnp.float32), 0.25, 1.75).astype(jnp.bfloat16),
        "q_proj": centred(arg_keys[11], (QUERY_HEADS * HEAD_SIZE, MODEL_WIDTH), MODEL_WIDTH ** -0.5, 0.15625, ((0, 8),)),
        "key_projection": centred(arg_keys[12], (KEY_VALUE_HEADS * HEAD_SIZE, MODEL_WIDTH), MODEL_WIDTH ** -0.5, 0.15625, ((0, 8),)),
        "value_projection": centred(arg_keys[13], (KEY_VALUE_HEADS * HEAD_SIZE, MODEL_WIDTH), MODEL_WIDTH ** -0.5, 0.15625, ((0, 8),)),
        "q_norm": jnp.clip(1.0 + 0.15 * jax.random.normal(arg_keys[14], (HEAD_SIZE,), jnp.float32), 0.25, 1.75).astype(jnp.bfloat16),
        "k_norm": jnp.clip(1.0 + 0.15 * jax.random.normal(arg_keys[15], (HEAD_SIZE,), jnp.float32), 0.25, 1.75).astype(jnp.bfloat16),
        "o_proj": centred(arg_keys[16], (MODEL_WIDTH, QUERY_HEADS * HEAD_SIZE), (QUERY_HEADS * HEAD_SIZE // 8) ** -0.5, 0.4375, ((0, 8),)),
        "norm_ff2": jnp.clip(1.0 + 0.15 * jax.random.normal(arg_keys[17], (MODEL_WIDTH,), jnp.float32), 0.25, 1.75).astype(jnp.bfloat16),
        "gate2": centred(arg_keys[18], (FF, MODEL_WIDTH), MODEL_WIDTH ** -0.5, 0.15625, ((0, 8),)),
        "up2": centred(arg_keys[19], (FF, MODEL_WIDTH), MODEL_WIDTH ** -0.5, 0.15625, ((0, 8),)),
        "down2": centred(arg_keys[20], (FF, MODEL_WIDTH), FF ** -0.5, 0.078125, ((0, 8),)),
    }


EPS = 1e-05
THETA = 1000000.0
NEG = -1e+30
HIGH = lax.Precision.HIGHEST

@jax.custom_vjp
def low(v):
    return lax.optimization_barrier(v.astype(jnp.bfloat16)).astype(jnp.float32)

@jax.custom_vjp
def low_back(v):
    return v

def low_keep(v):
    return (low(v), None)

def low_pass(kept, grad):
    return (grad,)

def back_keep(v):
    return (v, None)

def back_low(kept, grad):
    return (low(grad),)
low.defvjp(low_keep, low_pass)
low_back.defvjp(back_keep, back_low)

def rms_scale(value, gain):
    return value * lax.rsqrt(lax.optimization_barrier(jnp.mean(value * value, axis=-1, keepdims=True)) + EPS) * gain

def rotate(value, places):
    half_dim = value.shape[-1] // 2
    freqs = THETA ** (-jnp.arange(half_dim, dtype=jnp.float32) * 2.0 / value.shape[-1])
    angles = places[:, None] * freqs[None, :]
    cosine = jnp.cos(angles)[:, None, :]
    sine = jnp.sin(angles)[:, None, :]
    first = value[..., :half_dim]
    second = value[..., half_dim:]
    return jnp.concatenate([first * cosine - second * sine, second * cosine + first * sine], axis=-1)

def head_prep(raw, gain, places):
    width = gain.shape[0]
    heads = raw.reshape(raw.shape[0], raw.shape[1] // width, width)
    return rotate(rms_scale(heads, gain), places)

def project(value, weight):
    return jnp.einsum('rk,nk->rn', value, weight, precision=HIGH)

def feed_forward(normed, gate, up_w, down):
    gate_val = low_back(project(normed, gate))
    up_val = low_back(project(normed, up_w))
    hidden = low(jax.nn.silu(gate_val) * up_val)
    return low_back(jnp.einsum('rf,fd->rd', hidden, down, precision=HIGH))

def attend(query_rows, keys, value_rows):
    sequence_length = query_rows.shape[0]
    grouped_query_rows = query_rows.reshape(sequence_length, KEY_VALUE_HEADS, QUERY_HEADS // KEY_VALUE_HEADS, HEAD_SIZE)
    grouped_value_rows = value_rows.reshape(sequence_length, KEY_VALUE_HEADS, HEAD_SIZE)
    scores = jnp.einsum('rhgd,lhd->hgrl', grouped_query_rows, keys, precision=HIGH)
    scores = low_back(scores * HEAD_SIZE ** (-0.5))
    places = jnp.arange(sequence_length, dtype=jnp.int32)
    allowed = places[:, None] >= places[None, :]
    scores = jnp.where(allowed, scores, NEG)
    probs = jax.nn.softmax(scores, axis=-1)
    out = jnp.einsum('hgrl,lhd->rhgd', low(probs), grouped_value_rows, precision=HIGH)
    return out.reshape(sequence_length, QUERY_HEADS * HEAD_SIZE)

def forward_one(params, start):
    norm_mix, in_proj, conv_kernel, out_proj, norm_ff1, gate1, up1, down1, norm_attn, q_proj, key_projection, value_projection, q_norm, k_norm, o_proj, norm_ff2, gate2, up2, down2 = params
    places = jnp.arange(SEQ_LEN, dtype=jnp.int32).astype(jnp.float32)
    normed = low(rms_scale(start, norm_mix))
    projected = low_back(project(normed, in_proj))
    b_part, c_part, x_part = jnp.split(projected, 3, axis=-1)
    mixed = low(b_part * x_part)
    padded = jnp.pad(mixed, ((KW - 1, 0), (0, 0)))
    conv_out = padded[0:SEQ_LEN] * conv_kernel[:, 0]
    for place in range(1, KW):
        conv_out = conv_out + padded[place:place + SEQ_LEN] * conv_kernel[:, place]
    gated = low(c_part * conv_out)
    first = start + low_back(project(gated, out_proj))
    second = first + feed_forward(low(rms_scale(first, norm_ff1)), gate1, up1, down1)
    normed_attn = low(rms_scale(second, norm_attn))
    query_rows = low(head_prep(low_back(project(normed_attn, q_proj)), q_norm, places))
    keys = low(head_prep(low_back(project(normed_attn, key_projection)), k_norm, places))
    value_rows = low(low_back(project(normed_attn, value_projection)))
    attended = low(low_back(attend(query_rows, keys, value_rows)))
    third = second + low_back(project(attended, o_proj))
    return third + feed_forward(low(rms_scale(third, norm_ff2)), gate2, up2, down2)

def forward(params, start):
    return lax.map(jax.checkpoint(lambda one: forward_one(params, one)), start)

def stored_places():
    block = SEQ_LEN // (2 * N_CTX)
    token_rows = jnp.arange(SEQ_LEN, dtype=jnp.int32)
    device = token_rows // (2 * block)
    within = token_rows % (2 * block)
    which = jnp.where(within < block, device, 2 * N_CTX - 1 - device)
    return (which * block + within % block).astype(jnp.int32)

def reference(hidden_in, cotangent, norm_mix, in_proj, conv_kernel, out_proj, norm_ff1, gate1, up1, down1, norm_attn, q_proj, key_projection, value_projection, q_norm, k_norm, o_proj, norm_ff2, gate2, up2, down2):
    place_of_row = stored_places()
    row_of_place = jnp.argsort(place_of_row).astype(jnp.int32)
    start = jnp.take(hidden_in.astype(jnp.float32), row_of_place, axis=1)
    seed_grad = jnp.take(cotangent.astype(jnp.float32), row_of_place, axis=1)
    params = tuple((w.astype(jnp.float32) for w in (norm_mix, in_proj, conv_kernel, out_proj, norm_ff1, gate1, up1, down1, norm_attn, q_proj, key_projection, value_projection, q_norm, k_norm, o_proj, norm_ff2, gate2, up2, down2)))
    result, back = jax.vjp(forward, params, start)
    grads, grad_start = back(seed_grad)
    hidden_out = jnp.take(result, place_of_row, axis=1).astype(jnp.bfloat16)
    grad_in = jnp.take(grad_start, place_of_row, axis=1)
    return (hidden_out, grad_in, grads[0], grads[1], grads[2], grads[3], grads[4], grads[5], grads[6], grads[7], grads[8], grads[9], grads[10], grads[11], grads[12], grads[13], grads[14], grads[15], grads[16], grads[17], grads[18])
```

```python
from functools import partial

import jax
import jax.numpy as jnp
from jax import lax
from jax.experimental import pallas as pl
from jax.experimental.pallas import tpu as pltpu
from jax.sharding import PartitionSpec as P

MODEL_WIDTH = 1536
QUERY_HEADS = 24
KEY_VALUE_HEADS = 8
HEAD_SIZE = 64
KW = 3


EPS = 1e-05
THETA = 1000000.0
NEG = -1e30


def extended_2(array, sides, width):
    for axis, dim in sides:
        size, length = (lax.axis_size(axis), array.shape[dim])
        up = [(i, (i + 1) % size) for i in range(size - 1)]
        down = [(j, i) for i, j in up]
        last = lax.slice_in_dim(array, length - width, length, axis=dim)
        first = lax.slice_in_dim(array, 0, width, axis=dim)
        before = lax.ppermute(last, axis, up)
        after = lax.ppermute(first, axis, down)
        array = jnp.concatenate([before, array, after], axis=dim)
    return array


def rms_scale(value, gain):
    return value * lax.rsqrt(jnp.mean(value * value, axis=-1, keepdims=True) + EPS) * gain


def rotate(value, places):
    half_dim = value.shape[-1] // 2
    freqs = THETA ** (-jnp.arange(half_dim, dtype=jnp.float32) * 2.0 / value.shape[-1])
    angles = places[:, None] * freqs[None, :]
    cosine = jnp.cos(angles)[:, None, :]
    sine = jnp.sin(angles)[:, None, :]
    first = value[..., :half_dim]
    second = value[..., half_dim:]
    return jnp.concatenate(
        [first * cosine - second * sine, second * cosine + first * sine], axis=-1
    )


def head_prep(raw, gain, places):
    width = gain.shape[0]
    heads = raw.reshape(raw.shape[0], raw.shape[1] // width, width)
    return rotate(rms_scale(heads, gain), places)


def dot_rows(left, right):
    return lax.dot_general(
        left, right, (((1,), (1,)), ((), ())), preferred_element_type=jnp.float32
    )


def dot_cols(left, right):
    return lax.dot_general(
        left, right, (((0,), (0,)), ((), ())), preferred_element_type=jnp.float32
    )


def dot_plain(left, right):
    return jnp.dot(left, right, preferred_element_type=jnp.float32)


def swish_product(gate_val, up_val):
    return jax.nn.silu(gate_val) * up_val


def dealt_places(index, block, ctx_count):
    device = index // (2 * block)
    within = index % (2 * block)
    which = jnp.where(within < block, device, 2 * ctx_count - 1 - device)
    return which * block + within % block


def conv_apply(extended, kernel):
    sequence_length = extended.shape[0] - KW + 1
    total = extended[0:sequence_length] * kernel[:, 0]
    for place in range(1, KW):
        total = total + extended[place : place + sequence_length] * kernel[:, place]
    return total


def conv_input_grad(grad_conv, kernel):
    sequence_length = grad_conv.shape[0] + KW - 1
    padded = jnp.pad(grad_conv, ((KW - 1, KW - 1), (0, 0)))
    total = padded[KW - 1 : KW - 1 + sequence_length] * kernel[:, 0]
    for place in range(1, KW):
        total = total + padded[KW - 1 - place : KW - 1 - place + sequence_length] * kernel[:, place]
    return total


def kernel_grad(extended, grad_conv):
    sequence_length = grad_conv.shape[0]
    columns = [
        jnp.sum(grad_conv * extended[place : place + sequence_length], axis=0)
        for place in range(KW)
    ]
    return jnp.stack(columns, axis=1)


def masked_scores(query_narrow, grouped_key_rows, query_places, key_places):
    scores = jnp.einsum(
        "rhgd,lhd->hgrl", query_narrow, grouped_key_rows, preferred_element_type=jnp.float32
    )
    scores = scores * query_narrow.shape[-1] ** (-0.5)
    allowed = query_places[:, None] >= key_places[None, :]
    return jnp.where(allowed, scores, NEG)


def ff_weight_grads(inputs, grad_out, hidden, gate_low, up_low):
    inputs, grad_out, hidden, gate_low, up_low = [
        one.reshape(-1, one.shape[-1]) for one in (inputs, grad_out, hidden, gate_low, up_low)
    ]
    return (
        dot_cols(gate_low, inputs).astype(jnp.bfloat16),
        dot_cols(up_low, inputs).astype(jnp.bfloat16),
        dot_cols(hidden, grad_out).astype(jnp.bfloat16),
    )


def pick(value, index, axis):
    return lax.dynamic_index_in_dim(value, index, axis, keepdims=False)


def ring_sources():
    size = lax.axis_size("fsdp")
    place = lax.axis_index("fsdp")
    shard = jnp.arange(size, dtype=jnp.int32)
    hops = (place // 2 - shard // 2) % (size // 2)
    return 2 * hops + (shard + place) % 2


MESH = pl.DeviceIdType.MESH


def dims_nt(left, right):
    return lax.dot_general(
        left, right, (((1,), (1,)), ((), ())), preferred_element_type=jnp.float32
    )


def ff_kernel(chips, mode, *refs):
    forward = mode == "forward"
    if forward:
        x_ref, gate, up_w, down, out, xall = refs[:6]
        rest = refs[6:]
    else:
        x_ref, y_hbm, gate, up_w, down, out, xall, hid, dgate, dup = refs[:10]
        rest = refs[10:]
    part, other_send, other_recv, sum_send, sum_recv = rest[:5]
    ag_send, ag_recv, core_send, core_recv, ps_send, ps_recv, rs_send, rs_recv = rest[5:13]
    if not forward:
        ybuf, ysem = rest[13:]
    place = lax.axis_index("fsdp")
    chip = place // 2
    core = place % 2
    after = lax.rem(chip + 1, chips) * 2 + core
    before = lax.rem(chip + chips - 1, chips) * 2 + core
    peer = chip * 2 + 1 - core
    barrier = pltpu.get_barrier_semaphore()
    for target in (before, peer):
        pl.semaphore_signal(barrier, inc=1, device_id={"fsdp": target}, device_id_type=MESH)
    pl.semaphore_wait(barrier, 2)

    def remote(src, dst, send, recv, target):
        return pltpu.make_async_remote_copy(
            src_ref=src, dst_ref=dst, send_sem=send, recv_sem=recv,
            device_id={"fsdp": target}, device_id_type=MESH,
        )

    def ring_copy(k):
        return remote(xall.at[k, 0], xall.at[k + 1, 0], ag_send.at[k], ag_recv.at[k + 1], after)

    def core_copy(k):
        return remote(xall.at[k, 0], xall.at[k, 1], core_send.at[k], core_recv.at[k], peer)

    def part_copy(k):
        return remote(other_send.at[k], other_recv.at[k], ps_send.at[k], ps_recv.at[k], peer)

    def sum_copy(k):
        return remote(sum_send.at[k], sum_recv.at[k], rs_send.at[k], rs_recv.at[k], after)

    def y_copy(k, o):
        return pltpu.make_async_copy(y_hbm.at[k, o], ybuf.at[o], ysem.at[o])

    def block(k, o):
        x = xall[k, o]
        if forward:
            gate_val = dims_nt(x, gate[...])
            up_val = dims_nt(x, up_w[...])
            hidden = (gate_val / (1.0 + jnp.exp(-gate_val)) * up_val).astype(jnp.bfloat16)
            return jnp.dot(hidden, down[...], preferred_element_type=jnp.float32)
        y_copy(k, o).wait()
        y = ybuf[o]
        a, g = (x, y) if mode == "both" else (y, x)
        gate_val = dims_nt(a, gate[...])
        up_val = dims_nt(a, up_w[...])
        grad_hidden = dims_nt(g, down[...])
        sig = 1.0 / (1.0 + jnp.exp(-gate_val))
        act = gate_val * sig
        hid[k, o] = (act * up_val).astype(jnp.bfloat16)
        dup[k, o] = (grad_hidden * act).astype(jnp.bfloat16)
        dgate[k, o] = (
            grad_hidden * up_val * (sig * (1.0 + gate_val * (1.0 - sig)))
        ).astype(jnp.bfloat16)
        return jnp.dot(dgate[k, o], gate[...], preferred_element_type=jnp.float32) + jnp.dot(
            dup[k, o], up_w[...], preferred_element_type=jnp.float32
        )

    xall[0, 0] = x_ref[...]

    @pl.loop(0, chips)
    def _(k):
        if not forward:
            y_copy(k, 0).start()
            y_copy(k, 1).start()

        @pl.when(k > 0)
        def _():
            ring_copy(k - 1).wait_recv()

        @pl.when(k < chips - 1)
        def _():
            ring_copy(k).start()

        core_copy(k).start()
        own = jnp.minimum(k, 1)

        @pl.loop(0, 2)
        def _(o):
            @pl.when(o == 1)
            def _():
                core_copy(k).wait_recv()

            value = block(k, o)

            @pl.when(o == 0)
            def _():
                part[own] = value

            @pl.when(o == 1)
            def _():
                other_send[k] = value.astype(jnp.bfloat16)
                part_copy(k).start()

        @pl.when(k > 0)
        def _():
            part_copy(k).wait_recv()

            @pl.when(k == 1)
            def _():
                sum_send[k] = (part[1] + other_recv[k].astype(jnp.float32)).astype(jnp.bfloat16)

            @pl.when(k > 1)
            def _():
                sum_copy(k - 1).wait_recv()
                sum_send[k] = (
                    part[1]
                    + other_recv[k].astype(jnp.float32)
                    + sum_recv[k - 1].astype(jnp.float32)
                ).astype(jnp.bfloat16)

            sum_copy(k).start()

    part_copy(0).wait_recv()
    sum_copy(chips - 1).wait_recv()
    out[...] = (
        part[0] + other_recv[0].astype(jnp.float32) + sum_recv[chips - 1].astype(jnp.float32)
    )

    @pl.loop(0, chips)
    def _(k):
        core_copy(k).wait_send()
        part_copy(k).wait_send()

        @pl.when(k < chips - 1)
        def _():
            ring_copy(k).wait_send()

        @pl.when(k > 0)
        def _():
            sum_copy(k).wait_send()


def ff_call(mode, ident, x, gate, up_w, down, given=None):
    chips = lax.axis_size("fsdp") // 2
    rows, width = x.shape
    units = gate.shape[0]
    forward = mode == "forward"
    blocks = jax.ShapeDtypeStruct((chips, 2, rows, width), jnp.bfloat16)
    inner = jax.ShapeDtypeStruct((chips, 2, rows, units), jnp.bfloat16)
    vmem = pl.BlockSpec(memory_space=pltpu.VMEM)
    outs = [jax.ShapeDtypeStruct((rows, width), jnp.float32), blocks]
    args = [x, gate, up_w, down]
    specs = [vmem] * 4
    dma = pltpu.SemaphoreType.DMA
    scratch = [pltpu.VMEM((2, rows, width), jnp.float32)]
    scratch += [pltpu.VMEM((chips, rows, width), jnp.bfloat16)] * 4
    scratch += [dma((chips,))] * 8
    if not forward:
        outs += [inner] * 3
        args.insert(1, given)
        specs.insert(1, pl.BlockSpec(memory_space=pl.ANY))
        scratch += [pltpu.VMEM((2, rows, width), jnp.bfloat16), dma((2,))]
    total = chips * 2 * rows
    products = 3 if forward else 5
    return pl.pallas_call(
        partial(ff_kernel, chips, mode),
        out_shape=outs,
        in_specs=specs,
        out_specs=[vmem] * len(outs),
        scratch_shapes=scratch,
        compiler_params=pltpu.CompilerParams(
            collective_id=ident, has_side_effects=True, vmem_limit_bytes=60 * 2**20
        ),
        cost_estimate=pl.CostEstimate(
            flops=2 * products * total * units * width,
            bytes_accessed=4 * total * width,
            transcendentals=total * units,
        ),
    )(*args)


def places():
    count = lax.axis_size("fsdp") // 2
    place = lax.axis_index("fsdp")
    chip = place // 2
    core = place % 2
    after = lax.rem(chip + 1, count) * 2 + core
    before = lax.rem(chip + count - 1, count) * 2 + core
    return place, chip, core, after, before, chip * 2 + 1 - core


def greet(targets):
    barrier = pltpu.get_barrier_semaphore()
    for target in targets:
        pl.semaphore_signal(barrier, inc=1, device_id=target, device_id_type=MESH)
    pl.semaphore_wait(barrier, len(targets))


def push(src, dst, send, recv, target):
    return pltpu.make_async_remote_copy(
        src_ref=src, dst_ref=dst, send_sem=send, recv_sem=recv,
        device_id=target, device_id_type=MESH,
    )


def head_kernel(chips, count, *refs):
    shards = refs[:2]
    block, vector = refs[2:4]
    wholes = refs[4:6]
    blocks, vectors = refs[6:8]
    local, near_s, near_r, hop_s, hop_r, side_s, side_r, pass_s, pass_r = refs[8:]
    place, chip, core, after, before, peer = places()
    here = lax.axis_index("ctx")
    others = [{"ctx": lax.rem(here + t, count)} for t in range(1, count)]
    greet([{"fsdp": before}, {"fsdp": peer}] + others)
    started = []

    def go(copy):
        copy.start()
        started.append(copy)

    def shard_of(k):
        return lax.rem(chip + chips - k, chips) * 2 + core

    def hop(k, n):
        owner = shard_of(k)
        if n < 2:
            src = shards[n].at[here] if k == 0 else wholes[n].at[owner, here]
            dst = wholes[n].at[owner, here]
        elif n == 2:
            src = block if k == 0 else blocks.at[k, 0]
            dst = blocks.at[k + 1, 0]
        else:
            src = vector if k == 0 else vectors.at[owner]
            dst = vectors.at[owner]
        return push(src, dst, hop_s.at[n, k], hop_r.at[n, k], {"fsdp": after})

    def side(k, t, n):
        piece = wholes[n].at[shard_of(k), here]
        return push(piece, piece, side_s.at[n, k, t], side_r.at[n, k, t], others[t - 1])

    def side_in(k, t, n):
        piece = wholes[n].at[shard_of(k), lax.rem(here + count - t, count)]
        return piece, push(piece, piece, side_s.at[n, k, t], side_r.at[n, k, t], others[t - 1])

    def across(k, t, n):
        if n == 2:
            src, dst = blocks.at[k, 0], blocks.at[k, 1]
        elif n == 3:
            src = dst = vectors.at[shard_of(k)]
        else:
            src = dst = wholes[n].at[shard_of(k), lax.rem(here + count - t, count)]
        return push(src, dst, pass_s.at[n, k, t], pass_r.at[n, k, t], {"fsdp": peer})

    def across_in(k, t, n):
        owner = lax.rem(chip + chips - k, chips) * 2 + 1 - core
        if n == 2:
            dst = blocks.at[k, 1]
        elif n == 3:
            dst = vectors.at[owner]
        else:
            dst = wholes[n].at[owner, lax.rem(here + count - t, count)]
        return push(dst, dst, pass_s.at[n, k, t], pass_r.at[n, k, t], {"fsdp": peer})

    homes = [wholes[0].at[place], wholes[1].at[place], blocks.at[0, 0], vectors.at[place]]
    far = [wholes[0].at[place], wholes[1].at[place], blocks.at[0, 1], vectors.at[place]]
    came = [wholes[0].at[peer], wholes[1].at[peer], blocks.at[0, 1], vectors.at[peer]]
    sources = [shards[0], shards[1], block, vector]
    order = (3, 0, 1, 2)
    for n in order:
        go(hop(0, n))
    keeps = [pltpu.make_async_copy(sources[n], homes[n], local.at[n]) for n in order]
    for one in keeps:
        one.start()
    for n in order:
        go(push(sources[n], far[n], near_s.at[n], near_r.at[n], {"fsdp": peer}))
    for k in range(1, chips):
        for n in order:
            hop(k - 1, n).wait_recv()
            if k < chips - 1:
                go(hop(k, n))
            if n < 2:
                for t in range(1, count):
                    go(side(k, t, n))
            go(across(k, 0, n))
        if k > 1:
            for n in range(2):
                for t in range(1, count):
                    side_in(k - 1, t, n)[1].wait_recv()
                    go(across(k - 1, t, n))
    for n in range(2):
        for t in range(1, count):
            side_in(chips - 1, t, n)[1].wait_recv()
            go(across(chips - 1, t, n))
    for n in order:
        push(came[n], came[n], near_s.at[n], near_r.at[n], {"fsdp": peer}).wait_recv()
        for k in range(1, chips):
            for t in range(count if n < 2 else 1):
                across_in(k, t, n).wait_recv()
    for one in keeps:
        one.wait()
    for one in started:
        one.wait_send()


def head_call(ident, shard_a, shard_b, block, vector):
    size = lax.axis_size("fsdp")
    count = lax.axis_size("ctx")
    chips = size // 2
    width = shard_a.shape[1]
    shards = [one.reshape(count, -1, width) for one in (shard_a, shard_b)]
    outs = [jax.ShapeDtypeStruct((size,) + one.shape, jnp.bfloat16) for one in shards]
    outs.append(jax.ShapeDtypeStruct((chips, 2) + block.shape, jnp.bfloat16))
    outs.append(jax.ShapeDtypeStruct((size,) + vector.shape, jnp.bfloat16))
    anywhere = pl.BlockSpec(memory_space=pl.ANY)
    dma = pltpu.SemaphoreType.DMA
    whole_a, whole_b, blocks, vectors = pl.pallas_call(
        partial(head_kernel, chips, count),
        out_shape=outs,
        in_specs=[anywhere] * 4,
        out_specs=[anywhere] * 4,
        scratch_shapes=[
            dma((4,)), dma((4,)), dma((4,)),
            dma((4, chips)), dma((4, chips)),
            dma((2, chips, count)), dma((2, chips, count)),
            dma((4, chips, count)), dma((4, chips, count)),
        ],
        compiler_params=pltpu.CompilerParams(collective_id=ident, has_side_effects=True),
        cost_estimate=pl.CostEstimate(
            flops=0, bytes_accessed=2 * size * (shard_a.size + shard_b.size) * 2, transcendentals=0
        ),
    )(*shards, block, vector)
    return whole_a.reshape(-1, width), whole_b.reshape(-1, width), blocks, vectors


def tail_kernel(chips, count, pieces, *refs):
    number = len(pieces)
    grads = refs[:number]
    factor, inputs = refs[number : number + 2]
    total, total_in = refs[number + 2 : number + 4]
    own, near, out_sum, in_sum, fin, rc, fs, held, fin_in, rc_in, fs_in = refs[number + 4 : number + 15]
    (own_m, near_s, near_r, ring_s, ring_r, sc_s, sc_r, ag_s, ag_r, fac_m, fac_s, fac_r,
     sci_s, sci_r, agi_s, agi_r) = refs[number + 15 :]
    place, chip, core, after, before, peer = places()
    here = lax.axis_index("ctx")
    size = 2 * chips
    chunks = sum(pieces)
    ctx_others = [{"ctx": lax.rem(here + t, count)} for t in range(1, count)]
    shard_others = [{"fsdp": lax.rem(place + t, size)} for t in range(1, size)]
    greet(ctx_others + shard_others)

    def factor_copy(t):
        there = lax.rem(place + t, size)
        return push(factor.at[there], held.at[place], fac_s.at[t], fac_r.at[t], {"fsdp": there})

    for t in range(1, size):
        factor_copy(t).start()
    keep = pltpu.make_async_copy(factor.at[place], held.at[place], fac_m)
    keep.start()

    bases = [sum(pieces[:n]) for n in range(number)]

    def near_copy(n, j):
        at = bases[n] + j
        return push(
            grads[n].at[:, 1 - core, j], near.at[at], near_s.at[at], near_r.at[at], {"fsdp": peer}
        )

    def own_copy(n, j):
        at = bases[n] + j
        return pltpu.make_async_copy(grads[n].at[:, core, j], own.at[at], own_m.at[at])

    for n in range(number):
        @pl.loop(0, pieces[n])
        def _(j):
            near_copy(n, j).start()
            own_copy(n, j).start()

    def ring_copy(k, j):
        return push(
            out_sum.at[k, j], in_sum.at[k, j], ring_s.at[k, j], ring_r.at[k, j], {"fsdp": after}
        )

    def near_in(j):
        return push(near.at[j], near.at[j], near_s.at[j], near_r.at[j], {"fsdp": peer})

    def own_in(j):
        return pltpu.make_async_copy(own.at[j], own.at[j], own_m.at[j])

    def term(j, owner):
        return own[j, owner].astype(jnp.float32) + near[j, owner].astype(jnp.float32)

    def scatter_copy(j, t):
        there = lax.rem(here + t, count)
        return push(fin.at[j, there], rc.at[j, t], sc_s.at[j, t], sc_r.at[j, t], {"ctx": there})

    def gather_copy(j, t):
        return push(
            fs.at[j], total.at[j, here], ag_s.at[j, t], ag_r.at[j, t], ctx_others[t - 1]
        )

    def gather_in(j, t):
        there = total.at[j, lax.rem(here + count - t, count)]
        return push(there, there, ag_s.at[j, t], ag_r.at[j, t], ctx_others[t - 1])

    def scatter_in_copy(t):
        there = lax.rem(here + t, count)
        return push(fin_in.at[there], rc_in.at[t], sci_s.at[t], sci_r.at[t], {"ctx": there})

    def gather_in_copy(t):
        return push(fs_in, total_in.at[here], agi_s.at[t], agi_r.at[t], ctx_others[t - 1])

    def gather_in_wait(t):
        there = total_in.at[lax.rem(here + count - t, count)]
        return push(there, there, agi_s.at[t], agi_r.at[t], ctx_others[t - 1])

    def products():
        for t in range(1, size):
            src = held.at[lax.rem(place + size - t, size)]
            push(src, src, fac_s.at[t], fac_r.at[t], {"fsdp": peer}).wait_recv()
        keep.wait()

        @pl.loop(0, count)
        def _(c):
            sums = jnp.dot(held[0, c], inputs[0], preferred_element_type=jnp.float32)
            for s in range(1, size):
                sums = sums + jnp.dot(held[s, c], inputs[s], preferred_element_type=jnp.float32)
            fin_in[c] = sums.astype(jnp.bfloat16)

        for t in range(1, count):
            scatter_in_copy(t).start()

    def products_sum():
        sums = fin_in[here].astype(jnp.float32)
        for t in range(1, count):
            scatter_in_copy(t).wait_recv()
            sums = sums + rc_in[t].astype(jnp.float32)
        fs_in[...] = sums.astype(jnp.bfloat16)
        for t in range(1, count):
            gather_in_copy(t).start()
        total_in[here] = fs_in[...]

    @pl.loop(1, chips)
    def _(k):
        owner = lax.rem(chip + chips - k, chips)

        @pl.loop(0, chunks)
        def _(j):
            @pl.when(k == 1)
            def _():
                own_in(j).wait()
                near_in(j).wait_recv()
                out_sum[0, j] = term(j, owner).astype(jnp.bfloat16)

            @pl.when(k > 1)
            def _():
                ring_copy(k - 2, j).wait_recv()
                out_sum[k - 1, j] = (
                    term(j, owner) + in_sum[k - 2, j].astype(jnp.float32)
                ).astype(jnp.bfloat16)

            ring_copy(k - 1, j).start()

        @pl.when(k == 1)
        def _():
            products()

        @pl.when(k == 2)
        def _():
            products_sum()

    @pl.loop(0, chunks)
    def _(j):
        ring_copy(chips - 2, j).wait_recv()
        fin[j] = (term(j, chip) + in_sum[chips - 2, j].astype(jnp.float32)).astype(jnp.bfloat16)
        for t in range(1, count):
            scatter_copy(j, t).start()

    @pl.loop(0, chunks)
    def _(j):
        sums = fin[j, here].astype(jnp.float32)
        for t in range(1, count):
            scatter_copy(j, t).wait_recv()
            sums = sums + rc[j, t].astype(jnp.float32)
        fs[j] = sums.astype(jnp.bfloat16)
        for t in range(1, count):
            gather_copy(j, t).start()
        total[j, here] = fs[j]

    @pl.loop(0, chunks)
    def _(j):
        for t in range(1, count):
            gather_in(j, t).wait_recv()
            gather_copy(j, t).wait_send()
            scatter_copy(j, t).wait_send()

        near_in(j).wait_send()

        @pl.loop(0, chips - 1)
        def _(k):
            ring_copy(k, j).wait_send()

    for t in range(1, count):
        gather_in_wait(t).wait_recv()
        gather_in_copy(t).wait_send()
        scatter_in_copy(t).wait_send()
    for t in range(1, size):
        factor_copy(t).wait_send()


def tail_call(ident, grads, factor, inputs):
    size = lax.axis_size("fsdp")
    count = lax.axis_size("ctx")
    chips = size // 2
    width = inputs.shape[2]
    rows = inputs.shape[1]
    unit = min(one.shape[1] for one in grads) // 3
    pieces = [one.shape[1] // unit for one in grads]
    chunks = sum(pieces)
    part = unit // count
    views = [
        one.reshape(chips, 2, n, count, part, width) for one, n in zip(grads, pieces)
    ]
    factor = factor.T.reshape(size, count, -1, rows)
    mine = factor.shape[2]
    bf16 = jnp.bfloat16
    anywhere = pl.BlockSpec(memory_space=pl.ANY)
    vmem = pl.BlockSpec(memory_space=pltpu.VMEM)
    dma = pltpu.SemaphoreType.DMA
    total, total_in = pl.pallas_call(
        partial(tail_kernel, chips, count, pieces),
        out_shape=[
            jax.ShapeDtypeStruct((chunks, count, part, width), bf16),
            jax.ShapeDtypeStruct((count, mine, width), bf16),
        ],
        in_specs=[anywhere] * (len(views) + 1) + [vmem],
        out_specs=[vmem] * 2,
        scratch_shapes=[
            pltpu.VMEM((chunks, chips, count, part, width), bf16),
            pltpu.VMEM((chunks, chips, count, part, width), bf16),
            pltpu.VMEM((chips - 1, chunks, count, part, width), bf16),
            pltpu.VMEM((chips - 1, chunks, count, part, width), bf16),
            pltpu.VMEM((chunks, count, part, width), bf16),
            pltpu.VMEM((chunks, count, part, width), bf16),
            pltpu.VMEM((chunks, part, width), bf16),
            pltpu.VMEM((size, count, mine, rows), bf16),
            pltpu.VMEM((count, mine, width), bf16),
            pltpu.VMEM((count, mine, width), bf16),
            pltpu.VMEM((mine, width), bf16),
            dma((chunks,)), dma((chunks,)), dma((chunks,)),
            dma((chips - 1, chunks)), dma((chips - 1, chunks)),
            dma((chunks, count)), dma((chunks, count)), dma((chunks, count)), dma((chunks, count)),
            dma, dma((size,)), dma((size,)),
            dma((count,)), dma((count,)), dma((count,)), dma((count,)),
        ],
        compiler_params=pltpu.CompilerParams(
            collective_id=ident, has_side_effects=True, vmem_limit_bytes=61 * 2**20
        ),
        cost_estimate=pl.CostEstimate(
            flops=2 * size * rows * width * count * mine,
            bytes_accessed=4 * size * chunks * unit * width,
            transcendentals=0,
        ),
    )(*views, factor, inputs)
    total = total.reshape(-1, width).astype(jnp.float32)
    outs = []
    at = 0
    for one in grads:
        outs.append(total[at : at + one.shape[1]])
        at += one.shape[1]
    return outs + [total_in.reshape(-1, width).astype(jnp.float32)]


def local(
    hidden_in,
    cotangent,
    norm_mix,
    in_proj,
    conv_kernel,
    out_proj,
    norm_ff1,
    gate1,
    up1,
    down1,
    norm_attn,
    q_proj,
    key_projection,
    value_projection,
    q_norm,
    k_norm,
    o_proj,
    norm_ff2,
    gate2,
    up2,
    down2,
):
    narrow_dtype = jnp.bfloat16
    start = hidden_in[0].astype(jnp.float32)
    token_rows = start.shape[0]
    block = token_rows // 2
    margin = KW - 1
    ctx_count = lax.axis_size("ctx")
    ctx_place = lax.axis_index("ctx")
    is_last = ctx_place == ctx_count - 1
    query_places = dealt_places(
        ctx_place * token_rows + jnp.arange(token_rows, dtype=jnp.int32), block, ctx_count
    )
    key_places = dealt_places(jnp.arange(token_rows * ctx_count, dtype=jnp.int32), block, ctx_count)
    query_angles = query_places.astype(jnp.float32)
    vectors = (
        norm_mix, norm_ff1, norm_attn, norm_ff2, q_norm, k_norm, conv_kernel.reshape(-1)
    )
    lengths = [one.shape[0] for one in vectors]
    vector = jnp.concatenate(vectors)
    vector = jnp.pad(vector, (0, 2048 - sum(lengths))).reshape(16, 128)
    attn_shard = jnp.concatenate([q_proj, key_projection, value_projection, o_proj], axis=0)
    attn_rows = attn_shard.shape[0]
    attn_slice = pick(attn_shard.reshape(ctx_count, -1, MODEL_WIDTH), ctx_place, 0)
    attn_slices = lax.all_gather(attn_slice, "fsdp", axis=0)
    mix_in, mix_out, given, gathered_vectors = head_call(
        4, in_proj, out_proj, cotangent[0], vector
    )
    attn_slices, mix_in = lax.optimization_barrier((attn_slices, mix_in))
    attn_wholes = lax.all_gather(attn_slices, "ctx", axis=1)
    attn_wholes = attn_wholes.reshape(-1, attn_rows, MODEL_WIDTH)
    gathered_vectors = gathered_vectors.reshape(-1, 2048)
    wholes = []
    at = 0
    for one in lengths:
        wholes.append(gathered_vectors[:, at : at + one].reshape(-1))
        at += one
    mix_norm, ff_norm_one, attn_norm, ff_norm_two, query_gain, key_gain, mix_kernel = wholes
    mix_kernel = mix_kernel.reshape(-1, KW)
    kernel = mix_kernel.astype(jnp.float32)
    normed_one, norm_back_one = jax.vjp(rms_scale, start, mix_norm.astype(jnp.float32))
    normed_one_low = normed_one.astype(narrow_dtype)
    projected = dot_rows(normed_one_low, mix_in)
    b_part = projected[:, :MODEL_WIDTH]
    c_part = projected[:, MODEL_WIDTH : 2 * MODEL_WIDTH]
    x_part = projected[:, 2 * MODEL_WIDTH :]
    mixed_low = (b_part * x_part).astype(narrow_dtype)
    front_tail = mixed_low[block - margin : block]
    back_tail = mixed_low[token_rows - margin :]
    edges = extended_2(jnp.concatenate([back_tail, front_tail], axis=0), (("ctx", 0),), margin)
    before_front = edges[:margin]
    before_back = jnp.where(is_last, front_tail, edges[edges.shape[0] - margin :])
    front_ext = jnp.concatenate([before_front, mixed_low[:block]], axis=0).astype(jnp.float32)
    back_ext = jnp.concatenate([before_back, mixed_low[block:]], axis=0).astype(jnp.float32)
    conv_out = jnp.concatenate(
        [conv_apply(front_ext, kernel), conv_apply(back_ext, kernel)], axis=0
    )
    gated_low = (c_part * conv_out).astype(narrow_dtype)
    first = start + dot_rows(gated_low, mix_out)
    normed_two, norm_back_two = jax.vjp(rms_scale, first, ff_norm_one.astype(jnp.float32))
    ff_out_one, inputs_one = ff_call(
        "forward", 1, normed_two.astype(narrow_dtype), gate1, up1, down1
    )
    second = first + ff_out_one
    attn_parts = []
    at = 0
    for one in (q_proj, key_projection, value_projection, o_proj):
        attn_parts.append(attn_wholes[:, at : at + one.shape[0]].reshape(-1, MODEL_WIDTH))
        at += one.shape[0]
    w_query, w_key, w_value, w_output = attn_parts
    normed_three, norm_back_three = jax.vjp(rms_scale, second, attn_norm.astype(jnp.float32))
    three_low = normed_three.astype(narrow_dtype)
    query_raw = dot_rows(three_low, w_query)
    key_raw = dot_rows(three_low, w_key)
    value_raw = dot_rows(three_low, w_value)
    query_head_split, query_back = jax.vjp(
        partial(head_prep, places=query_angles), query_raw, query_gain.astype(jnp.float32)
    )
    key_head_split, key_reverse_rotation = jax.vjp(
        partial(head_prep, places=query_angles), key_raw, key_gain.astype(jnp.float32)
    )
    query_narrow = query_head_split.astype(narrow_dtype).reshape(
        token_rows, KEY_VALUE_HEADS, QUERY_HEADS // KEY_VALUE_HEADS, HEAD_SIZE
    )
    key_narrow = key_head_split.astype(narrow_dtype).reshape(
        token_rows, KEY_VALUE_HEADS * HEAD_SIZE
    )
    value_low = value_raw.astype(narrow_dtype)
    gathered = lax.all_gather(
        jnp.concatenate([key_narrow, value_low], axis=1), "ctx", axis=0, tiled=True
    )
    gathered_keys = gathered[:, : key_narrow.shape[1]]
    gathered_values = gathered[:, key_narrow.shape[1] :]
    normed_one_low, gathered = lax.optimization_barrier((normed_one_low, gathered))
    one_blocks = lax.all_gather(normed_one_low, "fsdp", axis=0)
    grouped_key_rows = gathered_keys.reshape(-1, KEY_VALUE_HEADS, HEAD_SIZE)
    grouped_value_rows = gathered_values.reshape(-1, KEY_VALUE_HEADS, HEAD_SIZE)
    scores = masked_scores(query_narrow, grouped_key_rows, query_places, key_places)
    peak = jnp.max(scores, axis=-1, keepdims=True)
    total = jnp.sum(jnp.exp(scores - peak), axis=-1, keepdims=True)
    probs_low = (jnp.exp(scores - peak) / total).astype(narrow_dtype)
    attended = jnp.einsum(
        "hgrl,lhd->rhgd", probs_low, grouped_value_rows, preferred_element_type=jnp.float32
    )
    attended_low = attended.reshape(token_rows, QUERY_HEADS * HEAD_SIZE).astype(narrow_dtype)
    third = second + dot_rows(attended_low, w_output)
    normed_four, norm_back_four = jax.vjp(rms_scale, third, ff_norm_two.astype(jnp.float32))
    grad_four, inputs_two, hidden_two, gate_low_two, up_low_two = ff_call(
        "both", 2, normed_four.astype(narrow_dtype), gate2, up2, down2, given
    )
    shards = lax.axis_size("fsdp")
    sources = ring_sources()
    outs_two = dot_plain(hidden_two.reshape(shards * token_rows, -1), down2).astype(narrow_dtype)
    outs_two = jnp.take(outs_two.reshape(shards, -1), sources, axis=0).reshape(-1, MODEL_WIDTH)
    final = third + lax.psum_scatter(
        outs_two, "fsdp", scatter_dimension=0, tiled=True
    ).astype(jnp.float32)
    grad_final = cotangent[0].astype(jnp.float32)
    two_grads = ff_weight_grads(inputs_two, given, hidden_two, gate_low_two, up_low_two)
    ff_two = [lax.psum(jnp.concatenate(two_grads, axis=0), "ctx")]
    grad_third_part, grad_ff_norm_two = norm_back_four(grad_four)
    grad_third = grad_final + grad_third_part
    output_low = grad_third.astype(narrow_dtype)
    attended_gradient = dot_plain(output_low, w_output)
    grad_w_output = (
        dot_cols(output_low, attended_low)
        .astype(narrow_dtype)
        .reshape(lax.axis_size("fsdp"), -1, MODEL_WIDTH)
    )
    attended_gradient_narrow = attended_gradient.astype(narrow_dtype).reshape(
        token_rows, KEY_VALUE_HEADS, QUERY_HEADS // KEY_VALUE_HEADS, HEAD_SIZE
    )
    scores = masked_scores(query_narrow, grouped_key_rows, query_places, key_places)
    probs = jnp.exp(scores - peak) / total
    probs_low = probs.astype(narrow_dtype)
    grad_probs = jnp.einsum(
        "rhgd,lhd->hgrl",
        attended_gradient_narrow,
        grouped_value_rows,
        preferred_element_type=jnp.float32,
    )
    weighted = jnp.sum(probs * grad_probs, axis=-1, keepdims=True)
    grad_scores = (probs * (grad_probs - weighted)).astype(narrow_dtype)
    scale = HEAD_SIZE ** (-0.5)
    grad_query = (
        jnp.einsum(
            "hgrl,lhd->rhgd", grad_scores, grouped_key_rows, preferred_element_type=jnp.float32
        )
        * scale
    )
    keys_gradient = (
        jnp.einsum("hgrl,rhgd->lhd", grad_scores, query_narrow, preferred_element_type=jnp.float32)
        * scale
    )
    values_gradient = jnp.einsum(
        "hgrl,rhgd->lhd", probs_low, attended_gradient_narrow, preferred_element_type=jnp.float32
    )
    both_grads = jnp.concatenate(
        [
            keys_gradient.reshape(-1, KEY_VALUE_HEADS * HEAD_SIZE),
            values_gradient.reshape(-1, KEY_VALUE_HEADS * HEAD_SIZE),
        ],
        axis=1,
    ).astype(jnp.bfloat16)
    both_grads = both_grads.reshape(ctx_count, token_rows, -1)
    own_grads = pick(both_grads, ctx_place, 0).astype(jnp.float32)
    for step in range(1, ctx_count):
        arrived = lax.ppermute(
            pick(both_grads, (ctx_place + step) % ctx_count, 0),
            "ctx",
            [(i, (i + step) % ctx_count) for i in range(ctx_count)],
        )
        own_grads = own_grads + arrived.astype(jnp.float32)
    local_keys = own_grads[:, : KEY_VALUE_HEADS * HEAD_SIZE]
    own_values = own_grads[:, KEY_VALUE_HEADS * HEAD_SIZE :]
    grad_query_raw, grad_query_gain = query_back(
        grad_query.reshape(token_rows, QUERY_HEADS, HEAD_SIZE)
    )
    raw_key_gradient, key_gain_gradient = key_reverse_rotation(
        local_keys.reshape(token_rows, KEY_VALUE_HEADS, HEAD_SIZE)
    )
    query_grad_low = grad_query_raw.astype(narrow_dtype)
    key_grad_low = raw_key_gradient.astype(narrow_dtype)
    value_grad_low = own_values.astype(narrow_dtype)
    grad_three = (
        dot_plain(query_grad_low, w_query)
        + dot_plain(key_grad_low, w_key)
        + dot_plain(value_grad_low, w_value)
    )
    grad_rows = [
        one.reshape(token_rows, shards, -1) for one in (query_grad_low, key_grad_low, value_grad_low)
    ]
    widths = [one.shape[2] for one in grad_rows]
    grad_rows = jnp.concatenate(grad_rows, axis=2).reshape(token_rows, -1)
    grad_w_qkv = (
        dot_cols(grad_rows, three_low).astype(narrow_dtype).reshape(shards, sum(widths), -1)
    )
    grad_second_part, grad_attn_norm = norm_back_three(grad_three)
    grad_second = grad_third + grad_second_part
    grad_two, grads_one, hidden_one, gate_low_one, up_low_one = ff_call(
        "backward", 3, grad_second.astype(narrow_dtype), gate1, up1, down1, inputs_one
    )
    one_grads = ff_weight_grads(inputs_one, grads_one, hidden_one, gate_low_one, up_low_one)
    one_packed, ff_two[0] = lax.optimization_barrier(
        (jnp.concatenate(one_grads, axis=0), ff_two[0])
    )
    ff_one = [lax.psum(one_packed, "ctx")]
    ff_one, ff_two = [
        [one[0][at : at + gate1.shape[0]].astype(jnp.float32) for at in range(0, 3 * gate1.shape[0], gate1.shape[0])]
        for one in (ff_one, ff_two)
    ]
    grad_first_part, grad_ff_norm_one = norm_back_two(grad_two)
    grad_first = grad_second + grad_first_part
    first_low = grad_first.astype(narrow_dtype)
    grad_gated = dot_plain(first_low, mix_out)
    grad_mix_out = (
        dot_cols(first_low, gated_low).astype(narrow_dtype).reshape(shards, -1, MODEL_WIDTH)
    )
    grad_c_part = grad_gated * conv_out
    grad_conv = grad_gated * c_part
    grad_front_ext = conv_input_grad(grad_conv[:block], kernel)
    grad_back_ext = conv_input_grad(grad_conv[block:], kernel)
    back_before = grad_back_ext[:margin]
    outgoing = jnp.concatenate(
        [grad_front_ext[:margin], jnp.where(is_last, 0.0, back_before)], axis=0
    )
    returned = extended_2(outgoing, (("ctx", 0),), margin)
    from_prev = returned[:margin]
    from_next = returned[returned.shape[0] - margin :]
    own_edge = jnp.where(is_last, back_before, 0.0)
    front_grad = grad_front_ext[margin:]
    back_grad = grad_back_ext[margin:]
    front_grad = jnp.concatenate(
        [front_grad[: block - margin], front_grad[block - margin :] + from_next + own_edge], axis=0
    )
    back_grad = jnp.concatenate(
        [back_grad[: block - margin], back_grad[block - margin :] + from_prev], axis=0
    )
    grad_mixed = jnp.concatenate([front_grad, back_grad], axis=0)
    grad_kernel = kernel_grad(front_ext, grad_conv[:block]) + kernel_grad(
        back_ext, grad_conv[block:]
    )
    grad_projected = jnp.concatenate(
        [grad_mixed * x_part, grad_c_part, grad_mixed * b_part], axis=-1
    ).astype(narrow_dtype)
    grad_w_qkv, grad_w_output, grad_mix_out, grad_mix_in = tail_call(
        5, [grad_w_qkv, grad_w_output, grad_mix_out], grad_projected, one_blocks
    )
    grad_w_query = grad_w_qkv[: widths[0]]
    grad_w_key = grad_w_qkv[widths[0] : widths[0] + widths[1]]
    grad_w_value = grad_w_qkv[widths[0] + widths[1] :]
    grad_one = dot_plain(grad_projected, mix_in)
    grad_start_part, grad_mix_norm = norm_back_one(grad_one)
    grad_start = grad_first + grad_start_part
    smalls = (
        grad_mix_norm,
        grad_kernel.reshape(-1),
        grad_ff_norm_one,
        grad_attn_norm,
        grad_query_gain,
        key_gain_gradient,
        grad_ff_norm_two,
    )
    small_sum = lax.psum(jnp.concatenate(smalls), ("fsdp", "ctx"))
    small_out = []
    at = 0
    shard = lax.axis_index("fsdp")
    for one in smalls:
        part = one.shape[0] // lax.axis_size("fsdp")
        small_out.append(lax.dynamic_slice_in_dim(small_sum, at + shard * part, part))
        at += one.shape[0]
    return (
        final.astype(narrow_dtype)[None],
        grad_start[None],
        small_out[0],
        grad_mix_in,
        small_out[1].reshape(-1, KW),
        grad_mix_out,
        small_out[2],
        ff_one[0],
        ff_one[1],
        ff_one[2],
        small_out[3],
        grad_w_query,
        grad_w_key,
        grad_w_value,
        small_out[4],
        small_out[5],
        grad_w_output,
        small_out[6],
        ff_two[0],
        ff_two[1],
        ff_two[2],
    )


def solution(mesh):
    in_specs = (
        P("fsdp", "ctx", None),
        P("fsdp", "ctx", None),
        P("fsdp"),
        P("fsdp", None),
        P("fsdp", None),
        P("fsdp", None),
        P("fsdp"),
        P("fsdp", None),
        P("fsdp", None),
        P("fsdp", None),
        P("fsdp"),
        P("fsdp", None),
        P("fsdp", None),
        P("fsdp", None),
        P("fsdp"),
        P("fsdp"),
        P("fsdp", None),
        P("fsdp"),
        P("fsdp", None),
        P("fsdp", None),
        P("fsdp", None),
    )
    out_specs = (
        P("fsdp", "ctx", None),
        P("fsdp", "ctx", None),
        P("fsdp"),
        P("fsdp", None),
        P("fsdp", None),
        P("fsdp", None),
        P("fsdp"),
        P("fsdp", None),
        P("fsdp", None),
        P("fsdp", None),
        P("fsdp"),
        P("fsdp", None),
        P("fsdp", None),
        P("fsdp", None),
        P("fsdp"),
        P("fsdp"),
        P("fsdp", None),
        P("fsdp"),
        P("fsdp", None),
        P("fsdp", None),
        P("fsdp", None),
    )
    return jax.shard_map(local, mesh=mesh, in_specs=in_specs, out_specs=out_specs, check_vma=False)
```

```python
from functools import partial

import jax
import jax.numpy as jnp
from jax import lax
from jax.experimental import pallas as pl
from jax.experimental.pallas import tpu as pltpu
from jax.sharding import PartitionSpec as P

MODEL_WIDTH = 1536
QUERY_HEADS = 24
KEY_VALUE_HEADS = 8
HEAD_SIZE = 64
KW = 3


EPS = 1e-05
THETA = 1000000.0
NEG = -1e30


def extended_2(array, sides, width):
    for axis, dim in sides:
        size, length = (lax.axis_size(axis), array.shape[dim])
        up = [(i, (i + 1) % size) for i in range(size - 1)]
        down = [(j, i) for i, j in up]
        last = lax.slice_in_dim(array, length - width, length, axis=dim)
        first = lax.slice_in_dim(array, 0, width, axis=dim)
        before = lax.ppermute(last, axis, up)
        after = lax.ppermute(first, axis, down)
        array = jnp.concatenate([before, array, after], axis=dim)
    return array


def rms_scale(value, gain):
    return value * lax.rsqrt(jnp.mean(value * value, axis=-1, keepdims=True) + EPS) * gain


def rotate(value, angles):
    half_dim = value.shape[1] // 2
    cosine = jnp.cos(angles)
    sine = jnp.sin(angles)
    first = value[:, :half_dim]
    second = value[:, half_dim:]
    return jnp.concatenate(
        [first * cosine - second * sine, second * cosine + first * sine], axis=1
    )


def head_prep(raw, gain, angles):
    heads = raw.reshape(-1, gain.shape[0], raw.shape[1])
    mean = jnp.mean(heads * heads, axis=1, keepdims=True)
    return rotate(heads * lax.rsqrt(mean + EPS) * gain[:, None], angles)


def dot_rows(left, right):
    return lax.dot_general(
        left, right, (((1,), (1,)), ((), ())), preferred_element_type=jnp.float32
    )


def dot_cols(left, right):
    return lax.dot_general(
        left, right, (((0,), (0,)), ((), ())), preferred_element_type=jnp.float32
    )


def dot_plain(left, right):
    return jnp.dot(left, right, preferred_element_type=jnp.float32)


def swish_product(gate_val, up_val):
    return jax.nn.silu(gate_val) * up_val


def dealt_places(index, block, ctx_count):
    device = index // (2 * block)
    within = index % (2 * block)
    which = jnp.where(within < block, device, 2 * ctx_count - 1 - device)
    return which * block + within % block


def conv_apply(extended, kernel):
    sequence_length = extended.shape[0] - KW + 1
    total = extended[0:sequence_length] * kernel[:, 0]
    for place in range(1, KW):
        total = total + extended[place : place + sequence_length] * kernel[:, place]
    return total


def conv_input_grad(grad_conv, kernel):
    sequence_length = grad_conv.shape[0] + KW - 1
    padded = jnp.pad(grad_conv, ((KW - 1, KW - 1), (0, 0)))
    total = padded[KW - 1 : KW - 1 + sequence_length] * kernel[:, 0]
    for place in range(1, KW):
        total = total + padded[KW - 1 - place : KW - 1 - place + sequence_length] * kernel[:, place]
    return total


def kernel_grad(extended, grad_conv):
    sequence_length = grad_conv.shape[0]
    columns = [
        jnp.sum(grad_conv * extended[place : place + sequence_length], axis=0)
        for place in range(KW)
    ]
    return jnp.stack(columns, axis=1)


def pick(value, index, axis):
    return lax.dynamic_index_in_dim(value, index, axis, keepdims=False)


MESH = pl.DeviceIdType.MESH


def dims_nt(left, right):
    return lax.dot_general(
        left, right, (((1,), (1,)), ((), ())), preferred_element_type=jnp.float32
    )


def dims_tn(left, right):
    return lax.dot_general(
        left, right, (((0,), (0,)), ((), ())), preferred_element_type=jnp.float32
    )


def ff_call(mode, ident, x, gate, up_w, down, given=None):
    size = lax.axis_size("fsdp")
    chips = size // 2
    rows, width = x.shape
    units = gate.shape[0]
    forward = mode == "forward"
    bf16 = jnp.bfloat16
    blocks = jax.ShapeDtypeStruct((size, rows, width), bf16)
    vmem = pl.BlockSpec(memory_space=pltpu.VMEM)
    anywhere = pl.BlockSpec(memory_space=pl.ANY)
    outs = [jax.ShapeDtypeStruct((rows, width), jnp.float32), blocks]
    out_specs = [vmem, vmem]
    args = [x, gate, up_w, down]
    specs = [vmem] * 4
    dma = pltpu.SemaphoreType.DMA
    scratch = [pltpu.VMEM((rows, width), jnp.float32)]
    scratch += [pltpu.VMEM((chips, rows, width), bf16)] * 3
    scratch += [pltpu.VMEM((chips + 1, rows, width), bf16)]
    scratch += [dma((chips,))] * 8 + [dma((chips, 4))] * 4
    if not forward:
        for share in (1, 2) if mode == "both" else (3,):
            outs.append(jax.ShapeDtypeStruct((share * units, width), bf16))
            out_specs.append(anywhere)
        if mode == "both":
            outs.append(blocks)
            out_specs.append(anywhere)
        args.insert(1, given)
        specs.insert(1, anywhere)
        scratch += [pltpu.VMEM(blocks.shape, bf16)]
        scratch += [pltpu.VMEM((units, size * rows), bf16)] * 3
        scratch += [pltpu.VMEM((2, units, 256), bf16), dma((size,)), dma((2,))]
        if mode == "both":
            scratch += [pltpu.VMEM((2, rows, width), bf16), dma((2,))]
    products = 3 if forward else 9
    return pl.pallas_call(
        partial(ff_kernel, chips, mode),
        out_shape=outs,
        in_specs=specs,
        out_specs=out_specs,
        scratch_shapes=scratch,
        compiler_params=pltpu.CompilerParams(
            collective_id=ident, has_side_effects=True, vmem_limit_bytes=61 * 2**20
        ),
        cost_estimate=pl.CostEstimate(
            flops=2 * products * size * rows * units * width,
            bytes_accessed=4 * size * rows * width,
            transcendentals=size * rows * units,
        ),
    )(*args)


def places():
    count = lax.axis_size("fsdp") // 2
    place = lax.axis_index("fsdp")
    chip = place // 2
    core = place % 2
    after = lax.rem(chip + 1, count) * 2 + core
    before = lax.rem(chip + count - 1, count) * 2 + core
    return place, chip, core, after, before, chip * 2 + 1 - core


def greet(targets):
    barrier = pltpu.get_barrier_semaphore()
    for target in targets:
        pl.semaphore_signal(barrier, inc=1, device_id=target, device_id_type=MESH)
    pl.semaphore_wait(barrier, len(targets))


def push(src, dst, send, recv, target):
    return pltpu.make_async_remote_copy(
        src_ref=src, dst_ref=dst, send_sem=send, recv_sem=recv,
        device_id=target, device_id_type=MESH,
    )


def ff_kernel(chips, mode, *refs):
    forward = mode == "forward"
    if forward:
        x_ref, gate, up_w, down, out, xall = refs[:6]
        rest = refs[6:]
    elif mode == "both":
        x_ref, y_hbm, gate, up_w, down, out, xall, gate_grads, weight_grads, result = refs[:10]
        rest = refs[10:]
    else:
        x_ref, y_hbm, gate, up_w, down, out, xall, weight_grads = refs[:8]
        rest = refs[8:]
    part, term, other_send, other_recv, in_sum = rest[:5]
    (up_s, up_r, down_s, down_r, core_s, core_r, ps_s, ps_r, ups_s, ups_r, downs_s, downs_r) = rest[5:17]
    if not forward:
        yall, hid, dgate, dup, stage, ysem, stage_sem = rest[17:24]
        if mode == "both":
            out_stage, out_sem = rest[24:]
    rows, width = x_ref.shape
    units = gate.shape[0]
    place, chip, core, _, _, peer = places()
    low_side = chip > 0
    high_side = chip < chips - 1
    below = {"fsdp": lax.rem(place + 2 * chips - 2, 2 * chips)}
    above = {"fsdp": lax.rem(place + 2, 2 * chips)}
    pieces = 4
    piece = rows // pieces
    greet([below, above, {"fsdp": peer}])

    def up_rows(d):
        block = xall.at[2 * d + core]
        return push(block, block, up_s.at[d], up_r.at[d], above)

    def down_rows(d):
        block = xall.at[2 * d + core]
        return push(block, block, down_s.at[d], down_r.at[d], below)

    def core_copy(d):
        block = xall.at[2 * d + core]
        return push(block, block, core_s.at[d], core_r.at[d], {"fsdp": peer})

    def core_in(d):
        block = xall.at[2 * d + 1 - core]
        return push(block, block, core_s.at[d], core_r.at[d], {"fsdp": peer})

    def part_copy(d):
        return push(other_send.at[d], other_recv.at[d], ps_s.at[d], ps_r.at[d], {"fsdp": peer})

    def span(b):
        return pl.ds(pl.multiple_of(b * piece, piece), piece)

    def up_sum(d, b):
        return push(
            term.at[d, span(b)], in_sum.at[d + 1, span(b)], ups_s.at[d, b], ups_r.at[d, b], above
        )

    def down_sum(d, b):
        return push(
            term.at[d, span(b)], in_sum.at[d, span(b)], downs_s.at[d, b], downs_r.at[d, b], below
        )

    def y_copy(s):
        return pltpu.make_async_copy(y_hbm.at[s], yall.at[s], ysem.at[s])

    def across(s):
        return pl.ds(pl.multiple_of(s * rows, rows), rows)

    def block(s):
        x = xall[s]
        if forward:
            gate_val = dims_nt(gate[...], x)
            up_val = dims_nt(up_w[...], x)
            hidden = (gate_val / (1.0 + jnp.exp(-gate_val)) * up_val).astype(jnp.bfloat16)
            return dims_tn(hidden, down[...])
        y_copy(s).wait()
        y = yall[s]
        a, g = (x, y) if mode == "both" else (y, x)
        gate_val = dims_nt(gate[...], a)
        up_val = dims_nt(up_w[...], a)
        grad_hidden = dims_nt(down[...], g)
        sig = 1.0 / (1.0 + jnp.exp(-gate_val))
        act = gate_val * sig
        grad_up = (grad_hidden * act).astype(jnp.bfloat16)
        grad_gate = (
            grad_hidden * up_val * (sig * (1.0 + gate_val * (1.0 - sig)))
        ).astype(jnp.bfloat16)
        hid[:, across(s)] = (act * up_val).astype(jnp.bfloat16)
        dup[:, across(s)] = grad_up
        dgate[:, across(s)] = grad_gate
        return dims_tn(grad_gate, gate[...]) + dims_tn(grad_up, up_w[...])

    xall[place] = x_ref[...]
    if not forward:
        @pl.loop(0, 2 * chips)
        def _(s):
            y_copy(s).start()

    @pl.when(high_side)
    def _():
        up_rows(chip).start()

    @pl.when(low_side)
    def _():
        down_rows(chip).start()

    inside = low_side & high_side
    reach = jnp.minimum(chip, chips - 1 - chip)

    def turn(r):
        far = jnp.where(r <= 2 * reach, (r + 1) // 2, r - reach)
        downward = jnp.where(r <= 2 * reach, r % 2 == 1, chip > chips - 1 - chip)
        return jnp.where(downward, chip - far, chip + far)

    def receive(r):
        d = turn(r)

        @pl.when(d < chip)
        def _():
            up_rows(d).wait_recv()

            @pl.when(high_side)
            def _():
                up_rows(d).start()

        @pl.when(d > chip)
        def _():
            down_rows(d).wait_recv()

            @pl.when(low_side)
            def _():
                down_rows(d).start()

        core_copy(d).start()

    core_copy(chip).start()

    @pl.loop(0, chips)
    def _(r):
        @pl.when((r == 1) | ((r > 1) & ~inside))
        def _():
            receive(r)

        @pl.when((r >= 1) & (r < chips - 1) & inside)
        def _():
            receive(r + 1)

        d = turn(r)

        @pl.loop(0, 2)
        def _(o):
            @pl.when(o == 1)
            def _():
                core_in(d).wait_recv()

            value = block(2 * d + (core + o) % 2)

            @pl.when(o == 0)
            def _():
                part[...] = value

            @pl.when(o == 1)
            def _():
                other_send[d] = value.astype(jnp.bfloat16)
                part_copy(d).start()

        part_copy(d).wait_recv()

        @pl.when(d == chip)
        def _():
            out[...] = part[...] + other_recv[d].astype(jnp.float32)

        @pl.when(d != chip)
        def _():
            term[d] = (part[...] + other_recv[d].astype(jnp.float32)).astype(jnp.bfloat16)

        @pl.when((d > chip) & (chip == 0))
        def _():
            for b in range(pieces):
                up_sum(d, b).start()

        @pl.when((d < chip) & (chip == chips - 1))
        def _():
            for b in range(pieces):
                down_sum(d, b).start()

    lag = 2
    items = (chips - 2) * pieces
    relays = items + lag * max(chips - 3, 0)

    def relay(n):
        rise = n - lag * (chip - 1)
        fall = n - lag * (chips - 2 - chip)
        high = jnp.maximum(rise, 0) // pieces + 2
        low = chips - 3 - jnp.maximum(fall, 0) // pieces

        @pl.when((rise >= 0) & (rise < items) & (high > chip) & low_side)
        def _():
            b = rise % pieces
            up_sum(high, b).wait_recv()
            term[high, span(b)] = (
                term[high, span(b)].astype(jnp.float32)
                + in_sum[high + 1, span(b)].astype(jnp.float32)
            ).astype(jnp.bfloat16)
            up_sum(high, b).start()

        @pl.when((fall >= 0) & (fall < items) & (low < chip) & high_side)
        def _():
            b = fall % pieces
            down_sum(low, b).wait_recv()
            term[low, span(b)] = (
                term[low, span(b)].astype(jnp.float32) + in_sum[low, span(b)].astype(jnp.float32)
            ).astype(jnp.bfloat16)
            down_sum(low, b).start()

    if forward:
        @pl.loop(0, relays)
        def _(n):
            relay(n)
    else:
        step = stage.shape[2]
        steps = width // step
        gate_right, hid_right = (xall, yall) if mode == "both" else (yall, xall)
        pairs = ((dgate, gate_right), (dup, gate_right), (hid, hid_right))

        def stage_copy(n, j):
            there, at = weight_grads, n
            if mode == "both":
                there, at = (gate_grads, 0) if n == 0 else (weight_grads, n - 1)
            there = there.at[
                pl.ds(at * units, units), pl.ds(pl.multiple_of(j * step, step), step)
            ]
            return pltpu.make_async_copy(stage.at[j % 2], there, stage_sem.at[j % 2])

        @pl.loop(0, max(2 * relays, 3 * steps))
        def _(m):
            @pl.when((m % 2 == 0) & (m < 2 * relays))
            def _():
                relay(m // 2)

            j = m % steps
            for n, (left, right) in enumerate(pairs):
                @pl.when(m // steps == n)
                def _():
                    @pl.when(m >= 2)
                    def _():
                        stage_copy(n, j).wait()

                    at = pl.ds(pl.multiple_of(j * step, step), step)
                    sums = jnp.dot(
                        left[...],
                        right[:, :, at].reshape(2 * chips * rows, step),
                        preferred_element_type=jnp.float32,
                    )
                    stage[j % 2] = sums.astype(jnp.bfloat16)
                    stage_copy(n, j).start()

        for j in range(2):
            stage_copy(2, j).wait()
        if mode == "both":
            def result_copy(s):
                return pltpu.make_async_copy(out_stage.at[s % 2], result.at[s], out_sem.at[s % 2])

            @pl.loop(0, 2 * chips)
            def _(s):
                @pl.when(s >= 2)
                def _():
                    result_copy(s).wait()

                out_stage[s % 2] = dims_tn(hid[:, across(s)], down[...]).astype(jnp.bfloat16)
                result_copy(s).start()

            for s in range(2):
                result_copy(s).wait()

    @pl.when(low_side)
    def _():
        for b in range(pieces):
            up_sum(chip, b).wait_recv()
        out[...] += in_sum[chip + 1].astype(jnp.float32)

    @pl.when(high_side)
    def _():
        for b in range(pieces):
            down_sum(chip, b).wait_recv()
        out[...] += in_sum[chip].astype(jnp.float32)

    @pl.loop(0, chips)
    def _(d):
        core_copy(d).wait_send()
        part_copy(d).wait_send()

        @pl.when((d <= chip) & high_side)
        def _():
            up_rows(d).wait_send()

        @pl.when((d >= chip) & low_side)
        def _():
            down_rows(d).wait_send()

        @pl.when(d > chip)
        def _():
            for b in range(pieces):
                up_sum(d, b).wait_send()

        @pl.when(d < chip)
        def _():
            for b in range(pieces):
                down_sum(d, b).wait_send()


def head_kernel(chips, count, *refs):
    shards = refs[:2]
    block, vector = refs[2:4]
    wholes = refs[4:6]
    blocks, vectors = refs[6:8]
    local, near_s, near_r, hop_s, hop_r, side_s, side_r, pass_s, pass_r = refs[8:]
    place, chip, core, after, before, peer = places()
    here = lax.axis_index("ctx")
    others = [{"ctx": lax.rem(here + t, count)} for t in range(1, count)]
    greet([{"fsdp": before}, {"fsdp": peer}] + others)
    started = []

    def go(copy):
        copy.start()
        started.append(copy)

    def shard_of(k):
        return lax.rem(chip + chips - k, chips) * 2 + core

    def hop(k, n):
        owner = shard_of(k)
        if n < 2:
            src = shards[n].at[here] if k == 0 else wholes[n].at[owner, here]
            dst = wholes[n].at[owner, here]
        elif n == 2:
            src = block if k == 0 else blocks.at[owner]
            dst = blocks.at[owner]
        else:
            src = vector if k == 0 else vectors.at[owner]
            dst = vectors.at[owner]
        return push(src, dst, hop_s.at[n, k], hop_r.at[n, k], {"fsdp": after})

    def side(k, t, n):
        piece = wholes[n].at[shard_of(k), here]
        return push(piece, piece, side_s.at[n, k, t], side_r.at[n, k, t], others[t - 1])

    def side_in(k, t, n):
        piece = wholes[n].at[shard_of(k), lax.rem(here + count - t, count)]
        return piece, push(piece, piece, side_s.at[n, k, t], side_r.at[n, k, t], others[t - 1])

    def across(k, t, n):
        if n == 2:
            src = dst = blocks.at[shard_of(k)]
        elif n == 3:
            src = dst = vectors.at[shard_of(k)]
        else:
            src = dst = wholes[n].at[shard_of(k), lax.rem(here + count - t, count)]
        return push(src, dst, pass_s.at[n, k, t], pass_r.at[n, k, t], {"fsdp": peer})

    def across_in(k, t, n):
        owner = lax.rem(chip + chips - k, chips) * 2 + 1 - core
        if n == 2:
            dst = blocks.at[owner]
        elif n == 3:
            dst = vectors.at[owner]
        else:
            dst = wholes[n].at[owner, lax.rem(here + count - t, count)]
        return push(dst, dst, pass_s.at[n, k, t], pass_r.at[n, k, t], {"fsdp": peer})

    homes = [one.at[place] for one in (*wholes, blocks, vectors)]
    came = [one.at[peer] for one in (*wholes, blocks, vectors)]
    sources = [shards[0], shards[1], block, vector]
    order = (3, 0, 1, 2)
    for n in order:
        go(hop(0, n))
    keeps = [pltpu.make_async_copy(sources[n], homes[n], local.at[n]) for n in order]
    for one in keeps:
        one.start()
    for n in order:
        go(push(sources[n], homes[n], near_s.at[n], near_r.at[n], {"fsdp": peer}))
    for k in range(1, chips):
        for n in order:
            hop(k - 1, n).wait_recv()
            if k < chips - 1:
                go(hop(k, n))
            if n < 2:
                for t in range(1, count):
                    go(side(k, t, n))
            go(across(k, 0, n))
        if k > 1:
            for n in range(2):
                for t in range(1, count):
                    side_in(k - 1, t, n)[1].wait_recv()
                    go(across(k - 1, t, n))
    for n in range(2):
        for t in range(1, count):
            side_in(chips - 1, t, n)[1].wait_recv()
            go(across(chips - 1, t, n))
    for n in order:
        push(came[n], came[n], near_s.at[n], near_r.at[n], {"fsdp": peer}).wait_recv()
        for k in range(1, chips):
            for t in range(count if n < 2 else 1):
                across_in(k, t, n).wait_recv()
    for one in keeps:
        one.wait()
    for one in started:
        one.wait_send()


def head_call(ident, shard_a, shard_b, block, vector):
    size = lax.axis_size("fsdp")
    count = lax.axis_size("ctx")
    chips = size // 2
    width = shard_a.shape[1]
    shards = [one.reshape(count, -1, width) for one in (shard_a, shard_b)]
    outs = [jax.ShapeDtypeStruct((size,) + one.shape, jnp.bfloat16) for one in shards]
    outs.append(jax.ShapeDtypeStruct((size,) + block.shape, jnp.bfloat16))
    outs.append(jax.ShapeDtypeStruct((size,) + vector.shape, jnp.bfloat16))
    anywhere = pl.BlockSpec(memory_space=pl.ANY)
    dma = pltpu.SemaphoreType.DMA
    whole_a, whole_b, blocks, vectors = pl.pallas_call(
        partial(head_kernel, chips, count),
        out_shape=outs,
        in_specs=[anywhere] * 4,
        out_specs=[anywhere] * 4,
        scratch_shapes=[
            dma((4,)), dma((4,)), dma((4,)),
            dma((4, chips)), dma((4, chips)),
            dma((2, chips, count)), dma((2, chips, count)),
            dma((4, chips, count)), dma((4, chips, count)),
        ],
        compiler_params=pltpu.CompilerParams(collective_id=ident, has_side_effects=True),
        cost_estimate=pl.CostEstimate(
            flops=0, bytes_accessed=2 * size * (shard_a.size + shard_b.size) * 2, transcendentals=0
        ),
    )(*shards, block, vector)
    return whole_a.reshape(-1, width), whole_b.reshape(-1, width), blocks, vectors


def tail_kernel(chips, count, pieces, *refs):
    number = len(pieces)
    grads = refs[:number]
    factor, inputs, small = refs[number : number + 3]
    total, total_in, small_total = refs[number + 3 : number + 6]
    rest = refs[number + 6 :]
    own, near, line, in_sum, fin, rc, fs, held, fin_in, rc_in, fs_in, small_in, small_sums = rest[:13]
    (own_m, near_s, near_r, up_s, up_r, down_s, down_r, sc_s, sc_r, ag_s, ag_r, fac_m, fac_s, fac_r,
     sci_s, sci_r, agi_s, agi_r, sm_s, sm_r, smc_s, smc_r) = rest[13:]
    place, chip, core, after, before, peer = places()
    here = lax.axis_index("ctx")
    size = 2 * chips
    chunks = sum(pieces)
    ctx_others = [{"ctx": lax.rem(here + t, count)} for t in range(1, count)]
    shard_others = [{"fsdp": lax.rem(place + t, size)} for t in range(1, size)]
    greet(ctx_others + shard_others)

    def factor_copy(t):
        there = lax.rem(place + t, size)
        return push(factor.at[there], held.at[place], fac_s.at[t], fac_r.at[t], {"fsdp": there})

    def small_copy(t):
        there = lax.rem(place + t, size)
        return push(small.at[there], small_in.at[t], sm_s.at[t], sm_r.at[t], {"fsdp": there})

    def small_share(t):
        return push(
            small_sums.at[0], small_sums.at[t], smc_s.at[t], smc_r.at[t], ctx_others[t - 1]
        )

    for t in range(1, size):
        small_copy(t).start()
        factor_copy(t).start()
    keep = pltpu.make_async_copy(factor.at[place], held.at[place], fac_m)
    keep.start()

    bases = [sum(pieces[:n]) for n in range(number)]

    def near_copy(n, j):
        at = bases[n] + j
        return push(
            grads[n].at[:, 1 - core, j], near.at[at], near_s.at[at], near_r.at[at], {"fsdp": peer}
        )

    def own_copy(n, j):
        at = bases[n] + j
        return pltpu.make_async_copy(grads[n].at[:, core, j], own.at[at], own_m.at[at])

    for n in range(number):
        @pl.loop(0, pieces[n])
        def _(j):
            near_copy(n, j).start()
            own_copy(n, j).start()

    def up_copy(d, j):
        there = {"fsdp": lax.rem(place + 2, size)}
        return push(own.at[j, d], in_sum.at[d + 1, j], up_s.at[d, j], up_r.at[d, j], there)

    def down_copy(d, j):
        there = {"fsdp": lax.rem(place + size - 2, size)}
        return push(own.at[j, d], in_sum.at[d, j], down_s.at[d, j], down_r.at[d, j], there)

    def near_in(j):
        return push(near.at[j], near.at[j], near_s.at[j], near_r.at[j], {"fsdp": peer})

    def own_in(j):
        return pltpu.make_async_copy(own.at[j], own.at[j], own_m.at[j])

    def term(j, owner):
        return own[j, owner].astype(jnp.float32) + near[j, owner].astype(jnp.float32)

    def scatter_copy(j, t):
        there = lax.rem(here + t, count)
        return push(fin.at[j, there], rc.at[j, t], sc_s.at[j, t], sc_r.at[j, t], {"ctx": there})

    def gather_copy(j, t):
        return push(
            fs.at[j], total.at[j, here], ag_s.at[j, t], ag_r.at[j, t], ctx_others[t - 1]
        )

    def gather_in(j, t):
        there = total.at[j, lax.rem(here + count - t, count)]
        return push(there, there, ag_s.at[j, t], ag_r.at[j, t], ctx_others[t - 1])

    def scatter_in_copy(t):
        there = lax.rem(here + t, count)
        return push(fin_in.at[there], rc_in.at[t], sci_s.at[t], sci_r.at[t], {"ctx": there})

    def gather_in_copy(t):
        return push(fs_in, total_in.at[here], agi_s.at[t], agi_r.at[t], ctx_others[t - 1])

    def gather_in_wait(t):
        there = total_in.at[lax.rem(here + count - t, count)]
        return push(there, there, agi_s.at[t], agi_r.at[t], ctx_others[t - 1])

    def products():
        for t in range(1, size):
            src = held.at[lax.rem(place + size - t, size)]
            push(src, src, fac_s.at[t], fac_r.at[t], {"fsdp": peer}).wait_recv()
        keep.wait()

        tall = held.shape[2]
        joined = 1 if tall % 16 else count
        step = 256

        @pl.loop(0, count // joined)
        def _(c):
            @pl.loop(0, inputs.shape[2] // step)
            def _(n):
                at = pl.ds(pl.multiple_of(n * step, step), step)
                sums = 0.0
                for s in range(size):
                    left = held[s].reshape(count * tall, -1) if joined > 1 else held[s, c]
                    sums = sums + jnp.dot(
                        left, inputs[s, :, at], preferred_element_type=jnp.float32
                    )
                sums = sums.astype(jnp.bfloat16)
                if joined > 1:
                    fin_in[:, :, at] = sums.reshape(count, tall, step)
                else:
                    fin_in[c, :, at] = sums

        for t in range(1, count):
            scatter_in_copy(t).start()
        sums = small[place]
        for t in range(1, size):
            small_copy(t).wait_recv()
            sums = sums + small_in[t]
        small_sums[0] = sums
        for t in range(1, count):
            small_share(t).start()

    def products_sum():
        sums = fin_in[here].astype(jnp.float32)
        for t in range(1, count):
            scatter_in_copy(t).wait_recv()
            sums = sums + rc_in[t].astype(jnp.float32)
        fs_in[...] = sums.astype(jnp.bfloat16)
        for t in range(1, count):
            gather_in_copy(t).start()
        total_in[here] = fs_in[...]
        sums = small_sums[0]
        for t in range(1, count):
            small_share(t).wait_recv()
            sums = sums + small_sums[t]
        small_total[...] = sums

    def relay(d, j, arrives, arrived, slot, leave):
        line[...] = term(j, d)

        @pl.when(arrives)
        def _():
            arrived(d, j).wait_recv()
            line[...] += in_sum[slot, j].astype(jnp.float32)

        own[j, d] = line[...].astype(jnp.bfloat16)
        leave(d, j).start()

    lag = 2
    items = (chips - 1) * chunks

    @pl.loop(0, items + lag * (chips - 1))
    def _(i):
        @pl.when(i < chunks)
        def _():
            own_in(i).wait()
            near_in(i).wait_recv()

        rise = i - lag * chip
        upward = chips - 1 - jnp.maximum(rise, 0) // chunks

        @pl.when((rise >= 0) & (rise < items) & (upward > chip))
        def _():
            relay(upward, rise % chunks, chip > 0, up_copy, upward + 1, up_copy)

        fall = i - lag * (chips - 1 - chip)
        downward = jnp.maximum(fall, 0) // chunks

        @pl.when((fall >= 0) & (fall < items) & (downward < chip))
        def _():
            relay(downward, fall % chunks, chip < chips - 1, down_copy, downward, down_copy)

        @pl.when(i == items // 2)
        def _():
            products()

    def reduce_chunk(j):
        sums = fin[j, here].astype(jnp.float32)
        for t in range(1, count):
            scatter_copy(j, t).wait_recv()
            sums = sums + rc[j, t].astype(jnp.float32)
        fs[j] = sums.astype(jnp.bfloat16)
        for t in range(1, count):
            gather_copy(j, t).start()
        total[j, here] = fs[j]

    @pl.loop(0, chunks)
    def _(j):
        line[...] = term(j, chip)

        @pl.when(chip > 0)
        def _():
            up_copy(chip, j).wait_recv()
            line[...] += in_sum[chip + 1, j].astype(jnp.float32)

        @pl.when(chip < chips - 1)
        def _():
            down_copy(chip, j).wait_recv()
            line[...] += in_sum[chip, j].astype(jnp.float32)

        fin[j] = line[...].astype(jnp.bfloat16)
        for t in range(1, count):
            scatter_copy(j, t).start()

        @pl.when(j >= 2)
        def _():
            reduce_chunk(j - 2)

        @pl.when(j == chunks // 2)
        def _():
            products_sum()

    @pl.loop(chunks - 2, chunks)
    def _(j):
        reduce_chunk(j)

    @pl.loop(0, chunks)
    def _(j):
        for t in range(1, count):
            gather_in(j, t).wait_recv()
            gather_copy(j, t).wait_send()
            scatter_copy(j, t).wait_send()

        near_in(j).wait_send()

        @pl.loop(0, chips)
        def _(d):
            @pl.when(d > chip)
            def _():
                up_copy(d, j).wait_send()

            @pl.when(d < chip)
            def _():
                down_copy(d, j).wait_send()

    for t in range(1, count):
        gather_in_wait(t).wait_recv()
        gather_in_copy(t).wait_send()
        scatter_in_copy(t).wait_send()
        small_share(t).wait_send()
    for t in range(1, size):
        small_copy(t).wait_send()
        factor_copy(t).wait_send()


def tail_call(ident, grads, factor, inputs, small):
    size = lax.axis_size("fsdp")
    count = lax.axis_size("ctx")
    chips = size // 2
    width = inputs.shape[2]
    rows = inputs.shape[1]
    unit = min(one.shape[1] for one in grads) // 3
    pieces = [one.shape[1] // unit for one in grads]
    chunks = sum(pieces)
    part = unit // count
    views = [
        one.reshape(chips, 2, n, count, part, width) for one, n in zip(grads, pieces)
    ]
    factor = factor.T.reshape(size, count, -1, rows)
    mine = factor.shape[2]
    bf16 = jnp.bfloat16
    anywhere = pl.BlockSpec(memory_space=pl.ANY)
    vmem = pl.BlockSpec(memory_space=pltpu.VMEM)
    dma = pltpu.SemaphoreType.DMA
    total, total_in, small_total = pl.pallas_call(
        partial(tail_kernel, chips, count, pieces),
        out_shape=[
            jax.ShapeDtypeStruct((chunks, count, part, width), bf16),
            jax.ShapeDtypeStruct((count, mine, width), bf16),
            jax.ShapeDtypeStruct(small.shape[1:], jnp.float32),
        ],
        in_specs=[anywhere] * (len(views) + 1) + [vmem] * 2,
        out_specs=[vmem] * 3,
        scratch_shapes=[
            pltpu.VMEM((chunks, chips, count, part, width), bf16),
            pltpu.VMEM((chunks, chips, count, part, width), bf16),
            pltpu.VMEM((count, part, width), jnp.float32),
            pltpu.VMEM((chips + 1, chunks, count, part, width), bf16),
            pltpu.VMEM((chunks, count, part, width), bf16),
            pltpu.VMEM((chunks, count, part, width), bf16),
            pltpu.VMEM((chunks, part, width), bf16),
            pltpu.VMEM((size, count, mine, rows), bf16),
            pltpu.VMEM((count, mine, width), bf16),
            pltpu.VMEM((count, mine, width), bf16),
            pltpu.VMEM((mine, width), bf16),
            pltpu.VMEM(small.shape, jnp.float32),
            pltpu.VMEM((count,) + small.shape[1:], jnp.float32),
            dma((chunks,)), dma((chunks,)), dma((chunks,)),
            dma((chips, chunks)), dma((chips, chunks)), dma((chips, chunks)), dma((chips, chunks)),
            dma((chunks, count)), dma((chunks, count)), dma((chunks, count)), dma((chunks, count)),
            dma, dma((size,)), dma((size,)),
            dma((count,)), dma((count,)), dma((count,)), dma((count,)),
            dma((size,)), dma((size,)), dma((count,)), dma((count,)),
        ],
        compiler_params=pltpu.CompilerParams(
            collective_id=ident, has_side_effects=True, vmem_limit_bytes=61 * 2**20
        ),
        cost_estimate=pl.CostEstimate(
            flops=2 * size * rows * width * count * mine,
            bytes_accessed=4 * size * chunks * unit * width,
            transcendentals=0,
        ),
    )(*views, factor, inputs, small)
    total = total.reshape(-1, width).astype(jnp.float32)
    outs = []
    at = 0
    for one in grads:
        outs.append(total[at : at + one.shape[1]])
        at += one.shape[1]
    return outs + [total_in.reshape(-1, width).astype(jnp.float32), small_total.reshape(-1)]


def attend_kernel(count, groups, q, kv, att, sums, kv_all, acc, send, recv):
    here = lax.axis_index("ctx")
    others = [{"ctx": lax.rem(here + t, count)} for t in range(1, count)]
    greet(others)
    key_heads = kv.shape[0] // 2
    rows = kv.shape[2]
    block = rows // 2
    scale = HEAD_SIZE ** (-0.5)

    def out_copy(t):
        return push(kv, kv_all.at[here], send.at[t], recv.at[t], others[t - 1])

    def in_copy(t):
        there = kv_all.at[lax.rem(here + count - t, count)]
        return push(there, there, send.at[t], recv.at[t], others[t - 1])

    for t in range(1, count):
        out_copy(t).start()
    kv_all[here] = kv[...]

    def weights(keys, queries, masked):
        value = jnp.exp(dims_tn(keys, queries) * scale)
        if masked:
            allowed = lax.broadcasted_iota(jnp.int32, value.shape, 1) >= lax.broadcasted_iota(
                jnp.int32, value.shape, 0
            )
            value = jnp.where(allowed, value, 0.0)
        return value

    def apply(values, part):
        return jnp.dot(values, part.astype(jnp.bfloat16), preferred_element_type=jnp.float32)

    @pl.loop(0, key_heads)
    def _(h):
        keys = kv[h]
        values = kv[key_heads + h]
        for g in range(groups):
            head = h * groups + g
            queries = q[head]
            part = weights(keys[:, :block], queries, True)
            acc[head] = apply(values[:, :block], part)
            sums[head] = jnp.sum(part, axis=0, keepdims=True)
            part = weights(keys[:, block:], queries[:, block:], True)
            acc[head, :, block:] += apply(values[:, block:], part)
            sums[head, :, block:] += jnp.sum(part, axis=0, keepdims=True)

    for t in range(1, count):
        there = lax.rem(here + count - t, count)
        in_copy(t).wait_recv()

        @pl.when(there < here)
        def _():
            @pl.loop(0, key_heads)
            def _(h):
                keys = kv_all[there, h]
                values = kv_all[there, key_heads + h]
                for g in range(groups):
                    head = h * groups + g
                    part = weights(keys[:, :block], q[head], False)
                    acc[head] += apply(values[:, :block], part)
                    sums[head] += jnp.sum(part, axis=0, keepdims=True)

        @pl.when(there > here)
        def _():
            @pl.loop(0, key_heads)
            def _(h):
                keys = kv_all[there, h]
                values = kv_all[there, key_heads + h]
                for g in range(groups):
                    head = h * groups + g
                    part = weights(keys, q[head][:, block:], False)
                    acc[head, :, block:] += apply(values, part)
                    sums[head, :, block:] += jnp.sum(part, axis=0, keepdims=True)

    @pl.loop(0, key_heads * groups)
    def _(head):
        att[head] = (acc[head] / sums[head]).astype(jnp.bfloat16)

    for t in range(1, count):
        out_copy(t).wait_send()


def attend_call(ident, q, kv):
    count = lax.axis_size("ctx")
    heads, size, rows = q.shape
    groups = heads // (kv.shape[0] // 2)
    vmem = pl.BlockSpec(memory_space=pltpu.VMEM)
    dma = pltpu.SemaphoreType.DMA
    return pl.pallas_call(
        partial(attend_kernel, count, groups),
        out_shape=[
            jax.ShapeDtypeStruct(q.shape, jnp.bfloat16),
            jax.ShapeDtypeStruct((heads, 1, rows), jnp.float32),
            jax.ShapeDtypeStruct((count,) + kv.shape, jnp.bfloat16),
        ],
        in_specs=[vmem] * 2,
        out_specs=[vmem] * 3,
        scratch_shapes=[pltpu.VMEM(q.shape, jnp.float32), dma((count,)), dma((count,))],
        compiler_params=pltpu.CompilerParams(
            collective_id=ident, has_side_effects=True, vmem_limit_bytes=40 * 2**20
        ),
        cost_estimate=pl.CostEstimate(
            flops=4 * heads * size * rows * rows * count,
            bytes_accessed=4 * (q.size + kv.size * count),
            transcendentals=heads * rows * rows * count,
        ),
    )(q, kv)


def attend_back_kernel(
    chips, count, groups, q, kv_all, grad, att, sums, outs, grad_q, grad_kv, result,
    delta, share, send_buf, recv_buf, own, near, out_sum, in_sum,
    send, recv, own_m, near_s, near_r, ring_s, ring_r
):
    place, chip, core, after, before, peer = places()
    here = lax.axis_index("ctx")
    others = [{"ctx": lax.rem(here + t, count)} for t in range(1, count)]
    greet([{"fsdp": before}, {"fsdp": peer}] + others)

    def near_copy(n):
        return push(
            outs.at[2 * n + 1 - core], near.at[n], near_s.at[n], near_r.at[n], {"fsdp": peer}
        )

    def own_copy(n):
        return pltpu.make_async_copy(outs.at[2 * n + core], own.at[n], own_m.at[n])

    def ring_copy(k):
        return push(out_sum.at[k], in_sum.at[k], ring_s.at[k], ring_r.at[k], {"fsdp": after})

    def term(k):
        owner = lax.rem(chip + chips - k, chips)
        own_copy(owner).wait()
        near_copy(owner).wait_recv()
        return own[owner].astype(jnp.float32) + near[owner].astype(jnp.float32)

    def hop(k):
        value = term(k)
        if k > 1:
            ring_copy(k - 2).wait_recv()
            value = value + in_sum[k - 2].astype(jnp.float32)
        out_sum[k - 1] = value.astype(jnp.bfloat16)
        ring_copy(k - 1).start()

    for n in range(chips):
        near_copy(n).start()
        own_copy(n).start()
    key_heads = kv_all.shape[1] // 2
    rows = q.shape[2]
    block = rows // 2
    scale = HEAD_SIZE ** (-0.5)
    every = slice(0, rows)
    front = slice(0, block)
    back = slice(block, rows)

    def copy(t):
        return push(send_buf.at[t], recv_buf.at[t], send.at[t], recv.at[t], others[t - 1])

    @pl.loop(0, key_heads * groups)
    def _(head):
        delta[head] = jnp.sum(
            grad[head].astype(jnp.float32) * att[head].astype(jnp.float32), axis=0, keepdims=True
        )
        share[head] = 1.0 / sums[head]
        grad_q[head] = jnp.zeros(grad_q.shape[1:], jnp.float32)

    def terms(keys, values, head, span, masked):
        queries = q[head][:, span]
        low = grad[head][:, span]
        probs = jnp.exp(dims_tn(keys, queries) * scale) * share[head][:, span]
        if masked:
            allowed = lax.broadcasted_iota(jnp.int32, probs.shape, 1) >= lax.broadcasted_iota(
                jnp.int32, probs.shape, 0
            )
            probs = jnp.where(allowed, probs, 0.0)
        grad_scores = (probs * (dims_tn(values, low) - delta[head][:, span])).astype(jnp.bfloat16)
        grad_q[head, :, span] += (
            jnp.dot(keys, grad_scores, preferred_element_type=jnp.float32) * scale
        )
        return (
            dims_nt(queries, grad_scores) * scale,
            dims_nt(low, probs.astype(jnp.bfloat16)),
        )

    def over_groups(keys, values, h, span, masked):
        grad_keys, grad_values = terms(keys, values, h * groups, span, masked)
        for g in range(1, groups):
            more_keys, more_values = terms(keys, values, h * groups + g, span, masked)
            grad_keys, grad_values = grad_keys + more_keys, grad_values + more_values
        return grad_keys, grad_values

    for t in range(1, max(count, chips)):
        if t >= count:
            hop(t)
            continue
        there = lax.rem(here + t, count)

        @pl.when(there < here)
        def _():
            @pl.loop(0, key_heads)
            def _(h):
                keys = kv_all[there, h][:, front]
                values = kv_all[there, key_heads + h][:, front]
                grad_keys, grad_values = over_groups(keys, values, h, every, False)
                zeros = jnp.zeros((keys.shape[0], rows - block), jnp.bfloat16)
                send_buf[t, h, :, front] = grad_keys.astype(jnp.bfloat16)
                send_buf[t, key_heads + h, :, front] = grad_values.astype(jnp.bfloat16)
                send_buf[t, h, :, back] = zeros
                send_buf[t, key_heads + h, :, back] = zeros

        @pl.when(there > here)
        def _():
            @pl.loop(0, key_heads)
            def _(h):
                keys = kv_all[there, h]
                values = kv_all[there, key_heads + h]
                grad_keys, grad_values = over_groups(keys, values, h, back, False)
                send_buf[t, h] = grad_keys.astype(jnp.bfloat16)
                send_buf[t, key_heads + h] = grad_values.astype(jnp.bfloat16)

        copy(t).start()
        if t < chips:
            hop(t)

    @pl.loop(0, key_heads)
    def _(h):
        keys = kv_all[here, h]
        values = kv_all[here, key_heads + h]
        grad_keys, grad_values = over_groups(keys[:, front], values[:, front], h, every, True)
        grad_kv[h, :, front] = grad_keys
        grad_kv[key_heads + h, :, front] = grad_values
        grad_keys, grad_values = over_groups(keys[:, back], values[:, back], h, back, True)
        grad_kv[h, :, back] = grad_keys
        grad_kv[key_heads + h, :, back] = grad_values

    for t in range(1, count):
        copy(t).wait_recv()

        @pl.loop(0, 2 * key_heads)
        def _(h):
            grad_kv[h] += recv_buf[t, h].astype(jnp.float32)

    value = term(0)
    ring_copy(chips - 2).wait_recv()
    result[...] = value + in_sum[chips - 2].astype(jnp.float32)
    for t in range(1, count):
        copy(t).wait_send()
    for n in range(chips):
        near_copy(n).wait_send()
    for k in range(chips - 1):
        ring_copy(k).wait_send()


def attend_back_call(ident, q, kv_all, grad, att, sums, outs):
    count = lax.axis_size("ctx")
    heads, size, rows = q.shape
    kv_shape = kv_all.shape[1:]
    chips = outs.shape[0] // 2
    block = outs.shape[1:]
    groups = heads // (kv_shape[0] // 2)
    vmem = pl.BlockSpec(memory_space=pltpu.VMEM)
    dma = pltpu.SemaphoreType.DMA
    return pl.pallas_call(
        partial(attend_back_kernel, chips, count, groups),
        out_shape=[
            jax.ShapeDtypeStruct(q.shape, jnp.float32),
            jax.ShapeDtypeStruct(kv_shape, jnp.float32),
            jax.ShapeDtypeStruct(block, jnp.float32),
        ],
        in_specs=[vmem] * 5 + [pl.BlockSpec(memory_space=pl.ANY)],
        out_specs=[vmem] * 3,
        scratch_shapes=[
            pltpu.VMEM(sums.shape, jnp.float32),
            pltpu.VMEM(sums.shape, jnp.float32),
            pltpu.VMEM(kv_all.shape, jnp.bfloat16),
            pltpu.VMEM(kv_all.shape, jnp.bfloat16),
            pltpu.VMEM((chips,) + block, jnp.bfloat16),
            pltpu.VMEM((chips,) + block, jnp.bfloat16),
            pltpu.VMEM((chips - 1,) + block, jnp.bfloat16),
            pltpu.VMEM((chips - 1,) + block, jnp.bfloat16),
            dma((count,)),
            dma((count,)),
            dma((chips,)),
            dma((chips,)),
            dma((chips,)),
            dma((chips,)),
            dma((chips,)),
        ],
        compiler_params=pltpu.CompilerParams(
            collective_id=ident, has_side_effects=True, vmem_limit_bytes=40 * 2**20
        ),
        cost_estimate=pl.CostEstimate(
            flops=10 * heads * size * rows * rows * count,
            bytes_accessed=4 * (3 * q.size + kv_all.size),
            transcendentals=heads * rows * rows * count,
        ),
    )(q, kv_all, grad, att, sums, outs)


def local(
    hidden_in,
    cotangent,
    norm_mix,
    in_proj,
    conv_kernel,
    out_proj,
    norm_ff1,
    gate1,
    up1,
    down1,
    norm_attn,
    q_proj,
    key_projection,
    value_projection,
    q_norm,
    k_norm,
    o_proj,
    norm_ff2,
    gate2,
    up2,
    down2,
):
    narrow_dtype = jnp.bfloat16
    start = hidden_in[0].astype(jnp.float32)
    token_rows = start.shape[0]
    block = token_rows // 2
    margin = KW - 1
    ctx_count = lax.axis_size("ctx")
    ctx_place = lax.axis_index("ctx")
    is_last = ctx_place == ctx_count - 1
    query_places = dealt_places(
        ctx_place * token_rows + jnp.arange(token_rows, dtype=jnp.int32), block, ctx_count
    )
    freqs = THETA ** (-jnp.arange(HEAD_SIZE // 2, dtype=jnp.float32) * 2.0 / HEAD_SIZE)
    angles = freqs[:, None] * query_places.astype(jnp.float32)[None, :]
    vectors = (
        norm_mix, norm_ff1, norm_attn, norm_ff2, q_norm, k_norm, conv_kernel.reshape(-1)
    )
    lengths = [one.shape[0] for one in vectors]
    vector = jnp.concatenate(vectors)
    vector = jnp.pad(vector, (0, 2048 - sum(lengths))).reshape(16, 128)
    attn_shard = jnp.concatenate([q_proj, key_projection, value_projection, o_proj], axis=0)
    attn_rows = attn_shard.shape[0]
    attn_slice = pick(attn_shard.reshape(ctx_count, -1, MODEL_WIDTH), ctx_place, 0)
    attn_slices = lax.all_gather(attn_slice, "fsdp", axis=0)
    mix_in, mix_out, given, gathered_vectors = head_call(
        4, in_proj, out_proj, cotangent[0], vector
    )
    attn_slices, mix_in = lax.optimization_barrier((attn_slices, mix_in))
    attn_wholes = lax.all_gather(attn_slices, "ctx", axis=1)
    attn_wholes = attn_wholes.reshape(-1, attn_rows, MODEL_WIDTH)
    gathered_vectors = gathered_vectors.reshape(-1, 2048)
    wholes = []
    at = 0
    for one in lengths:
        wholes.append(gathered_vectors[:, at : at + one].reshape(-1))
        at += one
    mix_norm, ff_norm_one, attn_norm, ff_norm_two, query_gain, key_gain, mix_kernel = wholes
    mix_kernel = mix_kernel.reshape(-1, KW)
    kernel = mix_kernel.astype(jnp.float32)
    normed_one, norm_back_one = jax.vjp(rms_scale, start, mix_norm.astype(jnp.float32))
    normed_one_low = normed_one.astype(narrow_dtype)
    projected = dot_rows(normed_one_low, mix_in)
    b_part = projected[:, :MODEL_WIDTH]
    c_part = projected[:, MODEL_WIDTH : 2 * MODEL_WIDTH]
    x_part = projected[:, 2 * MODEL_WIDTH :]
    mixed_low = (b_part * x_part).astype(narrow_dtype)
    front_tail = mixed_low[block - margin : block]
    back_tail = mixed_low[token_rows - margin :]
    edges = extended_2(jnp.concatenate([back_tail, front_tail], axis=0), (("ctx", 0),), margin)
    before_front = edges[:margin]
    before_back = jnp.where(is_last, front_tail, edges[edges.shape[0] - margin :])
    front_ext = jnp.concatenate([before_front, mixed_low[:block]], axis=0).astype(jnp.float32)
    back_ext = jnp.concatenate([before_back, mixed_low[block:]], axis=0).astype(jnp.float32)
    conv_out = jnp.concatenate(
        [conv_apply(front_ext, kernel), conv_apply(back_ext, kernel)], axis=0
    )
    gated_low = (c_part * conv_out).astype(narrow_dtype)
    first = start + dot_rows(gated_low, mix_out)
    normed_two, norm_back_two = jax.vjp(rms_scale, first, ff_norm_one.astype(jnp.float32))
    ff_out_one, inputs_one = ff_call(
        "forward", 1, normed_two.astype(narrow_dtype), gate1, up1, down1
    )
    one_low, ff_out_one = lax.optimization_barrier((normed_one_low, ff_out_one))
    one_blocks = lax.all_gather(one_low, "fsdp", axis=0)
    second = first + ff_out_one
    attn_parts = []
    at = 0
    for one in (q_proj, key_projection, value_projection, o_proj):
        attn_parts.append(attn_wholes[:, at : at + one.shape[0]].reshape(-1, MODEL_WIDTH))
        at += one.shape[0]
    w_query, w_key, w_value, w_output = attn_parts
    normed_three, norm_back_three = jax.vjp(rms_scale, second, attn_norm.astype(jnp.float32))
    three_low = normed_three.astype(narrow_dtype)
    query_raw = dot_rows(w_query, three_low)
    key_raw = dot_rows(w_key, three_low)
    value_raw = dot_rows(w_value, three_low)
    query_heads, query_back = jax.vjp(
        partial(head_prep, angles=angles), query_raw, query_gain.astype(jnp.float32)
    )
    key_heads, key_back = jax.vjp(
        partial(head_prep, angles=angles), key_raw, key_gain.astype(jnp.float32)
    )
    query_narrow = query_heads.astype(narrow_dtype)
    key_value = jnp.concatenate(
        [key_heads, value_raw.reshape(key_heads.shape)], axis=0
    ).astype(narrow_dtype)
    attended_low, exp_sums, key_value_all = attend_call(6, query_narrow, key_value)
    attended_flat = attended_low.reshape(-1, token_rows)
    third = second + lax.dot_general(
        attended_flat, w_output, (((0,), (1,)), ((), ())), preferred_element_type=jnp.float32
    )
    normed_four, norm_back_four = jax.vjp(rms_scale, third, ff_norm_two.astype(jnp.float32))
    four_low, one_blocks = lax.optimization_barrier((normed_four.astype(narrow_dtype), one_blocks))
    grad_four, _, two_gate, two_rest, outs_two = ff_call("both", 2, four_low, gate2, up2, down2, given)
    shards = lax.axis_size("fsdp")
    ff_two_gate = lax.psum(two_gate, "ctx")
    grad_final = cotangent[0].astype(jnp.float32)
    grad_third_part, grad_ff_norm_two = norm_back_four(grad_four)
    grad_third = grad_final + grad_third_part
    output_low = grad_third.astype(narrow_dtype)
    attended_gradient = lax.dot_general(
        w_output, output_low, (((0,), (1,)), ((), ())), preferred_element_type=jnp.float32
    )
    grad_w_output = (
        lax.dot_general(
            output_low, attended_flat, (((0,), (1,)), ((), ())), preferred_element_type=jnp.float32
        )
        .astype(narrow_dtype)
        .reshape(lax.axis_size("fsdp"), -1, MODEL_WIDTH)
    )
    grad_query, grad_key_value, ff_out_two = attend_back_call(
        7,
        query_narrow,
        key_value_all,
        attended_gradient.astype(narrow_dtype).reshape(query_narrow.shape),
        attended_low,
        exp_sums,
        outs_two,
    )
    final = third + ff_out_two
    grad_query, ff_two_gate = lax.optimization_barrier((grad_query, ff_two_gate))
    key_count = grad_key_value.shape[0] // 2
    grad_query_raw, grad_query_gain = query_back(grad_query)
    raw_key_gradient, key_gain_gradient = key_back(grad_key_value[:key_count])
    query_grad_low = grad_query_raw.astype(narrow_dtype)
    key_grad_low = raw_key_gradient.astype(narrow_dtype)
    value_grad_low = grad_key_value[key_count:].astype(narrow_dtype).reshape(key_grad_low.shape)
    grad_three = (
        dot_cols(query_grad_low, w_query)
        + dot_cols(key_grad_low, w_key)
        + dot_cols(value_grad_low, w_value)
    )
    grad_rows = [
        one.reshape(shards, -1, token_rows) for one in (query_grad_low, key_grad_low, value_grad_low)
    ]
    widths = [one.shape[1] for one in grad_rows]
    grad_rows = jnp.concatenate(grad_rows, axis=1).reshape(-1, token_rows)
    grad_w_qkv = (
        dot_plain(grad_rows, three_low).astype(narrow_dtype).reshape(shards, sum(widths), -1)
    )
    grad_second_part, grad_attn_norm = norm_back_three(grad_three)
    grad_second = grad_third + grad_second_part
    two_rest, ff_two_gate = lax.optimization_barrier((two_rest, ff_two_gate))
    ff_two_rest = lax.psum(two_rest, "ctx")
    grad_two, _, one_grads = ff_call(
        "backward", 3, grad_second.astype(narrow_dtype), gate1, up1, down1, inputs_one
    )
    grad_two, one_grads, ff_two_rest = lax.optimization_barrier((grad_two, one_grads, ff_two_rest))
    ff_one = lax.psum(one_grads, "ctx")
    ff_one, ff_two = [
        [
            one[at : at + gate1.shape[0]].astype(jnp.float32)
            for at in range(0, one.shape[0], gate1.shape[0])
        ]
        for one in (ff_one, ff_two_rest)
    ]
    ff_two = [ff_two_gate.astype(jnp.float32)] + ff_two
    grad_first_part, grad_ff_norm_one = norm_back_two(grad_two)
    grad_first = grad_second + grad_first_part
    first_low = grad_first.astype(narrow_dtype)
    grad_gated = dot_plain(first_low, mix_out)
    grad_mix_out = (
        dot_cols(first_low, gated_low).astype(narrow_dtype).reshape(shards, -1, MODEL_WIDTH)
    )
    grad_c_part = grad_gated * conv_out
    grad_conv = grad_gated * c_part
    grad_front_ext = conv_input_grad(grad_conv[:block], kernel)
    grad_back_ext = conv_input_grad(grad_conv[block:], kernel)
    back_before = grad_back_ext[:margin]
    outgoing = jnp.concatenate(
        [grad_front_ext[:margin], jnp.where(is_last, 0.0, back_before)], axis=0
    )
    returned = extended_2(outgoing, (("ctx", 0),), margin)
    from_prev = returned[:margin]
    from_next = returned[returned.shape[0] - margin :]
    own_edge = jnp.where(is_last, back_before, 0.0)
    front_grad = grad_front_ext[margin:]
    back_grad = grad_back_ext[margin:]
    front_grad = jnp.concatenate(
        [front_grad[: block - margin], front_grad[block - margin :] + from_next + own_edge], axis=0
    )
    back_grad = jnp.concatenate(
        [back_grad[: block - margin], back_grad[block - margin :] + from_prev], axis=0
    )
    grad_mixed = jnp.concatenate([front_grad, back_grad], axis=0)
    grad_kernel = kernel_grad(front_ext, grad_conv[:block]) + kernel_grad(
        back_ext, grad_conv[block:]
    )
    grad_projected = jnp.concatenate(
        [grad_mixed * x_part, grad_c_part, grad_mixed * b_part], axis=-1
    ).astype(narrow_dtype)
    grad_one = dot_plain(grad_projected, mix_in)
    grad_start_part, grad_mix_norm = norm_back_one(grad_one)
    grad_start = grad_first + grad_start_part
    smalls = (
        grad_mix_norm,
        grad_kernel.reshape(-1),
        grad_ff_norm_one,
        grad_attn_norm,
        grad_query_gain,
        key_gain_gradient,
        grad_ff_norm_two,
    )
    pieces = [one.reshape(shards, -1) for one in smalls]
    sizes = [one.shape[1] for one in pieces]
    small = jnp.concatenate(pieces + [jnp.zeros((shards, 2048 - sum(sizes)), jnp.float32)], axis=1)
    grad_w_qkv, grad_w_output, grad_mix_out, grad_mix_in, small_sum = tail_call(
        5, [grad_w_qkv, grad_w_output, grad_mix_out], grad_projected, one_blocks,
        small.reshape(shards, 16, 128),
    )
    grad_w_query = grad_w_qkv[: widths[0]]
    grad_w_key = grad_w_qkv[widths[0] : widths[0] + widths[1]]
    grad_w_value = grad_w_qkv[widths[0] + widths[1] :]
    small_out = []
    at = 0
    for one in sizes:
        small_out.append(small_sum[at : at + one])
        at += one
    return (
        final.astype(narrow_dtype)[None],
        grad_start[None],
        small_out[0],
        grad_mix_in,
        small_out[1].reshape(-1, KW),
        grad_mix_out,
        small_out[2],
        ff_one[0],
        ff_one[1],
        ff_one[2],
        small_out[3],
        grad_w_query,
        grad_w_key,
        grad_w_value,
        small_out[4],
        small_out[5],
        grad_w_output,
        small_out[6],
        ff_two[0],
        ff_two[1],
        ff_two[2],
    )


def solution(mesh):
    in_specs = (
        P("fsdp", "ctx", None),
        P("fsdp", "ctx", None),
        P("fsdp"),
        P("fsdp", None),
        P("fsdp", None),
        P("fsdp", None),
        P("fsdp"),
        P("fsdp", None),
        P("fsdp", None),
        P("fsdp", None),
        P("fsdp"),
        P("fsdp", None),
        P("fsdp", None),
        P("fsdp", None),
        P("fsdp"),
        P("fsdp"),
        P("fsdp", None),
        P("fsdp"),
        P("fsdp", None),
        P("fsdp", None),
        P("fsdp", None),
    )
    out_specs = (
        P("fsdp", "ctx", None),
        P("fsdp", "ctx", None),
        P("fsdp"),
        P("fsdp", None),
        P("fsdp", None),
        P("fsdp", None),
        P("fsdp"),
        P("fsdp", None),
        P("fsdp", None),
        P("fsdp", None),
        P("fsdp"),
        P("fsdp", None),
        P("fsdp", None),
        P("fsdp", None),
        P("fsdp"),
        P("fsdp"),
        P("fsdp", None),
        P("fsdp"),
        P("fsdp", None),
        P("fsdp", None),
        P("fsdp", None),
    )
    return jax.shard_map(local, mesh=mesh, in_specs=in_specs, out_specs=out_specs, check_vma=False)
```

```python
from functools import partial

import jax
import jax.numpy as jnp
from jax import lax
from jax.experimental import pallas as pl
from jax.experimental.pallas import tpu as pltpu
from jax.sharding import PartitionSpec as P

MODEL_WIDTH = 1536
QUERY_HEADS = 24
KEY_VALUE_HEADS = 8
HEAD_SIZE = 64
KW = 3


EPS = 1e-05
THETA = 1000000.0
NEG = -1e30


def extended_2(array, sides, width):
    for axis, dim in sides:
        size, length = (lax.axis_size(axis), array.shape[dim])
        up = [(i, (i + 1) % size) for i in range(size - 1)]
        down = [(j, i) for i, j in up]
        last = lax.slice_in_dim(array, length - width, length, axis=dim)
        first = lax.slice_in_dim(array, 0, width, axis=dim)
        before = lax.ppermute(last, axis, up)
        after = lax.ppermute(first, axis, down)
        array = jnp.concatenate([before, array, after], axis=dim)
    return array


def rms_scale(value, gain):
    return value * lax.rsqrt(jnp.mean(value * value, axis=-1, keepdims=True) + EPS) * gain


def rotate(value, angles):
    half_dim = value.shape[1] // 2
    cosine = jnp.cos(angles)
    sine = jnp.sin(angles)
    first = value[:, :half_dim]
    second = value[:, half_dim:]
    return jnp.concatenate(
        [first * cosine - second * sine, second * cosine + first * sine], axis=1
    )


def head_prep(raw, gain, angles):
    heads = raw.reshape(-1, gain.shape[0], raw.shape[1])
    mean = jnp.mean(heads * heads, axis=1, keepdims=True)
    return rotate(heads * lax.rsqrt(mean + EPS) * gain[:, None], angles)


def dot_rows(left, right):
    return lax.dot_general(
        left, right, (((1,), (1,)), ((), ())), preferred_element_type=jnp.float32
    )


def dot_cols(left, right):
    return lax.dot_general(
        left, right, (((0,), (0,)), ((), ())), preferred_element_type=jnp.float32
    )


def dot_plain(left, right):
    return jnp.dot(left, right, preferred_element_type=jnp.float32)


def swish_product(gate_val, up_val):
    return jax.nn.silu(gate_val) * up_val


def dealt_places(index, block, ctx_count):
    device = index // (2 * block)
    within = index % (2 * block)
    which = jnp.where(within < block, device, 2 * ctx_count - 1 - device)
    return which * block + within % block


def conv_apply(extended, kernel):
    sequence_length = extended.shape[0] - KW + 1
    total = extended[0:sequence_length] * kernel[:, 0]
    for place in range(1, KW):
        total = total + extended[place : place + sequence_length] * kernel[:, place]
    return total


def conv_input_grad(grad_conv, kernel):
    sequence_length = grad_conv.shape[0] + KW - 1
    padded = jnp.pad(grad_conv, ((KW - 1, KW - 1), (0, 0)))
    total = padded[KW - 1 : KW - 1 + sequence_length] * kernel[:, 0]
    for place in range(1, KW):
        total = total + padded[KW - 1 - place : KW - 1 - place + sequence_length] * kernel[:, place]
    return total


def kernel_grad(extended, grad_conv):
    sequence_length = grad_conv.shape[0]
    columns = [
        jnp.sum(grad_conv * extended[place : place + sequence_length], axis=0)
        for place in range(KW)
    ]
    return jnp.stack(columns, axis=1)


def pick(value, index, axis):
    return lax.dynamic_index_in_dim(value, index, axis, keepdims=False)


MESH = pl.DeviceIdType.MESH


def dims_nt(left, right):
    return lax.dot_general(
        left, right, (((1,), (1,)), ((), ())), preferred_element_type=jnp.float32
    )


def dims_tn(left, right):
    return lax.dot_general(
        left, right, (((0,), (0,)), ((), ())), preferred_element_type=jnp.float32
    )


def ff_call(mode, ident, x, gate, up_w, down, given=None):
    size = lax.axis_size("fsdp")
    chips = size // 2
    rows, width = x.shape
    units = gate.shape[0]
    forward = mode == "forward"
    bf16 = jnp.bfloat16
    blocks = jax.ShapeDtypeStruct((size, rows, width), bf16)
    vmem = pl.BlockSpec(memory_space=pltpu.VMEM)
    anywhere = pl.BlockSpec(memory_space=pl.ANY)
    outs = [jax.ShapeDtypeStruct((rows, width), jnp.float32)] + [blocks] * forward
    out_specs = [vmem] * len(outs)
    args = [x, gate, up_w, down]
    specs = [vmem] + [anywhere] * 3
    dma = pltpu.SemaphoreType.DMA
    scratch = [] if forward else [pltpu.VMEM(blocks.shape, bf16)]
    scratch += [pltpu.VMEM(gate.shape, bf16)] * 3 + [dma((3,))]
    scratch += [pltpu.VMEM((rows, width), jnp.float32)]
    scratch += [pltpu.VMEM((chips, rows, width), bf16)] * 3
    scratch += [pltpu.VMEM((chips + 1, rows, width), bf16)]
    scratch += [dma((chips,))] * 8 + [dma((chips, 4))] * 4
    if not forward:
        for share in (1, 2) if mode == "both" else (3,):
            outs.append(jax.ShapeDtypeStruct((share * units, width), bf16))
            out_specs.append(anywhere)
        if mode == "both":
            outs.append(blocks)
            out_specs.append(anywhere)
        args.insert(1, given)
        specs.insert(1, anywhere)
        scratch += [pltpu.VMEM(blocks.shape, bf16)]
        scratch += [pltpu.VMEM((units, size * rows), bf16)] * 3
        scratch += [pltpu.VMEM((2, units, 256), bf16), dma((size,)), dma((2,))]
        if mode == "both":
            scratch += [pltpu.VMEM((2, rows, width), bf16), dma((2,))]
    products = 3 if forward else 9
    return pl.pallas_call(
        partial(ff_kernel, chips, mode),
        out_shape=outs,
        in_specs=specs,
        out_specs=out_specs,
        scratch_shapes=scratch,
        compiler_params=pltpu.CompilerParams(
            collective_id=ident, has_side_effects=True, vmem_limit_bytes=61 * 2**20
        ),
        cost_estimate=pl.CostEstimate(
            flops=2 * products * size * rows * units * width,
            bytes_accessed=4 * size * rows * width,
            transcendentals=size * rows * units,
        ),
    )(*args)


def places():
    count = lax.axis_size("fsdp") // 2
    place = lax.axis_index("fsdp")
    chip = place // 2
    core = place % 2
    after = lax.rem(chip + 1, count) * 2 + core
    before = lax.rem(chip + count - 1, count) * 2 + core
    return place, chip, core, after, before, chip * 2 + 1 - core


def greet(targets):
    barrier = pltpu.get_barrier_semaphore()
    for target in targets:
        pl.semaphore_signal(barrier, inc=1, device_id=target, device_id_type=MESH)
    pl.semaphore_wait(barrier, len(targets))


def push(src, dst, send, recv, target):
    return pltpu.make_async_remote_copy(
        src_ref=src, dst_ref=dst, send_sem=send, recv_sem=recv,
        device_id=target, device_id_type=MESH,
    )


def ff_kernel(chips, mode, *refs):
    forward = mode == "forward"
    if forward:
        x_ref, gate, up_w, down, out, xall = refs[:6]
        rest = refs[6:]
    elif mode == "both":
        x_ref, y_hbm, gate, up_w, down, out, gate_grads, weight_grads, result, xall = refs[:10]
        rest = refs[10:]
    else:
        x_ref, y_hbm, gate, up_w, down, out, weight_grads, xall = refs[:8]
        rest = refs[8:]
    weights = (gate, up_w, down)
    gate, up_w, down, weight_m, part, term, other_send, other_recv, in_sum = rest[:9]
    (up_s, up_r, down_s, down_r, core_s, core_r, ps_s, ps_r, ups_s, ups_r, downs_s, downs_r) = rest[9:21]
    if not forward:
        yall, hid, dgate, dup, stage, ysem, stage_sem = rest[21:28]
        if mode == "both":
            out_stage, out_sem = rest[28:]
    rows, width = x_ref.shape
    units = gate.shape[0]
    place, chip, core, _, _, peer = places()
    low_side = chip > 0
    high_side = chip < chips - 1
    below = {"fsdp": lax.rem(place + 2 * chips - 2, 2 * chips)}
    above = {"fsdp": lax.rem(place + 2, 2 * chips)}
    pieces = 4
    piece = rows // pieces
    loads = [
        pltpu.make_async_copy(one, into, weight_m.at[n])
        for n, (one, into) in enumerate(zip(weights, (gate, up_w, down)))
    ]
    for one in loads:
        one.start()
    greet([below, above, {"fsdp": peer}])

    def up_rows(d):
        block = xall.at[2 * d + core]
        return push(block, block, up_s.at[d], up_r.at[d], above)

    def down_rows(d):
        block = xall.at[2 * d + core]
        return push(block, block, down_s.at[d], down_r.at[d], below)

    def core_copy(d):
        block = xall.at[2 * d + core]
        return push(block, block, core_s.at[d], core_r.at[d], {"fsdp": peer})

    def core_in(d):
        block = xall.at[2 * d + 1 - core]
        return push(block, block, core_s.at[d], core_r.at[d], {"fsdp": peer})

    def part_copy(d):
        return push(other_send.at[d], other_recv.at[d], ps_s.at[d], ps_r.at[d], {"fsdp": peer})

    def span(b):
        return pl.ds(pl.multiple_of(b * piece, piece), piece)

    def up_sum(d, b):
        return push(
            term.at[d, span(b)], in_sum.at[d + 1, span(b)], ups_s.at[d, b], ups_r.at[d, b], above
        )

    def down_sum(d, b):
        return push(
            term.at[d, span(b)], in_sum.at[d, span(b)], downs_s.at[d, b], downs_r.at[d, b], below
        )

    def y_copy(s):
        return pltpu.make_async_copy(y_hbm.at[s], yall.at[s], ysem.at[s])

    def across(s):
        return pl.ds(pl.multiple_of(s * rows, rows), rows)

    def block(s):
        x = xall[s]
        if forward:
            gate_val = dims_nt(gate[...], x)
            up_val = dims_nt(up_w[...], x)
            hidden = (gate_val / (1.0 + jnp.exp(-gate_val)) * up_val).astype(jnp.bfloat16)
            return dims_tn(hidden, down[...])
        y_copy(s).wait()
        y = yall[s]
        a, g = (x, y) if mode == "both" else (y, x)
        gate_val = dims_nt(gate[...], a)
        up_val = dims_nt(up_w[...], a)
        grad_hidden = dims_nt(down[...], g)
        sig = 1.0 / (1.0 + jnp.exp(-gate_val))
        act = gate_val * sig
        grad_up = (grad_hidden * act).astype(jnp.bfloat16)
        grad_gate = (
            grad_hidden * up_val * (sig * (1.0 + gate_val * (1.0 - sig)))
        ).astype(jnp.bfloat16)
        hid[:, across(s)] = (act * up_val).astype(jnp.bfloat16)
        dup[:, across(s)] = grad_up
        dgate[:, across(s)] = grad_gate
        return dims_tn(grad_gate, gate[...]) + dims_tn(grad_up, up_w[...])

    xall[place] = x_ref[...]
    if not forward:
        @pl.loop(0, 2 * chips)
        def _(s):
            y_copy(s).start()

    @pl.when(high_side)
    def _():
        up_rows(chip).start()

    @pl.when(low_side)
    def _():
        down_rows(chip).start()

    inside = low_side & high_side
    reach = jnp.minimum(chip, chips - 1 - chip)

    def turn(r):
        far = jnp.where(r <= 2 * reach, (r + 1) // 2, r - reach)
        downward = jnp.where(r <= 2 * reach, r % 2 == 1, chip > chips - 1 - chip)
        return jnp.where(downward, chip - far, chip + far)

    def receive(r):
        d = turn(r)

        @pl.when(d < chip)
        def _():
            up_rows(d).wait_recv()

            @pl.when(high_side)
            def _():
                up_rows(d).start()

        @pl.when(d > chip)
        def _():
            down_rows(d).wait_recv()

            @pl.when(low_side)
            def _():
                down_rows(d).start()

        core_copy(d).start()

    core_copy(chip).start()

    @pl.loop(0, chips)
    def _(r):
        @pl.when((r == 1) | ((r > 1) & ~inside))
        def _():
            receive(r)

        @pl.when((r >= 1) & (r < chips - 1) & inside)
        def _():
            receive(r + 1)

        d = turn(r)

        @pl.when(r == 0)
        def _():
            for one in loads:
                one.wait()

        @pl.loop(0, 2)
        def _(o):
            @pl.when(o == 1)
            def _():
                core_in(d).wait_recv()

            value = block(2 * d + (core + o) % 2)

            @pl.when(o == 0)
            def _():
                part[...] = value

            @pl.when(o == 1)
            def _():
                other_send[d] = value.astype(jnp.bfloat16)
                part_copy(d).start()

        part_copy(d).wait_recv()

        @pl.when(d == chip)
        def _():
            out[...] = part[...] + other_recv[d].astype(jnp.float32)

        @pl.when(d != chip)
        def _():
            term[d] = (part[...] + other_recv[d].astype(jnp.float32)).astype(jnp.bfloat16)

        @pl.when((d > chip) & (chip == 0))
        def _():
            for b in range(pieces):
                up_sum(d, b).start()

        @pl.when((d < chip) & (chip == chips - 1))
        def _():
            for b in range(pieces):
                down_sum(d, b).start()

    lag = 2
    items = (chips - 2) * pieces
    relays = items + lag * max(chips - 3, 0)

    def relay(n):
        rise = n - lag * (chip - 1)
        fall = n - lag * (chips - 2 - chip)
        high = jnp.maximum(rise, 0) // pieces + 2
        low = chips - 3 - jnp.maximum(fall, 0) // pieces

        @pl.when((rise >= 0) & (rise < items) & (high > chip) & low_side)
        def _():
            b = rise % pieces
            up_sum(high, b).wait_recv()
            term[high, span(b)] = (
                term[high, span(b)].astype(jnp.float32)
                + in_sum[high + 1, span(b)].astype(jnp.float32)
            ).astype(jnp.bfloat16)
            up_sum(high, b).start()

        @pl.when((fall >= 0) & (fall < items) & (low < chip) & high_side)
        def _():
            b = fall % pieces
            down_sum(low, b).wait_recv()
            term[low, span(b)] = (
                term[low, span(b)].astype(jnp.float32) + in_sum[low, span(b)].astype(jnp.float32)
            ).astype(jnp.bfloat16)
            down_sum(low, b).start()

    if forward:
        @pl.loop(0, relays)
        def _(n):
            relay(n)
    else:
        step = stage.shape[2]
        steps = width // step
        gate_right, hid_right = (xall, yall) if mode == "both" else (yall, xall)
        pairs = ((dgate, gate_right), (dup, gate_right), (hid, hid_right))

        def stage_copy(n, j):
            there, at = weight_grads, n
            if mode == "both":
                there, at = (gate_grads, 0) if n == 0 else (weight_grads, n - 1)
            there = there.at[
                pl.ds(at * units, units), pl.ds(pl.multiple_of(j * step, step), step)
            ]
            return pltpu.make_async_copy(stage.at[j % 2], there, stage_sem.at[j % 2])

        @pl.loop(0, max(2 * relays, 3 * steps))
        def _(m):
            @pl.when((m % 2 == 0) & (m < 2 * relays))
            def _():
                relay(m // 2)

            j = m % steps
            for n, (left, right) in enumerate(pairs):
                @pl.when(m // steps == n)
                def _():
                    @pl.when(m >= 2)
                    def _():
                        stage_copy(n, j).wait()

                    at = pl.ds(pl.multiple_of(j * step, step), step)
                    sums = jnp.dot(
                        left[...],
                        right[:, :, at].reshape(2 * chips * rows, step),
                        preferred_element_type=jnp.float32,
                    )
                    stage[j % 2] = sums.astype(jnp.bfloat16)
                    stage_copy(n, j).start()

        for j in range(2):
            stage_copy(2, j).wait()
        if mode == "both":
            def result_copy(s):
                return pltpu.make_async_copy(out_stage.at[s % 2], result.at[s], out_sem.at[s % 2])

            @pl.loop(0, 2 * chips)
            def _(s):
                @pl.when(s >= 2)
                def _():
                    result_copy(s).wait()

                out_stage[s % 2] = dims_tn(hid[:, across(s)], down[...]).astype(jnp.bfloat16)
                result_copy(s).start()

            for s in range(2):
                result_copy(s).wait()

    @pl.when(low_side)
    def _():
        for b in range(pieces):
            up_sum(chip, b).wait_recv()
        out[...] += in_sum[chip + 1].astype(jnp.float32)

    @pl.when(high_side)
    def _():
        for b in range(pieces):
            down_sum(chip, b).wait_recv()
        out[...] += in_sum[chip].astype(jnp.float32)

    @pl.loop(0, chips)
    def _(d):
        core_copy(d).wait_send()
        part_copy(d).wait_send()

        @pl.when((d <= chip) & high_side)
        def _():
            up_rows(d).wait_send()

        @pl.when((d >= chip) & low_side)
        def _():
            down_rows(d).wait_send()

        @pl.when(d > chip)
        def _():
            for b in range(pieces):
                up_sum(d, b).wait_send()

        @pl.when(d < chip)
        def _():
            for b in range(pieces):
                down_sum(d, b).wait_send()


def head_kernel(chips, count, *refs):
    shards = refs[:2]
    block, vector, edge = refs[2:5]
    wholes = refs[5:7]
    blocks, vectors, edges = refs[7:10]
    local, near_s, near_r, hop_s, hop_r, side_s, side_r, pass_s, pass_r, edge_s, edge_r = refs[10:]
    place, chip, core, after, before, peer = places()
    here = lax.axis_index("ctx")
    others = [{"ctx": lax.rem(here + t, count)} for t in range(1, count)]
    greet([{"fsdp": before}, {"fsdp": peer}] + others)
    started = []

    def go(copy):
        copy.start()
        started.append(copy)

    def shard_of(k):
        return lax.rem(chip + chips - k, chips) * 2 + core

    def hop(k, n):
        owner = shard_of(k)
        if n < 2:
            src = shards[n].at[here] if k == 0 else wholes[n].at[owner, here]
            dst = wholes[n].at[owner, here]
        elif n == 2:
            src = block if k == 0 else blocks.at[owner]
            dst = blocks.at[owner]
        else:
            src = vector if k == 0 else vectors.at[owner]
            dst = vectors.at[owner]
        return push(src, dst, hop_s.at[n, k], hop_r.at[n, k], {"fsdp": after})

    def side(k, t, n):
        piece = wholes[n].at[shard_of(k), here]
        return push(piece, piece, side_s.at[n, k, t], side_r.at[n, k, t], others[t - 1])

    def side_in(k, t, n):
        piece = wholes[n].at[shard_of(k), lax.rem(here + count - t, count)]
        return piece, push(piece, piece, side_s.at[n, k, t], side_r.at[n, k, t], others[t - 1])

    def across(k, t, n):
        if n == 2:
            src = dst = blocks.at[shard_of(k)]
        elif n == 3:
            src = dst = vectors.at[shard_of(k)]
        else:
            src = dst = wholes[n].at[shard_of(k), lax.rem(here + count - t, count)]
        return push(src, dst, pass_s.at[n, k, t], pass_r.at[n, k, t], {"fsdp": peer})

    def across_in(k, t, n):
        owner = lax.rem(chip + chips - k, chips) * 2 + 1 - core
        if n == 2:
            dst = blocks.at[owner]
        elif n == 3:
            dst = vectors.at[owner]
        else:
            dst = wholes[n].at[owner, lax.rem(here + count - t, count)]
        return push(dst, dst, pass_s.at[n, k, t], pass_r.at[n, k, t], {"fsdp": peer})

    homes = [one.at[place] for one in (*wholes, blocks, vectors)]
    came = [one.at[peer] for one in (*wholes, blocks, vectors)]
    sources = [shards[0], shards[1], block, vector]
    order = (3, 0, 1, 2)

    def edge_copy(t):
        return push(edge, edges.at[t], edge_s.at[t], edge_r.at[t], others[t - 1])

    for t in range(1, count):
        go(edge_copy(t))
    first = pltpu.make_async_copy(edge, edges.at[0], edge_s.at[0])
    first.start()
    for n in order:
        go(hop(0, n))
    keeps = [pltpu.make_async_copy(sources[n], homes[n], local.at[n]) for n in order]
    for one in keeps:
        one.start()
    for n in order:
        go(push(sources[n], homes[n], near_s.at[n], near_r.at[n], {"fsdp": peer}))
    for k in range(1, chips):
        for n in order:
            hop(k - 1, n).wait_recv()
            if k < chips - 1:
                go(hop(k, n))
            if n < 2:
                for t in range(1, count):
                    go(side(k, t, n))
            go(across(k, 0, n))
        if k > 1:
            for n in range(2):
                for t in range(1, count):
                    side_in(k - 1, t, n)[1].wait_recv()
                    go(across(k - 1, t, n))
    for n in range(2):
        for t in range(1, count):
            side_in(chips - 1, t, n)[1].wait_recv()
            go(across(chips - 1, t, n))
    for n in order:
        push(came[n], came[n], near_s.at[n], near_r.at[n], {"fsdp": peer}).wait_recv()
        for k in range(1, chips):
            for t in range(count if n < 2 else 1):
                across_in(k, t, n).wait_recv()
    for t in range(1, count):
        edge_copy(t).wait_recv()
    first.wait()
    for one in keeps:
        one.wait()
    for one in started:
        one.wait_send()


def head_call(ident, shard_a, shard_b, block, vector, edge):
    size = lax.axis_size("fsdp")
    count = lax.axis_size("ctx")
    chips = size // 2
    width = shard_a.shape[1]
    shards = [one.reshape(count, -1, width) for one in (shard_a, shard_b)]
    outs = [jax.ShapeDtypeStruct((size,) + one.shape, jnp.bfloat16) for one in shards]
    outs.append(jax.ShapeDtypeStruct((size,) + block.shape, jnp.bfloat16))
    outs.append(jax.ShapeDtypeStruct((size,) + vector.shape, jnp.bfloat16))
    outs.append(jax.ShapeDtypeStruct((count,) + edge.shape, jnp.bfloat16))
    anywhere = pl.BlockSpec(memory_space=pl.ANY)
    dma = pltpu.SemaphoreType.DMA
    whole_a, whole_b, blocks, vectors, edges = pl.pallas_call(
        partial(head_kernel, chips, count),
        out_shape=outs,
        in_specs=[anywhere] * 5,
        out_specs=[anywhere] * 5,
        scratch_shapes=[
            dma((4,)), dma((4,)), dma((4,)),
            dma((4, chips)), dma((4, chips)),
            dma((2, chips, count)), dma((2, chips, count)),
            dma((4, chips, count)), dma((4, chips, count)),
            dma((count,)), dma((count,)),
        ],
        compiler_params=pltpu.CompilerParams(collective_id=ident, has_side_effects=True),
        cost_estimate=pl.CostEstimate(
            flops=0, bytes_accessed=2 * size * (shard_a.size + shard_b.size) * 2, transcendentals=0
        ),
    )(*shards, block, vector, edge)
    return whole_a.reshape(-1, width), whole_b.reshape(-1, width), blocks, vectors, edges


def tail_kernel(chips, count, pieces, *refs):
    number = len(pieces)
    grads = refs[:number]
    factor, inputs, small = refs[number : number + 3]
    total, total_in, small_total = refs[number + 3 : number + 6]
    rest = refs[number + 6 :]
    own, near, line, in_sum, fin, rc, fs, held, fin_in, rc_in, fs_in, small_in, small_sums = rest[:13]
    (own_m, near_s, near_r, up_s, up_r, down_s, down_r, sc_s, sc_r, ag_s, ag_r, fac_m, fac_s, fac_r,
     sci_s, sci_r, agi_s, agi_r, sm_s, sm_r, smc_s, smc_r) = rest[13:]
    place, chip, core, after, before, peer = places()
    here = lax.axis_index("ctx")
    size = 2 * chips
    chunks = sum(pieces)
    ctx_others = [{"ctx": lax.rem(here + t, count)} for t in range(1, count)]
    shard_others = [{"fsdp": lax.rem(place + t, size)} for t in range(1, size)]
    greet(ctx_others + shard_others)

    def factor_copy(t):
        there = lax.rem(place + t, size)
        return push(factor.at[there], held.at[place], fac_s.at[t], fac_r.at[t], {"fsdp": there})

    def small_copy(t):
        there = lax.rem(place + t, size)
        return push(small.at[there], small_in.at[t], sm_s.at[t], sm_r.at[t], {"fsdp": there})

    def small_share(t):
        return push(
            small_sums.at[0], small_sums.at[t], smc_s.at[t], smc_r.at[t], ctx_others[t - 1]
        )

    for t in range(1, size):
        small_copy(t).start()
        factor_copy(t).start()
    keep = pltpu.make_async_copy(factor.at[place], held.at[place], fac_m)
    keep.start()

    bases = [sum(pieces[:n]) for n in range(number)]

    def near_copy(n, j):
        at = bases[n] + j
        return push(
            grads[n].at[:, 1 - core, j], near.at[at], near_s.at[at], near_r.at[at], {"fsdp": peer}
        )

    def own_copy(n, j):
        at = bases[n] + j
        return pltpu.make_async_copy(grads[n].at[:, core, j], own.at[at], own_m.at[at])

    for n in range(number):
        @pl.loop(0, pieces[n])
        def _(j):
            near_copy(n, j).start()
            own_copy(n, j).start()

    def up_copy(d, j):
        there = {"fsdp": lax.rem(place + 2, size)}
        return push(own.at[j, d], in_sum.at[d + 1, j], up_s.at[d, j], up_r.at[d, j], there)

    def down_copy(d, j):
        there = {"fsdp": lax.rem(place + size - 2, size)}
        return push(own.at[j, d], in_sum.at[d, j], down_s.at[d, j], down_r.at[d, j], there)

    def near_in(j):
        return push(near.at[j], near.at[j], near_s.at[j], near_r.at[j], {"fsdp": peer})

    def own_in(j):
        return pltpu.make_async_copy(own.at[j], own.at[j], own_m.at[j])

    def term(j, owner):
        return own[j, owner].astype(jnp.float32) + near[j, owner].astype(jnp.float32)

    def scatter_copy(j, t):
        there = lax.rem(here + t, count)
        return push(fin.at[j, there], rc.at[j, t], sc_s.at[j, t], sc_r.at[j, t], {"ctx": there})

    def gather_copy(j, t):
        return push(
            fs.at[j], total.at[j, here], ag_s.at[j, t], ag_r.at[j, t], ctx_others[t - 1]
        )

    def gather_in(j, t):
        there = total.at[j, lax.rem(here + count - t, count)]
        return push(there, there, ag_s.at[j, t], ag_r.at[j, t], ctx_others[t - 1])

    def scatter_in_copy(t):
        there = lax.rem(here + t, count)
        return push(fin_in.at[there], rc_in.at[t], sci_s.at[t], sci_r.at[t], {"ctx": there})

    def gather_in_copy(t):
        return push(fs_in, total_in.at[here], agi_s.at[t], agi_r.at[t], ctx_others[t - 1])

    def gather_in_wait(t):
        there = total_in.at[lax.rem(here + count - t, count)]
        return push(there, there, agi_s.at[t], agi_r.at[t], ctx_others[t - 1])

    def products():
        for t in range(1, size):
            src = held.at[lax.rem(place + size - t, size)]
            push(src, src, fac_s.at[t], fac_r.at[t], {"fsdp": peer}).wait_recv()
        keep.wait()

        tall = held.shape[2]
        joined = 1 if tall % 16 else count
        step = 256

        @pl.loop(0, count // joined)
        def _(c):
            @pl.loop(0, inputs.shape[2] // step)
            def _(n):
                at = pl.ds(pl.multiple_of(n * step, step), step)
                sums = 0.0
                for s in range(size):
                    left = held[s].reshape(count * tall, -1) if joined > 1 else held[s, c]
                    sums = sums + jnp.dot(
                        left, inputs[s, :, at], preferred_element_type=jnp.float32
                    )
                sums = sums.astype(jnp.bfloat16)
                if joined > 1:
                    fin_in[:, :, at] = sums.reshape(count, tall, step)
                else:
                    fin_in[c, :, at] = sums

        for t in range(1, count):
            scatter_in_copy(t).start()
        sums = small[place]
        for t in range(1, size):
            small_copy(t).wait_recv()
            sums = sums + small_in[t]
        small_sums[0] = sums
        for t in range(1, count):
            small_share(t).start()

    def products_sum():
        sums = fin_in[here].astype(jnp.float32)
        for t in range(1, count):
            scatter_in_copy(t).wait_recv()
            sums = sums + rc_in[t].astype(jnp.float32)
        fs_in[...] = sums.astype(jnp.bfloat16)
        for t in range(1, count):
            gather_in_copy(t).start()
        total_in[here] = fs_in[...]
        sums = small_sums[0]
        for t in range(1, count):
            small_share(t).wait_recv()
            sums = sums + small_sums[t]
        small_total[...] = sums

    def relay(d, j, arrives, arrived, slot, leave):
        line[...] = term(j, d)

        @pl.when(arrives)
        def _():
            arrived(d, j).wait_recv()
            line[...] += in_sum[slot, j].astype(jnp.float32)

        own[j, d] = line[...].astype(jnp.bfloat16)
        leave(d, j).start()

    lag = 2
    items = (chips - 1) * chunks

    @pl.loop(0, items + lag * (chips - 1))
    def _(i):
        @pl.when(i < chunks)
        def _():
            own_in(i).wait()
            near_in(i).wait_recv()

        rise = i - lag * chip
        upward = chips - 1 - jnp.maximum(rise, 0) // chunks

        @pl.when((rise >= 0) & (rise < items) & (upward > chip))
        def _():
            relay(upward, rise % chunks, chip > 0, up_copy, upward + 1, up_copy)

        fall = i - lag * (chips - 1 - chip)
        downward = jnp.maximum(fall, 0) // chunks

        @pl.when((fall >= 0) & (fall < items) & (downward < chip))
        def _():
            relay(downward, fall % chunks, chip < chips - 1, down_copy, downward, down_copy)

        @pl.when(i == items // 2)
        def _():
            products()

    def reduce_chunk(j):
        sums = fin[j, here].astype(jnp.float32)
        for t in range(1, count):
            scatter_copy(j, t).wait_recv()
            sums = sums + rc[j, t].astype(jnp.float32)
        fs[j] = sums.astype(jnp.bfloat16)
        for t in range(1, count):
            gather_copy(j, t).start()
        total[j, here] = fs[j]

    @pl.loop(0, chunks)
    def _(j):
        line[...] = term(j, chip)

        @pl.when(chip > 0)
        def _():
            up_copy(chip, j).wait_recv()
            line[...] += in_sum[chip + 1, j].astype(jnp.float32)

        @pl.when(chip < chips - 1)
        def _():
            down_copy(chip, j).wait_recv()
            line[...] += in_sum[chip, j].astype(jnp.float32)

        fin[j] = line[...].astype(jnp.bfloat16)
        for t in range(1, count):
            scatter_copy(j, t).start()

        @pl.when(j >= 2)
        def _():
            reduce_chunk(j - 2)

        @pl.when(j == chunks // 2)
        def _():
            products_sum()

    @pl.loop(chunks - 2, chunks)
    def _(j):
        reduce_chunk(j)

    @pl.loop(0, chunks)
    def _(j):
        for t in range(1, count):
            gather_in(j, t).wait_recv()
            gather_copy(j, t).wait_send()
            scatter_copy(j, t).wait_send()

        near_in(j).wait_send()

        @pl.loop(0, chips)
        def _(d):
            @pl.when(d > chip)
            def _():
                up_copy(d, j).wait_send()

            @pl.when(d < chip)
            def _():
                down_copy(d, j).wait_send()

    for t in range(1, count):
        gather_in_wait(t).wait_recv()
        gather_in_copy(t).wait_send()
        scatter_in_copy(t).wait_send()
        small_share(t).wait_send()
    for t in range(1, size):
        small_copy(t).wait_send()
        factor_copy(t).wait_send()


def tail_call(ident, grads, factor, inputs, small):
    size = lax.axis_size("fsdp")
    count = lax.axis_size("ctx")
    chips = size // 2
    width = inputs.shape[2]
    rows = inputs.shape[1]
    unit = min(one.shape[1] for one in grads) // 3
    pieces = [one.shape[1] // unit for one in grads]
    chunks = sum(pieces)
    part = unit // count
    views = [
        one.reshape(chips, 2, n, count, part, width) for one, n in zip(grads, pieces)
    ]
    factor = factor.T.reshape(size, count, -1, rows)
    mine = factor.shape[2]
    bf16 = jnp.bfloat16
    anywhere = pl.BlockSpec(memory_space=pl.ANY)
    vmem = pl.BlockSpec(memory_space=pltpu.VMEM)
    dma = pltpu.SemaphoreType.DMA
    total, total_in, small_total = pl.pallas_call(
        partial(tail_kernel, chips, count, pieces),
        out_shape=[
            jax.ShapeDtypeStruct((chunks, count, part, width), bf16),
            jax.ShapeDtypeStruct((count, mine, width), bf16),
            jax.ShapeDtypeStruct(small.shape[1:], jnp.float32),
        ],
        in_specs=[anywhere] * (len(views) + 1) + [vmem] * 2,
        out_specs=[vmem] * 3,
        scratch_shapes=[
            pltpu.VMEM((chunks, chips, count, part, width), bf16),
            pltpu.VMEM((chunks, chips, count, part, width), bf16),
            pltpu.VMEM((count, part, width), jnp.float32),
            pltpu.VMEM((chips + 1, chunks, count, part, width), bf16),
            pltpu.VMEM((chunks, count, part, width), bf16),
            pltpu.VMEM((chunks, count, part, width), bf16),
            pltpu.VMEM((chunks, part, width), bf16),
            pltpu.VMEM((size, count, mine, rows), bf16),
            pltpu.VMEM((count, mine, width), bf16),
            pltpu.VMEM((count, mine, width), bf16),
            pltpu.VMEM((mine, width), bf16),
            pltpu.VMEM(small.shape, jnp.float32),
            pltpu.VMEM((count,) + small.shape[1:], jnp.float32),
            dma((chunks,)), dma((chunks,)), dma((chunks,)),
            dma((chips, chunks)), dma((chips, chunks)), dma((chips, chunks)), dma((chips, chunks)),
            dma((chunks, count)), dma((chunks, count)), dma((chunks, count)), dma((chunks, count)),
            dma, dma((size,)), dma((size,)),
            dma((count,)), dma((count,)), dma((count,)), dma((count,)),
            dma((size,)), dma((size,)), dma((count,)), dma((count,)),
        ],
        compiler_params=pltpu.CompilerParams(
            collective_id=ident, has_side_effects=True, vmem_limit_bytes=61 * 2**20
        ),
        cost_estimate=pl.CostEstimate(
            flops=2 * size * rows * width * count * mine,
            bytes_accessed=4 * size * chunks * unit * width,
            transcendentals=0,
        ),
    )(*views, factor, inputs, small)
    total = total.reshape(-1, width).astype(jnp.float32)
    outs = []
    at = 0
    for one in grads:
        outs.append(total[at : at + one.shape[1]])
        at += one.shape[1]
    return outs + [total_in.reshape(-1, width).astype(jnp.float32), small_total.reshape(-1)]


def attend_kernel(count, groups, q, kv, att, sums, kv_all, acc, send, recv):
    here = lax.axis_index("ctx")
    others = [{"ctx": lax.rem(here + t, count)} for t in range(1, count)]
    greet(others)
    key_heads = kv.shape[0] // 2
    rows = kv.shape[2]
    block = rows // 2
    scale = HEAD_SIZE ** (-0.5)

    def out_copy(t):
        return push(kv, kv_all.at[here], send.at[t], recv.at[t], others[t - 1])

    def in_copy(t):
        there = kv_all.at[lax.rem(here + count - t, count)]
        return push(there, there, send.at[t], recv.at[t], others[t - 1])

    for t in range(1, count):
        out_copy(t).start()
    kv_all[here] = kv[...]

    def weights(keys, queries, masked):
        value = jnp.exp(dims_tn(keys, queries) * scale)
        if masked:
            allowed = lax.broadcasted_iota(jnp.int32, value.shape, 1) >= lax.broadcasted_iota(
                jnp.int32, value.shape, 0
            )
            value = jnp.where(allowed, value, 0.0)
        return value

    def apply(values, part):
        return jnp.dot(values, part.astype(jnp.bfloat16), preferred_element_type=jnp.float32)

    @pl.loop(0, key_heads, unroll=2)
    def _(h):
        keys = kv[h]
        values = kv[key_heads + h]
        for g in range(groups):
            head = h * groups + g
            queries = q[head]
            part = weights(keys[:, :block], queries, True)
            acc[head] = apply(values[:, :block], part)
            sums[head] = jnp.sum(part, axis=0, keepdims=True)
            part = weights(keys[:, block:], queries[:, block:], True)
            acc[head, :, block:] += apply(values[:, block:], part)
            sums[head, :, block:] += jnp.sum(part, axis=0, keepdims=True)

    for t in range(1, count):
        there = lax.rem(here + count - t, count)
        in_copy(t).wait_recv()

        @pl.when(there < here)
        def _():
            @pl.loop(0, key_heads, unroll=2)
            def _(h):
                keys = kv_all[there, h]
                values = kv_all[there, key_heads + h]
                for g in range(groups):
                    head = h * groups + g
                    part = weights(keys[:, :block], q[head], False)
                    acc[head] += apply(values[:, :block], part)
                    sums[head] += jnp.sum(part, axis=0, keepdims=True)

        @pl.when(there > here)
        def _():
            @pl.loop(0, key_heads, unroll=2)
            def _(h):
                keys = kv_all[there, h]
                values = kv_all[there, key_heads + h]
                for g in range(groups):
                    head = h * groups + g
                    part = weights(keys, q[head][:, block:], False)
                    acc[head, :, block:] += apply(values, part)
                    sums[head, :, block:] += jnp.sum(part, axis=0, keepdims=True)

    @pl.loop(0, key_heads * groups)
    def _(head):
        att[head] = (acc[head] / sums[head]).astype(jnp.bfloat16)

    for t in range(1, count):
        out_copy(t).wait_send()


def attend_call(ident, q, kv):
    count = lax.axis_size("ctx")
    heads, size, rows = q.shape
    groups = heads // (kv.shape[0] // 2)
    vmem = pl.BlockSpec(memory_space=pltpu.VMEM)
    dma = pltpu.SemaphoreType.DMA
    return pl.pallas_call(
        partial(attend_kernel, count, groups),
        out_shape=[
            jax.ShapeDtypeStruct(q.shape, jnp.bfloat16),
            jax.ShapeDtypeStruct((heads, 1, rows), jnp.float32),
            jax.ShapeDtypeStruct((count,) + kv.shape, jnp.bfloat16),
        ],
        in_specs=[vmem] * 2,
        out_specs=[vmem] * 3,
        scratch_shapes=[pltpu.VMEM(q.shape, jnp.float32), dma((count,)), dma((count,))],
        compiler_params=pltpu.CompilerParams(
            collective_id=ident, has_side_effects=True, vmem_limit_bytes=40 * 2**20
        ),
        cost_estimate=pl.CostEstimate(
            flops=4 * heads * size * rows * rows * count,
            bytes_accessed=4 * (q.size + kv.size * count),
            transcendentals=heads * rows * rows * count,
        ),
    )(q, kv)


def attend_back_kernel(
    chips, count, groups, q, kv_all, grad, att, sums, outs, grad_q, grad_kv, result,
    delta, share, send_buf, recv_buf, own, near, out_sum, in_sum,
    send, recv, own_m, near_s, near_r, ring_s, ring_r
):
    place, chip, core, after, before, peer = places()
    here = lax.axis_index("ctx")
    others = [{"ctx": lax.rem(here + t, count)} for t in range(1, count)]
    greet([{"fsdp": before}, {"fsdp": peer}] + others)

    def near_copy(n):
        return push(
            outs.at[2 * n + 1 - core], near.at[n], near_s.at[n], near_r.at[n], {"fsdp": peer}
        )

    def own_copy(n):
        return pltpu.make_async_copy(outs.at[2 * n + core], own.at[n], own_m.at[n])

    def ring_copy(k):
        return push(out_sum.at[k], in_sum.at[k], ring_s.at[k], ring_r.at[k], {"fsdp": after})

    def term(k):
        owner = lax.rem(chip + chips - k, chips)
        own_copy(owner).wait()
        near_copy(owner).wait_recv()
        return own[owner].astype(jnp.float32) + near[owner].astype(jnp.float32)

    def hop(k):
        value = term(k)
        if k > 1:
            ring_copy(k - 2).wait_recv()
            value = value + in_sum[k - 2].astype(jnp.float32)
        out_sum[k - 1] = value.astype(jnp.bfloat16)
        ring_copy(k - 1).start()

    for n in range(chips):
        near_copy(n).start()
        own_copy(n).start()
    key_heads = kv_all.shape[1] // 2
    rows = q.shape[2]
    block = rows // 2
    scale = HEAD_SIZE ** (-0.5)
    every = slice(0, rows)
    front = slice(0, block)
    back = slice(block, rows)

    def copy(t):
        return push(send_buf.at[t], recv_buf.at[t], send.at[t], recv.at[t], others[t - 1])

    @pl.loop(0, key_heads * groups)
    def _(head):
        delta[head] = jnp.sum(
            grad[head].astype(jnp.float32) * att[head].astype(jnp.float32), axis=0, keepdims=True
        )
        share[head] = 1.0 / sums[head]
        grad_q[head] = jnp.zeros(grad_q.shape[1:], jnp.float32)

    def terms(keys, values, head, span, masked):
        queries = q[head][:, span]
        low = grad[head][:, span]
        probs = jnp.exp(dims_tn(keys, queries) * scale) * share[head][:, span]
        if masked:
            allowed = lax.broadcasted_iota(jnp.int32, probs.shape, 1) >= lax.broadcasted_iota(
                jnp.int32, probs.shape, 0
            )
            probs = jnp.where(allowed, probs, 0.0)
        grad_scores = (probs * (dims_tn(values, low) - delta[head][:, span])).astype(jnp.bfloat16)
        grad_q[head, :, span] += (
            jnp.dot(keys, grad_scores, preferred_element_type=jnp.float32) * scale
        )
        return (
            dims_nt(queries, grad_scores) * scale,
            dims_nt(low, probs.astype(jnp.bfloat16)),
        )

    def over_groups(keys, values, h, span, masked):
        grad_keys, grad_values = terms(keys, values, h * groups, span, masked)
        for g in range(1, groups):
            more_keys, more_values = terms(keys, values, h * groups + g, span, masked)
            grad_keys, grad_values = grad_keys + more_keys, grad_values + more_values
        return grad_keys, grad_values

    for t in range(1, max(count, chips)):
        if t >= count:
            hop(t)
            continue
        there = lax.rem(here + t, count)

        @pl.when(there < here)
        def _():
            @pl.loop(0, key_heads, unroll=2)
            def _(h):
                keys = kv_all[there, h][:, front]
                values = kv_all[there, key_heads + h][:, front]
                grad_keys, grad_values = over_groups(keys, values, h, every, False)
                zeros = jnp.zeros((keys.shape[0], rows - block), jnp.bfloat16)
                send_buf[t, h, :, front] = grad_keys.astype(jnp.bfloat16)
                send_buf[t, key_heads + h, :, front] = grad_values.astype(jnp.bfloat16)
                send_buf[t, h, :, back] = zeros
                send_buf[t, key_heads + h, :, back] = zeros

        @pl.when(there > here)
        def _():
            @pl.loop(0, key_heads, unroll=2)
            def _(h):
                keys = kv_all[there, h]
                values = kv_all[there, key_heads + h]
                grad_keys, grad_values = over_groups(keys, values, h, back, False)
                send_buf[t, h] = grad_keys.astype(jnp.bfloat16)
                send_buf[t, key_heads + h] = grad_values.astype(jnp.bfloat16)

        copy(t).start()
        if t < chips:
            hop(t)

    @pl.loop(0, key_heads, unroll=2)
    def _(h):
        keys = kv_all[here, h]
        values = kv_all[here, key_heads + h]
        grad_keys, grad_values = over_groups(keys[:, front], values[:, front], h, every, True)
        grad_kv[h, :, front] = grad_keys
        grad_kv[key_heads + h, :, front] = grad_values
        grad_keys, grad_values = over_groups(keys[:, back], values[:, back], h, back, True)
        grad_kv[h, :, back] = grad_keys
        grad_kv[key_heads + h, :, back] = grad_values

    for t in range(1, count):
        copy(t).wait_recv()

        @pl.loop(0, 2 * key_heads)
        def _(h):
            grad_kv[h] += recv_buf[t, h].astype(jnp.float32)

    value = term(0)
    ring_copy(chips - 2).wait_recv()
    result[...] = value + in_sum[chips - 2].astype(jnp.float32)
    for t in range(1, count):
        copy(t).wait_send()
    for n in range(chips):
        near_copy(n).wait_send()
    for k in range(chips - 1):
        ring_copy(k).wait_send()


def attend_back_call(ident, q, kv_all, grad, att, sums, outs):
    count = lax.axis_size("ctx")
    heads, size, rows = q.shape
    kv_shape = kv_all.shape[1:]
    chips = outs.shape[0] // 2
    block = outs.shape[1:]
    groups = heads // (kv_shape[0] // 2)
    vmem = pl.BlockSpec(memory_space=pltpu.VMEM)
    dma = pltpu.SemaphoreType.DMA
    return pl.pallas_call(
        partial(attend_back_kernel, chips, count, groups),
        out_shape=[
            jax.ShapeDtypeStruct(q.shape, jnp.float32),
            jax.ShapeDtypeStruct(kv_shape, jnp.float32),
            jax.ShapeDtypeStruct(block, jnp.float32),
        ],
        in_specs=[vmem] * 5 + [pl.BlockSpec(memory_space=pl.ANY)],
        out_specs=[vmem] * 3,
        scratch_shapes=[
            pltpu.VMEM(sums.shape, jnp.float32),
            pltpu.VMEM(sums.shape, jnp.float32),
            pltpu.VMEM(kv_all.shape, jnp.bfloat16),
            pltpu.VMEM(kv_all.shape, jnp.bfloat16),
            pltpu.VMEM((chips,) + block, jnp.bfloat16),
            pltpu.VMEM((chips,) + block, jnp.bfloat16),
            pltpu.VMEM((chips - 1,) + block, jnp.bfloat16),
            pltpu.VMEM((chips - 1,) + block, jnp.bfloat16),
            dma((count,)),
            dma((count,)),
            dma((chips,)),
            dma((chips,)),
            dma((chips,)),
            dma((chips,)),
            dma((chips,)),
        ],
        compiler_params=pltpu.CompilerParams(
            collective_id=ident, has_side_effects=True, vmem_limit_bytes=40 * 2**20
        ),
        cost_estimate=pl.CostEstimate(
            flops=10 * heads * size * rows * rows * count,
            bytes_accessed=4 * (3 * q.size + kv_all.size),
            transcendentals=heads * rows * rows * count,
        ),
    )(q, kv_all, grad, att, sums, outs)


def local(
    hidden_in,
    cotangent,
    norm_mix,
    in_proj,
    conv_kernel,
    out_proj,
    norm_ff1,
    gate1,
    up1,
    down1,
    norm_attn,
    q_proj,
    key_projection,
    value_projection,
    q_norm,
    k_norm,
    o_proj,
    norm_ff2,
    gate2,
    up2,
    down2,
):
    narrow_dtype = jnp.bfloat16
    start = hidden_in[0].astype(jnp.float32)
    token_rows = start.shape[0]
    block = token_rows // 2
    margin = KW - 1
    ctx_count = lax.axis_size("ctx")
    ctx_place = lax.axis_index("ctx")
    is_last = ctx_place == ctx_count - 1
    query_places = dealt_places(
        ctx_place * token_rows + jnp.arange(token_rows, dtype=jnp.int32), block, ctx_count
    )
    freqs = THETA ** (-jnp.arange(HEAD_SIZE // 2, dtype=jnp.float32) * 2.0 / HEAD_SIZE)
    angles = freqs[:, None] * query_places.astype(jnp.float32)[None, :]
    vectors = (
        norm_mix, norm_ff1, norm_attn, norm_ff2, q_norm, k_norm, conv_kernel.reshape(-1)
    )
    lengths = [one.shape[0] for one in vectors]
    vector = jnp.concatenate(vectors)
    vector = jnp.pad(vector, (0, 2048 - sum(lengths))).reshape(16, 128)
    attn_shard = jnp.concatenate([q_proj, key_projection, value_projection, o_proj], axis=0)
    attn_rows = attn_shard.shape[0]
    attn_slice = pick(attn_shard.reshape(ctx_count, -1, MODEL_WIDTH), ctx_place, 0)
    attn_slices = lax.all_gather(attn_slice, "fsdp", axis=0)
    tails = jnp.concatenate(
        [
            hidden_in[0, block - margin : block],
            hidden_in[0, token_rows - margin :],
            jnp.zeros((16 - 2 * margin, MODEL_WIDTH), narrow_dtype),
        ],
        axis=0,
    )
    mix_in, mix_out, given, gathered_vectors, edges = head_call(
        4, in_proj, out_proj, cotangent[0], vector, tails
    )
    edge_rows = jnp.concatenate(
        [
            jnp.where(ctx_place == 0, 0.0, edges[1, :margin]).astype(narrow_dtype),
            jnp.where(is_last, tails[:margin], edges[-1, margin : 2 * margin]),
            tails[2 * margin :],
        ],
        axis=0,
    )
    attn_slices, mix_in = lax.optimization_barrier((attn_slices, mix_in))
    attn_wholes = lax.all_gather(attn_slices, "ctx", axis=1)
    attn_wholes = attn_wholes.reshape(-1, attn_rows, MODEL_WIDTH)
    gathered_vectors = gathered_vectors.reshape(-1, 2048)
    wholes = []
    at = 0
    for one in lengths:
        wholes.append(gathered_vectors[:, at : at + one].reshape(-1))
        at += one
    mix_norm, ff_norm_one, attn_norm, ff_norm_two, query_gain, key_gain, mix_kernel = wholes
    mix_kernel = mix_kernel.reshape(-1, KW)
    kernel = mix_kernel.astype(jnp.float32)
    gain_one = mix_norm.astype(jnp.float32)
    normed_one, norm_back_one = jax.vjp(rms_scale, start, gain_one)
    normed_one_low = normed_one.astype(narrow_dtype)
    edges_low = rms_scale(edge_rows.astype(jnp.float32), gain_one).astype(narrow_dtype)
    projected_all = dot_rows(jnp.concatenate([normed_one_low, edges_low], axis=0), mix_in)
    projected = projected_all[:token_rows]
    edge_mixed = (
        projected_all[token_rows:, :MODEL_WIDTH] * projected_all[token_rows:, 2 * MODEL_WIDTH :]
    ).astype(narrow_dtype)
    b_part = projected[:, :MODEL_WIDTH]
    c_part = projected[:, MODEL_WIDTH : 2 * MODEL_WIDTH]
    x_part = projected[:, 2 * MODEL_WIDTH :]
    mixed_low = (b_part * x_part).astype(narrow_dtype)
    before_front = edge_mixed[:margin]
    before_back = edge_mixed[margin : 2 * margin]
    front_ext = jnp.concatenate([before_front, mixed_low[:block]], axis=0).astype(jnp.float32)
    back_ext = jnp.concatenate([before_back, mixed_low[block:]], axis=0).astype(jnp.float32)
    conv_out = jnp.concatenate(
        [conv_apply(front_ext, kernel), conv_apply(back_ext, kernel)], axis=0
    )
    gated_low = (c_part * conv_out).astype(narrow_dtype)
    first = start + dot_rows(gated_low, mix_out)
    normed_two, norm_back_two = jax.vjp(rms_scale, first, ff_norm_one.astype(jnp.float32))
    ff_out_one, inputs_one = ff_call(
        "forward", 1, normed_two.astype(narrow_dtype), gate1, up1, down1
    )
    one_low, ff_out_one = lax.optimization_barrier((normed_one_low, ff_out_one))
    one_blocks = lax.all_gather(one_low, "fsdp", axis=0)
    second = first + ff_out_one
    attn_parts = []
    at = 0
    for one in (q_proj, key_projection, value_projection, o_proj):
        attn_parts.append(attn_wholes[:, at : at + one.shape[0]].reshape(-1, MODEL_WIDTH))
        at += one.shape[0]
    w_query, w_key, w_value, w_output = attn_parts
    normed_three, norm_back_three = jax.vjp(rms_scale, second, attn_norm.astype(jnp.float32))
    three_low = normed_three.astype(narrow_dtype)
    query_raw = dot_rows(w_query, three_low)
    key_raw = dot_rows(w_key, three_low)
    value_raw = dot_rows(w_value, three_low)
    query_heads, query_back = jax.vjp(
        partial(head_prep, angles=angles), query_raw, query_gain.astype(jnp.float32)
    )
    key_heads, key_back = jax.vjp(
        partial(head_prep, angles=angles), key_raw, key_gain.astype(jnp.float32)
    )
    query_narrow = query_heads.astype(narrow_dtype)
    key_value = jnp.concatenate(
        [key_heads, value_raw.reshape(key_heads.shape)], axis=0
    ).astype(narrow_dtype)
    attended_low, exp_sums, key_value_all = attend_call(6, query_narrow, key_value)
    attended_flat = attended_low.reshape(-1, token_rows)
    third = second + lax.dot_general(
        attended_flat, w_output, (((0,), (1,)), ((), ())), preferred_element_type=jnp.float32
    )
    normed_four, norm_back_four = jax.vjp(rms_scale, third, ff_norm_two.astype(jnp.float32))
    four_low, one_blocks = lax.optimization_barrier((normed_four.astype(narrow_dtype), one_blocks))
    grad_four, two_gate, two_rest, outs_two = ff_call("both", 2, four_low, gate2, up2, down2, given)
    shards = lax.axis_size("fsdp")
    ff_two_gate = lax.psum(two_gate, "ctx")
    grad_final = cotangent[0].astype(jnp.float32)
    grad_third_part, grad_ff_norm_two = norm_back_four(grad_four)
    grad_third = grad_final + grad_third_part
    output_low = grad_third.astype(narrow_dtype)
    attended_gradient = lax.dot_general(
        w_output, output_low, (((0,), (1,)), ((), ())), preferred_element_type=jnp.float32
    )
    grad_w_output = (
        lax.dot_general(
            output_low, attended_flat, (((0,), (1,)), ((), ())), preferred_element_type=jnp.float32
        )
        .astype(narrow_dtype)
        .reshape(lax.axis_size("fsdp"), -1, MODEL_WIDTH)
    )
    grad_query, grad_key_value, ff_out_two = attend_back_call(
        7,
        query_narrow,
        key_value_all,
        attended_gradient.astype(narrow_dtype).reshape(query_narrow.shape),
        attended_low,
        exp_sums,
        outs_two,
    )
    final = third + ff_out_two
    grad_query, ff_two_gate = lax.optimization_barrier((grad_query, ff_two_gate))
    key_count = grad_key_value.shape[0] // 2
    grad_query_raw, grad_query_gain = query_back(grad_query)
    raw_key_gradient, key_gain_gradient = key_back(grad_key_value[:key_count])
    query_grad_low = grad_query_raw.astype(narrow_dtype)
    key_grad_low = raw_key_gradient.astype(narrow_dtype)
    value_grad_low = grad_key_value[key_count:].astype(narrow_dtype).reshape(key_grad_low.shape)
    grad_three = (
        dot_cols(query_grad_low, w_query)
        + dot_cols(key_grad_low, w_key)
        + dot_cols(value_grad_low, w_value)
    )
    grad_rows = [
        one.reshape(shards, -1, token_rows) for one in (query_grad_low, key_grad_low, value_grad_low)
    ]
    widths = [one.shape[1] for one in grad_rows]
    grad_rows = jnp.concatenate(grad_rows, axis=1).reshape(-1, token_rows)
    grad_w_qkv = (
        dot_plain(grad_rows, three_low).astype(narrow_dtype).reshape(shards, sum(widths), -1)
    )
    grad_second_part, grad_attn_norm = norm_back_three(grad_three)
    grad_second = grad_third + grad_second_part
    two_rest, ff_two_gate = lax.optimization_barrier((two_rest, ff_two_gate))
    ff_two_rest = lax.psum(two_rest, "ctx")
    grad_two, one_grads = ff_call(
        "backward", 3, grad_second.astype(narrow_dtype), gate1, up1, down1, inputs_one
    )
    grad_two, one_grads, ff_two_rest = lax.optimization_barrier((grad_two, one_grads, ff_two_rest))
    ff_one = lax.psum(one_grads, "ctx")
    ff_one, ff_two = [
        [
            one[at : at + gate1.shape[0]].astype(jnp.float32)
            for at in range(0, one.shape[0], gate1.shape[0])
        ]
        for one in (ff_one, ff_two_rest)
    ]
    ff_two = [ff_two_gate.astype(jnp.float32)] + ff_two
    grad_first_part, grad_ff_norm_one = norm_back_two(grad_two)
    grad_first = grad_second + grad_first_part
    first_low = grad_first.astype(narrow_dtype)
    grad_gated = dot_plain(first_low, mix_out)
    grad_mix_out = (
        dot_cols(first_low, gated_low).astype(narrow_dtype).reshape(shards, -1, MODEL_WIDTH)
    )
    grad_c_part = grad_gated * conv_out
    grad_conv = grad_gated * c_part
    grad_front_ext = conv_input_grad(grad_conv[:block], kernel)
    grad_back_ext = conv_input_grad(grad_conv[block:], kernel)
    back_before = grad_back_ext[:margin]
    outgoing = jnp.concatenate(
        [grad_front_ext[:margin], jnp.where(is_last, 0.0, back_before)], axis=0
    )
    returned = extended_2(outgoing, (("ctx", 0),), margin)
    from_prev = returned[:margin]
    from_next = returned[returned.shape[0] - margin :]
    own_edge = jnp.where(is_last, back_before, 0.0)
    front_grad = grad_front_ext[margin:]
    back_grad = grad_back_ext[margin:]
    front_grad = jnp.concatenate(
        [front_grad[: block - margin], front_grad[block - margin :] + from_next + own_edge], axis=0
    )
    back_grad = jnp.concatenate(
        [back_grad[: block - margin], back_grad[block - margin :] + from_prev], axis=0
    )
    grad_mixed = jnp.concatenate([front_grad, back_grad], axis=0)
    grad_kernel = kernel_grad(front_ext, grad_conv[:block]) + kernel_grad(
        back_ext, grad_conv[block:]
    )
    grad_projected = jnp.concatenate(
        [grad_mixed * x_part, grad_c_part, grad_mixed * b_part], axis=-1
    ).astype(narrow_dtype)
    grad_one = dot_plain(grad_projected, mix_in)
    grad_start_part, grad_mix_norm = norm_back_one(grad_one)
    grad_start = grad_first + grad_start_part
    smalls = (
        grad_mix_norm,
        grad_kernel.reshape(-1),
        grad_ff_norm_one,
        grad_attn_norm,
        grad_query_gain,
        key_gain_gradient,
        grad_ff_norm_two,
    )
    pieces = [one.reshape(shards, -1) for one in smalls]
    sizes = [one.shape[1] for one in pieces]
    small = jnp.concatenate(pieces + [jnp.zeros((shards, 2048 - sum(sizes)), jnp.float32)], axis=1)
    grad_w_qkv, grad_w_output, grad_mix_out, grad_mix_in, small_sum = tail_call(
        5, [grad_w_qkv, grad_w_output, grad_mix_out], grad_projected, one_blocks,
        small.reshape(shards, 16, 128),
    )
    grad_w_query = grad_w_qkv[: widths[0]]
    grad_w_key = grad_w_qkv[widths[0] : widths[0] + widths[1]]
    grad_w_value = grad_w_qkv[widths[0] + widths[1] :]
    small_out = []
    at = 0
    for one in sizes:
        small_out.append(small_sum[at : at + one])
        at += one
    return (
        final.astype(narrow_dtype)[None],
        grad_start[None],
        small_out[0],
        grad_mix_in,
        small_out[1].reshape(-1, KW),
        grad_mix_out,
        small_out[2],
        ff_one[0],
        ff_one[1],
        ff_one[2],
        small_out[3],
        grad_w_query,
        grad_w_key,
        grad_w_value,
        small_out[4],
        small_out[5],
        grad_w_output,
        small_out[6],
        ff_two[0],
        ff_two[1],
        ff_two[2],
    )


def solution(mesh):
    in_specs = (
        P("fsdp", "ctx", None),
        P("fsdp", "ctx", None),
        P("fsdp"),
        P("fsdp", None),
        P("fsdp", None),
        P("fsdp", None),
        P("fsdp"),
        P("fsdp", None),
        P("fsdp", None),
        P("fsdp", None),
        P("fsdp"),
        P("fsdp", None),
        P("fsdp", None),
        P("fsdp", None),
        P("fsdp"),
        P("fsdp"),
        P("fsdp", None),
        P("fsdp"),
        P("fsdp", None),
        P("fsdp", None),
        P("fsdp", None),
    )
    out_specs = (
        P("fsdp", "ctx", None),
        P("fsdp", "ctx", None),
        P("fsdp"),
        P("fsdp", None),
        P("fsdp", None),
        P("fsdp", None),
        P("fsdp"),
        P("fsdp", None),
        P("fsdp", None),
        P("fsdp", None),
        P("fsdp"),
        P("fsdp", None),
        P("fsdp", None),
        P("fsdp", None),
        P("fsdp"),
        P("fsdp"),
        P("fsdp", None),
        P("fsdp"),
        P("fsdp", None),
        P("fsdp", None),
        P("fsdp", None),
    )
    return jax.shard_map(local, mesh=mesh, in_specs=in_specs, out_specs=out_specs, check_vma=False)
```

```python
from functools import partial

import jax
import jax.numpy as jnp
from jax import lax
from jax.experimental import pallas as pl
from jax.experimental.pallas import tpu as pltpu
from jax.sharding import PartitionSpec as P

MODEL_WIDTH = 1536
QUERY_HEADS = 24
KEY_VALUE_HEADS = 8
HEAD_SIZE = 64
KW = 3


EPS = 1e-05
THETA = 1000000.0
NEG = -1e30


def extended_2(array, sides, width):
    for axis, dim in sides:
        size, length = (lax.axis_size(axis), array.shape[dim])
        up = [(i, (i + 1) % size) for i in range(size - 1)]
        down = [(j, i) for i, j in up]
        last = lax.slice_in_dim(array, length - width, length, axis=dim)
        first = lax.slice_in_dim(array, 0, width, axis=dim)
        before = lax.ppermute(last, axis, up)
        after = lax.ppermute(first, axis, down)
        array = jnp.concatenate([before, array, after], axis=dim)
    return array


def rms_scale(value, gain):
    return value * lax.rsqrt(jnp.mean(value * value, axis=-1, keepdims=True) + EPS) * gain


def rotate(value, angles):
    half_dim = value.shape[1] // 2
    cosine = jnp.cos(angles)
    sine = jnp.sin(angles)
    first = value[:, :half_dim]
    second = value[:, half_dim:]
    return jnp.concatenate(
        [first * cosine - second * sine, second * cosine + first * sine], axis=1
    )


def head_prep(raw, gain, angles):
    heads = raw.reshape(-1, gain.shape[0], raw.shape[1])
    mean = jnp.mean(heads * heads, axis=1, keepdims=True)
    return rotate(heads * lax.rsqrt(mean + EPS) * gain[:, None], angles)


def dot_rows(left, right):
    return lax.dot_general(
        left, right, (((1,), (1,)), ((), ())), preferred_element_type=jnp.float32
    )


def dot_cols(left, right):
    return lax.dot_general(
        left, right, (((0,), (0,)), ((), ())), preferred_element_type=jnp.float32
    )


def dot_plain(left, right):
    return jnp.dot(left, right, preferred_element_type=jnp.float32)


def swish_product(gate_val, up_val):
    return jax.nn.silu(gate_val) * up_val


def dealt_places(index, block, ctx_count):
    device = index // (2 * block)
    within = index % (2 * block)
    which = jnp.where(within < block, device, 2 * ctx_count - 1 - device)
    return which * block + within % block


def conv_apply(extended, kernel):
    sequence_length = extended.shape[0] - KW + 1
    total = extended[0:sequence_length] * kernel[:, 0]
    for place in range(1, KW):
        total = total + extended[place : place + sequence_length] * kernel[:, place]
    return total


def conv_input_grad(grad_conv, kernel):
    sequence_length = grad_conv.shape[0] + KW - 1
    padded = jnp.pad(grad_conv, ((KW - 1, KW - 1), (0, 0)))
    total = padded[KW - 1 : KW - 1 + sequence_length] * kernel[:, 0]
    for place in range(1, KW):
        total = total + padded[KW - 1 - place : KW - 1 - place + sequence_length] * kernel[:, place]
    return total


def kernel_grad(extended, grad_conv):
    sequence_length = grad_conv.shape[0]
    columns = [
        jnp.sum(grad_conv * extended[place : place + sequence_length], axis=0)
        for place in range(KW)
    ]
    return jnp.stack(columns, axis=1)


def pick(value, index, axis):
    return lax.dynamic_index_in_dim(value, index, axis, keepdims=False)


MESH = pl.DeviceIdType.MESH


def dims_nt(left, right):
    return lax.dot_general(
        left, right, (((1,), (1,)), ((), ())), preferred_element_type=jnp.float32
    )


def dims_tn(left, right):
    return lax.dot_general(
        left, right, (((0,), (0,)), ((), ())), preferred_element_type=jnp.float32
    )


def ff_call(mode, ident, x, gate, up_w, down, given=None):
    size = lax.axis_size("fsdp")
    chips = size // 2
    rows, width = x.shape
    units = gate.shape[0]
    forward = mode == "forward"
    bf16 = jnp.bfloat16
    blocks = jax.ShapeDtypeStruct((size, rows, width), bf16)
    vmem = pl.BlockSpec(memory_space=pltpu.VMEM)
    anywhere = pl.BlockSpec(memory_space=pl.ANY)
    outs = [jax.ShapeDtypeStruct((rows, width), jnp.float32)] + [blocks] * forward
    out_specs = [vmem] * len(outs)
    args = [x, gate, up_w, down]
    specs = [vmem] + [anywhere] * 3
    dma = pltpu.SemaphoreType.DMA
    scratch = [] if forward else [pltpu.VMEM(blocks.shape, bf16)]
    scratch += [pltpu.VMEM(gate.shape, bf16)] * 3 + [dma((3,))]
    scratch += [pltpu.VMEM((rows, width), jnp.float32)]
    scratch += [pltpu.VMEM((chips, rows, width), bf16)] * 3
    scratch += [pltpu.VMEM((chips + 1, rows, width), bf16)]
    scratch += [dma((chips,))] * 8 + [dma((chips, 4))] * 4
    if not forward:
        outs.append(jax.ShapeDtypeStruct((3 * units, width), bf16))
        out_specs.append(anywhere)
        if mode == "both":
            outs.append(blocks)
            out_specs.append(anywhere)
        args.insert(1, given)
        specs.insert(1, anywhere)
        scratch += [pltpu.VMEM(blocks.shape, bf16)]
        scratch += [pltpu.VMEM((units, size * rows), bf16)] * 3
        scratch += [pltpu.VMEM((2, units, 256), bf16), dma((size,)), dma((2,))]
        if mode == "both":
            scratch += [pltpu.VMEM((2, rows, width), bf16), dma((2,))]
    products = 3 if forward else 9
    return pl.pallas_call(
        partial(ff_kernel, chips, mode),
        out_shape=outs,
        in_specs=specs,
        out_specs=out_specs,
        scratch_shapes=scratch,
        compiler_params=pltpu.CompilerParams(
            collective_id=ident, has_side_effects=True, vmem_limit_bytes=61 * 2**20
        ),
        cost_estimate=pl.CostEstimate(
            flops=1 if mode == "backward" else 2 * products * size * rows * units * width,
            bytes_accessed=1 if mode == "backward" else 4 * size * rows * width,
            transcendentals=0 if mode == "backward" else size * rows * units,
        ),
    )(*args)


def places():
    count = lax.axis_size("fsdp") // 2
    place = lax.axis_index("fsdp")
    chip = place // 2
    core = place % 2
    after = lax.rem(chip + 1, count) * 2 + core
    before = lax.rem(chip + count - 1, count) * 2 + core
    return place, chip, core, after, before, chip * 2 + 1 - core


def greet(targets):
    barrier = pltpu.get_barrier_semaphore()
    for target in targets:
        pl.semaphore_signal(barrier, inc=1, device_id=target, device_id_type=MESH)
    pl.semaphore_wait(barrier, len(targets))


def push(src, dst, send, recv, target):
    return pltpu.make_async_remote_copy(
        src_ref=src, dst_ref=dst, send_sem=send, recv_sem=recv,
        device_id=target, device_id_type=MESH,
    )


def ff_kernel(chips, mode, *refs):
    forward = mode == "forward"
    if forward:
        x_ref, gate, up_w, down, out, xall = refs[:6]
        rest = refs[6:]
    elif mode == "both":
        x_ref, y_hbm, gate, up_w, down, out, weight_grads, result, xall = refs[:9]
        rest = refs[9:]
    else:
        x_ref, y_hbm, gate, up_w, down, out, weight_grads, xall = refs[:8]
        rest = refs[8:]
    weights = (gate, up_w, down)
    gate, up_w, down, weight_m, part, term, other_send, other_recv, in_sum = rest[:9]
    (up_s, up_r, down_s, down_r, core_s, core_r, ps_s, ps_r, ups_s, ups_r, downs_s, downs_r) = rest[9:21]
    if not forward:
        yall, hid, dgate, dup, stage, ysem, stage_sem = rest[21:28]
        if mode == "both":
            out_stage, out_sem = rest[28:]
    rows, width = x_ref.shape
    units = gate.shape[0]
    place, chip, core, _, _, peer = places()
    low_side = chip > 0
    high_side = chip < chips - 1
    below = {"fsdp": lax.rem(place + 2 * chips - 2, 2 * chips)}
    above = {"fsdp": lax.rem(place + 2, 2 * chips)}
    pieces = 4
    piece = rows // pieces
    loads = [
        pltpu.make_async_copy(one, into, weight_m.at[n])
        for n, (one, into) in enumerate(zip(weights, (gate, up_w, down)))
    ]
    for one in loads:
        one.start()
    greet([below, above, {"fsdp": peer}])

    def up_rows(d):
        block = xall.at[2 * d + core]
        return push(block, block, up_s.at[d], up_r.at[d], above)

    def down_rows(d):
        block = xall.at[2 * d + core]
        return push(block, block, down_s.at[d], down_r.at[d], below)

    def core_copy(d):
        block = xall.at[2 * d + core]
        return push(block, block, core_s.at[d], core_r.at[d], {"fsdp": peer})

    def core_in(d):
        block = xall.at[2 * d + 1 - core]
        return push(block, block, core_s.at[d], core_r.at[d], {"fsdp": peer})

    def part_copy(d):
        return push(other_send.at[d], other_recv.at[d], ps_s.at[d], ps_r.at[d], {"fsdp": peer})

    def span(b):
        return pl.ds(pl.multiple_of(b * piece, piece), piece)

    def up_sum(d, b):
        return push(
            term.at[d, span(b)], in_sum.at[d + 1, span(b)], ups_s.at[d, b], ups_r.at[d, b], above
        )

    def down_sum(d, b):
        return push(
            term.at[d, span(b)], in_sum.at[d, span(b)], downs_s.at[d, b], downs_r.at[d, b], below
        )

    def y_copy(s):
        return pltpu.make_async_copy(y_hbm.at[s], yall.at[s], ysem.at[s])

    def across(s):
        return pl.ds(pl.multiple_of(s * rows, rows), rows)

    def block(s):
        x = xall[s]
        if forward:
            gate_val = dims_nt(gate[...], x)
            up_val = dims_nt(up_w[...], x)
            hidden = (gate_val / (1.0 + jnp.exp(-gate_val)) * up_val).astype(jnp.bfloat16)
            return dims_tn(hidden, down[...])
        y_copy(s).wait()
        y = yall[s]
        a, g = (x, y) if mode == "both" else (y, x)
        gate_val = dims_nt(gate[...], a)
        up_val = dims_nt(up_w[...], a)
        grad_hidden = dims_nt(down[...], g)
        sig = 1.0 / (1.0 + jnp.exp(-gate_val))
        act = gate_val * sig
        grad_up = (grad_hidden * act).astype(jnp.bfloat16)
        grad_gate = (
            grad_hidden * up_val * (sig * (1.0 + gate_val * (1.0 - sig)))
        ).astype(jnp.bfloat16)
        hid[:, across(s)] = (act * up_val).astype(jnp.bfloat16)
        dup[:, across(s)] = grad_up
        dgate[:, across(s)] = grad_gate
        return dims_tn(grad_gate, gate[...]) + dims_tn(grad_up, up_w[...])

    xall[place] = x_ref[...]
    if not forward:
        @pl.loop(0, 2 * chips)
        def _(s):
            y_copy(s).start()

    @pl.when(high_side)
    def _():
        up_rows(chip).start()

    @pl.when(low_side)
    def _():
        down_rows(chip).start()

    inside = low_side & high_side
    reach = jnp.minimum(chip, chips - 1 - chip)

    def turn(r):
        far = jnp.where(r <= 2 * reach, (r + 1) // 2, r - reach)
        downward = jnp.where(r <= 2 * reach, r % 2 == 1, chip > chips - 1 - chip)
        return jnp.where(downward, chip - far, chip + far)

    def receive(r):
        d = turn(r)

        @pl.when(d < chip)
        def _():
            up_rows(d).wait_recv()

            @pl.when(high_side)
            def _():
                up_rows(d).start()

        @pl.when(d > chip)
        def _():
            down_rows(d).wait_recv()

            @pl.when(low_side)
            def _():
                down_rows(d).start()

        core_copy(d).start()

    core_copy(chip).start()

    @pl.loop(0, chips)
    def _(r):
        @pl.when((r == 1) | ((r > 1) & ~inside))
        def _():
            receive(r)

        @pl.when((r >= 1) & (r < chips - 1) & inside)
        def _():
            receive(r + 1)

        d = turn(r)

        @pl.when(r == 0)
        def _():
            for one in loads:
                one.wait()

        @pl.loop(0, 2)
        def _(o):
            @pl.when(o == 1)
            def _():
                core_in(d).wait_recv()

            value = block(2 * d + (core + o) % 2)

            @pl.when(o == 0)
            def _():
                part[...] = value

            @pl.when(o == 1)
            def _():
                other_send[d] = value.astype(jnp.bfloat16)
                part_copy(d).start()

        part_copy(d).wait_recv()

        @pl.when(d == chip)
        def _():
            out[...] = part[...] + other_recv[d].astype(jnp.float32)

        @pl.when(d != chip)
        def _():
            term[d] = (part[...] + other_recv[d].astype(jnp.float32)).astype(jnp.bfloat16)

        @pl.when((d > chip) & (chip == 0))
        def _():
            for b in range(pieces):
                up_sum(d, b).start()

        @pl.when((d < chip) & (chip == chips - 1))
        def _():
            for b in range(pieces):
                down_sum(d, b).start()

    lag = 2
    items = (chips - 2) * pieces
    relays = items + lag * max(chips - 3, 0)

    def relay(n):
        rise = n - lag * (chip - 1)
        fall = n - lag * (chips - 2 - chip)
        high = jnp.maximum(rise, 0) // pieces + 2
        low = chips - 3 - jnp.maximum(fall, 0) // pieces

        @pl.when((rise >= 0) & (rise < items) & (high > chip) & low_side)
        def _():
            b = rise % pieces
            up_sum(high, b).wait_recv()
            term[high, span(b)] = (
                term[high, span(b)].astype(jnp.float32)
                + in_sum[high + 1, span(b)].astype(jnp.float32)
            ).astype(jnp.bfloat16)
            up_sum(high, b).start()

        @pl.when((fall >= 0) & (fall < items) & (low < chip) & high_side)
        def _():
            b = fall % pieces
            down_sum(low, b).wait_recv()
            term[low, span(b)] = (
                term[low, span(b)].astype(jnp.float32) + in_sum[low, span(b)].astype(jnp.float32)
            ).astype(jnp.bfloat16)
            down_sum(low, b).start()

    if forward:
        @pl.loop(0, relays)
        def _(n):
            relay(n)
    else:
        step = stage.shape[2]
        steps = width // step
        gate_right, hid_right = (xall, yall) if mode == "both" else (yall, xall)
        pairs = ((dgate, gate_right), (dup, gate_right), (hid, hid_right))

        def stage_copy(n, j):
            there = weight_grads.at[
                pl.ds(n * units, units), pl.ds(pl.multiple_of(j * step, step), step)
            ]
            return pltpu.make_async_copy(stage.at[j % 2], there, stage_sem.at[j % 2])

        @pl.loop(0, max(2 * relays, 3 * steps))
        def _(m):
            @pl.when((m % 2 == 0) & (m < 2 * relays))
            def _():
                relay(m // 2)

            j = m % steps
            for n, (left, right) in enumerate(pairs):
                @pl.when(m // steps == n)
                def _():
                    @pl.when(m >= 2)
                    def _():
                        stage_copy(n, j).wait()

                    at = pl.ds(pl.multiple_of(j * step, step), step)
                    sums = jnp.dot(
                        left[...],
                        right[:, :, at].reshape(2 * chips * rows, step),
                        preferred_element_type=jnp.float32,
                    )
                    stage[j % 2] = sums.astype(jnp.bfloat16)
                    stage_copy(n, j).start()

        for j in range(2):
            stage_copy(2, j).wait()
        if mode == "both":
            def result_copy(s):
                return pltpu.make_async_copy(out_stage.at[s % 2], result.at[s], out_sem.at[s % 2])

            @pl.loop(0, 2 * chips)
            def _(s):
                @pl.when(s >= 2)
                def _():
                    result_copy(s).wait()

                out_stage[s % 2] = dims_tn(hid[:, across(s)], down[...]).astype(jnp.bfloat16)
                result_copy(s).start()

            for s in range(2):
                result_copy(s).wait()

    @pl.when(low_side)
    def _():
        for b in range(pieces):
            up_sum(chip, b).wait_recv()
        out[...] += in_sum[chip + 1].astype(jnp.float32)

    @pl.when(high_side)
    def _():
        for b in range(pieces):
            down_sum(chip, b).wait_recv()
        out[...] += in_sum[chip].astype(jnp.float32)

    @pl.loop(0, chips)
    def _(d):
        core_copy(d).wait_send()
        part_copy(d).wait_send()

        @pl.when((d <= chip) & high_side)
        def _():
            up_rows(d).wait_send()

        @pl.when((d >= chip) & low_side)
        def _():
            down_rows(d).wait_send()

        @pl.when(d > chip)
        def _():
            for b in range(pieces):
                up_sum(d, b).wait_send()

        @pl.when(d < chip)
        def _():
            for b in range(pieces):
                down_sum(d, b).wait_send()


def head_kernel(chips, count, *refs):
    shards = refs[:2]
    block, vector, edge = refs[2:5]
    wholes = refs[5:7]
    blocks, vectors, edges = refs[7:10]
    local, near_s, near_r, hop_s, hop_r, side_s, side_r, pass_s, pass_r, edge_s, edge_r = refs[10:]
    place, chip, core, after, before, peer = places()
    here = lax.axis_index("ctx")
    others = [{"ctx": lax.rem(here + t, count)} for t in range(1, count)]
    greet([{"fsdp": before}, {"fsdp": peer}] + others)
    started = []

    def go(copy):
        copy.start()
        started.append(copy)

    def shard_of(k):
        return lax.rem(chip + chips - k, chips) * 2 + core

    def hop(k, n):
        owner = shard_of(k)
        if n < 2:
            src = shards[n].at[here] if k == 0 else wholes[n].at[owner, here]
            dst = wholes[n].at[owner, here]
        elif n == 2:
            src = block if k == 0 else blocks.at[owner]
            dst = blocks.at[owner]
        else:
            src = vector if k == 0 else vectors.at[owner]
            dst = vectors.at[owner]
        return push(src, dst, hop_s.at[n, k], hop_r.at[n, k], {"fsdp": after})

    def side(k, t, n):
        piece = wholes[n].at[shard_of(k), here]
        return push(piece, piece, side_s.at[n, k, t], side_r.at[n, k, t], others[t - 1])

    def side_in(k, t, n):
        piece = wholes[n].at[shard_of(k), lax.rem(here + count - t, count)]
        return piece, push(piece, piece, side_s.at[n, k, t], side_r.at[n, k, t], others[t - 1])

    def across(k, t, n):
        if n == 2:
            src = dst = blocks.at[shard_of(k)]
        elif n == 3:
            src = dst = vectors.at[shard_of(k)]
        else:
            src = dst = wholes[n].at[shard_of(k), lax.rem(here + count - t, count)]
        return push(src, dst, pass_s.at[n, k, t], pass_r.at[n, k, t], {"fsdp": peer})

    def across_in(k, t, n):
        owner = lax.rem(chip + chips - k, chips) * 2 + 1 - core
        if n == 2:
            dst = blocks.at[owner]
        elif n == 3:
            dst = vectors.at[owner]
        else:
            dst = wholes[n].at[owner, lax.rem(here + count - t, count)]
        return push(dst, dst, pass_s.at[n, k, t], pass_r.at[n, k, t], {"fsdp": peer})

    homes = [one.at[place] for one in (*wholes, blocks, vectors)]
    came = [one.at[peer] for one in (*wholes, blocks, vectors)]
    sources = [shards[0], shards[1], block, vector]
    order = (3, 0, 1, 2)

    def edge_copy(t):
        return push(edge, edges.at[t], edge_s.at[t], edge_r.at[t], others[t - 1])

    for t in range(1, count):
        go(edge_copy(t))
    first = pltpu.make_async_copy(edge, edges.at[0], edge_s.at[0])
    first.start()
    for n in order:
        go(hop(0, n))
    keeps = [pltpu.make_async_copy(sources[n], homes[n], local.at[n]) for n in order]
    for one in keeps:
        one.start()
    for n in order:
        go(push(sources[n], homes[n], near_s.at[n], near_r.at[n], {"fsdp": peer}))
    for k in range(1, chips):
        for n in order:
            hop(k - 1, n).wait_recv()
            if k < chips - 1:
                go(hop(k, n))
            if n < 2:
                for t in range(1, count):
                    go(side(k, t, n))
            go(across(k, 0, n))
        if k > 1:
            for n in range(2):
                for t in range(1, count):
                    side_in(k - 1, t, n)[1].wait_recv()
                    go(across(k - 1, t, n))
    for n in range(2):
        for t in range(1, count):
            side_in(chips - 1, t, n)[1].wait_recv()
            go(across(chips - 1, t, n))
    for n in order:
        push(came[n], came[n], near_s.at[n], near_r.at[n], {"fsdp": peer}).wait_recv()
        for k in range(1, chips):
            for t in range(count if n < 2 else 1):
                across_in(k, t, n).wait_recv()
    for t in range(1, count):
        edge_copy(t).wait_recv()
    first.wait()
    for one in keeps:
        one.wait()
    for one in started:
        one.wait_send()


def head_call(ident, shard_a, shard_b, block, vector, edge):
    size = lax.axis_size("fsdp")
    count = lax.axis_size("ctx")
    chips = size // 2
    width = shard_a.shape[1]
    shards = [one.reshape(count, -1, width) for one in (shard_a, shard_b)]
    outs = [jax.ShapeDtypeStruct((size,) + one.shape, jnp.bfloat16) for one in shards]
    outs.append(jax.ShapeDtypeStruct((size,) + block.shape, jnp.bfloat16))
    outs.append(jax.ShapeDtypeStruct((size,) + vector.shape, jnp.bfloat16))
    outs.append(jax.ShapeDtypeStruct((count,) + edge.shape, jnp.bfloat16))
    anywhere = pl.BlockSpec(memory_space=pl.ANY)
    dma = pltpu.SemaphoreType.DMA
    whole_a, whole_b, blocks, vectors, edges = pl.pallas_call(
        partial(head_kernel, chips, count),
        out_shape=outs,
        in_specs=[anywhere] * 5,
        out_specs=[anywhere] * 5,
        scratch_shapes=[
            dma((4,)), dma((4,)), dma((4,)),
            dma((4, chips)), dma((4, chips)),
            dma((2, chips, count)), dma((2, chips, count)),
            dma((4, chips, count)), dma((4, chips, count)),
            dma((count,)), dma((count,)),
        ],
        compiler_params=pltpu.CompilerParams(collective_id=ident, has_side_effects=True),
        cost_estimate=pl.CostEstimate(
            flops=0, bytes_accessed=2 * size * (shard_a.size + shard_b.size) * 2, transcendentals=0
        ),
    )(*shards, block, vector, edge)
    return whole_a.reshape(-1, width), whole_b.reshape(-1, width), blocks, vectors, edges


def tail_kernel(chips, count, pieces, *refs):
    number = len(pieces)
    grads = refs[:number]
    factor, inputs, small = refs[number : number + 3]
    total, total_in, small_total = refs[number + 3 : number + 6]
    rest = refs[number + 6 :]
    own, near, line, in_sum, fin, rc, fs, held, fin_in, rc_in, fs_in, small_in, small_sums = rest[:13]
    (own_m, near_s, near_r, up_s, up_r, down_s, down_r, sc_s, sc_r, ag_s, ag_r, fac_m, fac_s, fac_r,
     sci_s, sci_r, agi_s, agi_r, sm_s, sm_r, smc_s, smc_r) = rest[13:]
    place, chip, core, after, before, peer = places()
    here = lax.axis_index("ctx")
    size = 2 * chips
    chunks = sum(pieces)
    ctx_others = [{"ctx": lax.rem(here + t, count)} for t in range(1, count)]
    shard_others = [{"fsdp": lax.rem(place + t, size)} for t in range(1, size)]
    greet(ctx_others + shard_others)

    def factor_copy(t):
        there = lax.rem(place + t, size)
        return push(factor.at[there], held.at[place], fac_s.at[t], fac_r.at[t], {"fsdp": there})

    def small_copy(t):
        there = lax.rem(place + t, size)
        return push(small.at[there], small_in.at[t], sm_s.at[t], sm_r.at[t], {"fsdp": there})

    def small_share(t):
        return push(
            small_sums.at[0], small_sums.at[t], smc_s.at[t], smc_r.at[t], ctx_others[t - 1]
        )

    for t in range(1, size):
        small_copy(t).start()
        factor_copy(t).start()
    keep = pltpu.make_async_copy(factor.at[place], held.at[place], fac_m)
    keep.start()

    bases = [sum(pieces[:n]) for n in range(number)]

    def near_copy(n, j):
        at = bases[n] + j
        return push(
            grads[n].at[:, 1 - core, j], near.at[at], near_s.at[at], near_r.at[at], {"fsdp": peer}
        )

    def own_copy(n, j):
        at = bases[n] + j
        return pltpu.make_async_copy(grads[n].at[:, core, j], own.at[at], own_m.at[at])

    for n in range(number):
        @pl.loop(0, pieces[n])
        def _(j):
            near_copy(n, j).start()
            own_copy(n, j).start()

    def up_copy(d, j):
        there = {"fsdp": lax.rem(place + 2, size)}
        return push(own.at[j, d], in_sum.at[d + 1, j], up_s.at[d, j], up_r.at[d, j], there)

    def down_copy(d, j):
        there = {"fsdp": lax.rem(place + size - 2, size)}
        return push(own.at[j, d], in_sum.at[d, j], down_s.at[d, j], down_r.at[d, j], there)

    def near_in(j):
        return push(near.at[j], near.at[j], near_s.at[j], near_r.at[j], {"fsdp": peer})

    def own_in(j):
        return pltpu.make_async_copy(own.at[j], own.at[j], own_m.at[j])

    def term(j, owner):
        return own[j, owner].astype(jnp.float32) + near[j, owner].astype(jnp.float32)

    def scatter_copy(j, t):
        there = lax.rem(here + t, count)
        return push(fin.at[j, there], rc.at[j, t], sc_s.at[j, t], sc_r.at[j, t], {"ctx": there})

    def gather_copy(j, t):
        return push(
            fs.at[j], total.at[j, here], ag_s.at[j, t], ag_r.at[j, t], ctx_others[t - 1]
        )

    def gather_in(j, t):
        there = total.at[j, lax.rem(here + count - t, count)]
        return push(there, there, ag_s.at[j, t], ag_r.at[j, t], ctx_others[t - 1])

    def scatter_in_copy(t):
        there = lax.rem(here + t, count)
        return push(fin_in.at[there], rc_in.at[t], sci_s.at[t], sci_r.at[t], {"ctx": there})

    def gather_in_copy(t):
        return push(fs_in, total_in.at[here], agi_s.at[t], agi_r.at[t], ctx_others[t - 1])

    def gather_in_wait(t):
        there = total_in.at[lax.rem(here + count - t, count)]
        return push(there, there, agi_s.at[t], agi_r.at[t], ctx_others[t - 1])

    def products():
        for t in range(1, size):
            src = held.at[lax.rem(place + size - t, size)]
            push(src, src, fac_s.at[t], fac_r.at[t], {"fsdp": peer}).wait_recv()
        keep.wait()

        tall = held.shape[2]
        joined = 1 if tall % 16 else count
        step = 256

        @pl.loop(0, count // joined)
        def _(c):
            @pl.loop(0, inputs.shape[2] // step)
            def _(n):
                at = pl.ds(pl.multiple_of(n * step, step), step)
                sums = 0.0
                for s in range(size):
                    left = held[s].reshape(count * tall, -1) if joined > 1 else held[s, c]
                    sums = sums + jnp.dot(
                        left, inputs[s, :, at], preferred_element_type=jnp.float32
                    )
                sums = sums.astype(jnp.bfloat16)
                if joined > 1:
                    fin_in[:, :, at] = sums.reshape(count, tall, step)
                else:
                    fin_in[c, :, at] = sums

        for t in range(1, count):
            scatter_in_copy(t).start()
        sums = small[place]
        for t in range(1, size):
            small_copy(t).wait_recv()
            sums = sums + small_in[t]
        small_sums[0] = sums
        for t in range(1, count):
            small_share(t).start()

    def products_sum():
        sums = fin_in[here].astype(jnp.float32)
        for t in range(1, count):
            scatter_in_copy(t).wait_recv()
            sums = sums + rc_in[t].astype(jnp.float32)
        fs_in[...] = sums.astype(jnp.bfloat16)
        for t in range(1, count):
            gather_in_copy(t).start()
        total_in[here] = fs_in[...]
        sums = small_sums[0]
        for t in range(1, count):
            small_share(t).wait_recv()
            sums = sums + small_sums[t]
        small_total[...] = sums

    def relay(d, j, arrives, arrived, slot, leave):
        line[...] = term(j, d)

        @pl.when(arrives)
        def _():
            arrived(d, j).wait_recv()
            line[...] += in_sum[slot, j].astype(jnp.float32)

        own[j, d] = line[...].astype(jnp.bfloat16)
        leave(d, j).start()

    lag = 2
    items = (chips - 1) * chunks

    @pl.loop(0, items + lag * (chips - 1))
    def _(i):
        @pl.when(i < chunks)
        def _():
            own_in(i).wait()
            near_in(i).wait_recv()

        rise = i - lag * chip
        upward = chips - 1 - jnp.maximum(rise, 0) // chunks

        @pl.when((rise >= 0) & (rise < items) & (upward > chip))
        def _():
            relay(upward, rise % chunks, chip > 0, up_copy, upward + 1, up_copy)

        fall = i - lag * (chips - 1 - chip)
        downward = jnp.maximum(fall, 0) // chunks

        @pl.when((fall >= 0) & (fall < items) & (downward < chip))
        def _():
            relay(downward, fall % chunks, chip < chips - 1, down_copy, downward, down_copy)

        @pl.when(i == items // 2)
        def _():
            products()

    def reduce_chunk(j):
        sums = fin[j, here].astype(jnp.float32)
        for t in range(1, count):
            scatter_copy(j, t).wait_recv()
            sums = sums + rc[j, t].astype(jnp.float32)
        fs[j] = sums.astype(jnp.bfloat16)
        for t in range(1, count):
            gather_copy(j, t).start()
        total[j, here] = fs[j]

    @pl.loop(0, chunks)
    def _(j):
        line[...] = term(j, chip)

        @pl.when(chip > 0)
        def _():
            up_copy(chip, j).wait_recv()
            line[...] += in_sum[chip + 1, j].astype(jnp.float32)

        @pl.when(chip < chips - 1)
        def _():
            down_copy(chip, j).wait_recv()
            line[...] += in_sum[chip, j].astype(jnp.float32)

        fin[j] = line[...].astype(jnp.bfloat16)
        for t in range(1, count):
            scatter_copy(j, t).start()

        @pl.when(j >= 2)
        def _():
            reduce_chunk(j - 2)

        @pl.when(j == chunks // 2)
        def _():
            products_sum()

    @pl.loop(chunks - 2, chunks)
    def _(j):
        reduce_chunk(j)

    @pl.loop(0, chunks)
    def _(j):
        for t in range(1, count):
            gather_in(j, t).wait_recv()
            gather_copy(j, t).wait_send()
            scatter_copy(j, t).wait_send()

        near_in(j).wait_send()

        @pl.loop(0, chips)
        def _(d):
            @pl.when(d > chip)
            def _():
                up_copy(d, j).wait_send()

            @pl.when(d < chip)
            def _():
                down_copy(d, j).wait_send()

    for t in range(1, count):
        gather_in_wait(t).wait_recv()
        gather_in_copy(t).wait_send()
        scatter_in_copy(t).wait_send()
        small_share(t).wait_send()
    for t in range(1, size):
        small_copy(t).wait_send()
        factor_copy(t).wait_send()


def tail_call(ident, grads, factor, inputs, small):
    size = lax.axis_size("fsdp")
    count = lax.axis_size("ctx")
    chips = size // 2
    width = inputs.shape[2]
    rows = inputs.shape[1]
    unit = min(one.shape[1] for one in grads) // 3
    pieces = [one.shape[1] // unit for one in grads]
    chunks = sum(pieces)
    part = unit // count
    views = [
        one.reshape(chips, 2, n, count, part, width) for one, n in zip(grads, pieces)
    ]
    factor = factor.T.reshape(size, count, -1, rows)
    mine = factor.shape[2]
    bf16 = jnp.bfloat16
    anywhere = pl.BlockSpec(memory_space=pl.ANY)
    vmem = pl.BlockSpec(memory_space=pltpu.VMEM)
    dma = pltpu.SemaphoreType.DMA
    total, total_in, small_total = pl.pallas_call(
        partial(tail_kernel, chips, count, pieces),
        out_shape=[
            jax.ShapeDtypeStruct((chunks, count, part, width), bf16),
            jax.ShapeDtypeStruct((count, mine, width), bf16),
            jax.ShapeDtypeStruct(small.shape[1:], jnp.float32),
        ],
        in_specs=[anywhere] * (len(views) + 1) + [vmem] * 2,
        out_specs=[vmem] * 3,
        scratch_shapes=[
            pltpu.VMEM((chunks, chips, count, part, width), bf16),
            pltpu.VMEM((chunks, chips, count, part, width), bf16),
            pltpu.VMEM((count, part, width), jnp.float32),
            pltpu.VMEM((chips + 1, chunks, count, part, width), bf16),
            pltpu.VMEM((chunks, count, part, width), bf16),
            pltpu.VMEM((chunks, count, part, width), bf16),
            pltpu.VMEM((chunks, part, width), bf16),
            pltpu.VMEM((size, count, mine, rows), bf16),
            pltpu.VMEM((count, mine, width), bf16),
            pltpu.VMEM((count, mine, width), bf16),
            pltpu.VMEM((mine, width), bf16),
            pltpu.VMEM(small.shape, jnp.float32),
            pltpu.VMEM((count,) + small.shape[1:], jnp.float32),
            dma((chunks,)), dma((chunks,)), dma((chunks,)),
            dma((chips, chunks)), dma((chips, chunks)), dma((chips, chunks)), dma((chips, chunks)),
            dma((chunks, count)), dma((chunks, count)), dma((chunks, count)), dma((chunks, count)),
            dma, dma((size,)), dma((size,)),
            dma((count,)), dma((count,)), dma((count,)), dma((count,)),
            dma((size,)), dma((size,)), dma((count,)), dma((count,)),
        ],
        compiler_params=pltpu.CompilerParams(
            collective_id=ident, has_side_effects=True, vmem_limit_bytes=61 * 2**20
        ),
        cost_estimate=pl.CostEstimate(
            flops=2 * size * rows * width * count * mine,
            bytes_accessed=4 * size * chunks * unit * width,
            transcendentals=0,
        ),
    )(*views, factor, inputs, small)
    total = total.reshape(-1, width).astype(jnp.float32)
    outs = []
    at = 0
    for one in grads:
        outs.append(total[at : at + one.shape[1]])
        at += one.shape[1]
    return outs + [total_in.reshape(-1, width).astype(jnp.float32), small_total.reshape(-1)]


def attend_kernel(count, groups, q, kv, att, sums, kv_all, acc, send, recv):
    here = lax.axis_index("ctx")
    others = [{"ctx": lax.rem(here + t, count)} for t in range(1, count)]
    greet(others)
    key_heads = kv.shape[0] // 2
    rows = kv.shape[2]
    block = rows // 2
    scale = HEAD_SIZE ** (-0.5)

    def out_copy(t):
        return push(kv, kv_all.at[here], send.at[t], recv.at[t], others[t - 1])

    def in_copy(t):
        there = kv_all.at[lax.rem(here + count - t, count)]
        return push(there, there, send.at[t], recv.at[t], others[t - 1])

    for t in range(1, count):
        out_copy(t).start()
    kv_all[here] = kv[...]

    def weights(keys, queries, masked):
        value = jnp.exp(dims_tn(keys, queries) * scale)
        if masked:
            allowed = lax.broadcasted_iota(jnp.int32, value.shape, 1) >= lax.broadcasted_iota(
                jnp.int32, value.shape, 0
            )
            value = jnp.where(allowed, value, 0.0)
        return value

    def apply(values, part):
        return jnp.dot(values, part.astype(jnp.bfloat16), preferred_element_type=jnp.float32)

    @pl.loop(0, key_heads, unroll=2)
    def _(h):
        keys = kv[h]
        values = kv[key_heads + h]
        for g in range(groups):
            head = h * groups + g
            queries = q[head]
            part = weights(keys[:, :block], queries, True)
            acc[head] = apply(values[:, :block], part)
            sums[head] = jnp.sum(part, axis=0, keepdims=True)
            part = weights(keys[:, block:], queries[:, block:], True)
            acc[head, :, block:] += apply(values[:, block:], part)
            sums[head, :, block:] += jnp.sum(part, axis=0, keepdims=True)

    for t in range(1, count):
        there = lax.rem(here + count - t, count)
        in_copy(t).wait_recv()

        @pl.when(there < here)
        def _():
            @pl.loop(0, key_heads, unroll=2)
            def _(h):
                keys = kv_all[there, h]
                values = kv_all[there, key_heads + h]
                for g in range(groups):
                    head = h * groups + g
                    part = weights(keys[:, :block], q[head], False)
                    acc[head] += apply(values[:, :block], part)
                    sums[head] += jnp.sum(part, axis=0, keepdims=True)

        @pl.when(there > here)
        def _():
            @pl.loop(0, key_heads, unroll=2)
            def _(h):
                keys = kv_all[there, h]
                values = kv_all[there, key_heads + h]
                for g in range(groups):
                    head = h * groups + g
                    part = weights(keys, q[head][:, block:], False)
                    acc[head, :, block:] += apply(values, part)
                    sums[head, :, block:] += jnp.sum(part, axis=0, keepdims=True)

    @pl.loop(0, key_heads * groups)
    def _(head):
        att[head] = (acc[head] / sums[head]).astype(jnp.bfloat16)

    for t in range(1, count):
        out_copy(t).wait_send()


def attend_call(ident, q, kv):
    count = lax.axis_size("ctx")
    heads, size, rows = q.shape
    groups = heads // (kv.shape[0] // 2)
    vmem = pl.BlockSpec(memory_space=pltpu.VMEM)
    dma = pltpu.SemaphoreType.DMA
    return pl.pallas_call(
        partial(attend_kernel, count, groups),
        out_shape=[
            jax.ShapeDtypeStruct(q.shape, jnp.bfloat16),
            jax.ShapeDtypeStruct((heads, 1, rows), jnp.float32),
            jax.ShapeDtypeStruct((count,) + kv.shape, jnp.bfloat16),
        ],
        in_specs=[vmem] * 2,
        out_specs=[vmem] * 3,
        scratch_shapes=[pltpu.VMEM(q.shape, jnp.float32), dma((count,)), dma((count,))],
        compiler_params=pltpu.CompilerParams(
            collective_id=ident, has_side_effects=True, vmem_limit_bytes=40 * 2**20
        ),
        cost_estimate=pl.CostEstimate(
            flops=4 * heads * size * rows * rows * count,
            bytes_accessed=4 * (q.size + kv.size * count),
            transcendentals=heads * rows * rows * count,
        ),
    )(q, kv)


def attend_back_kernel(
    chips, count, groups, q, kv_all, grad, att, sums, outs, grad_q, grad_kv, result,
    delta, share, send_buf, recv_buf, own, near, out_sum, in_sum,
    send, recv, own_m, near_s, near_r, ring_s, ring_r
):
    place, chip, core, after, before, peer = places()
    here = lax.axis_index("ctx")
    others = [{"ctx": lax.rem(here + t, count)} for t in range(1, count)]
    greet([{"fsdp": before}, {"fsdp": peer}] + others)

    def near_copy(n):
        return push(
            outs.at[2 * n + 1 - core], near.at[n], near_s.at[n], near_r.at[n], {"fsdp": peer}
        )

    def own_copy(n):
        return pltpu.make_async_copy(outs.at[2 * n + core], own.at[n], own_m.at[n])

    def ring_copy(k):
        return push(out_sum.at[k], in_sum.at[k], ring_s.at[k], ring_r.at[k], {"fsdp": after})

    def term(k):
        owner = lax.rem(chip + chips - k, chips)
        own_copy(owner).wait()
        near_copy(owner).wait_recv()
        return own[owner].astype(jnp.float32) + near[owner].astype(jnp.float32)

    def hop(k):
        value = term(k)
        if k > 1:
            ring_copy(k - 2).wait_recv()
            value = value + in_sum[k - 2].astype(jnp.float32)
        out_sum[k - 1] = value.astype(jnp.bfloat16)
        ring_copy(k - 1).start()

    for n in range(chips):
        near_copy(n).start()
        own_copy(n).start()
    key_heads = kv_all.shape[1] // 2
    rows = q.shape[2]
    block = rows // 2
    scale = HEAD_SIZE ** (-0.5)
    every = slice(0, rows)
    front = slice(0, block)
    back = slice(block, rows)

    def copy(t):
        return push(send_buf.at[t], recv_buf.at[t], send.at[t], recv.at[t], others[t - 1])

    @pl.loop(0, key_heads * groups)
    def _(head):
        delta[head] = jnp.sum(
            grad[head].astype(jnp.float32) * att[head].astype(jnp.float32), axis=0, keepdims=True
        )
        share[head] = 1.0 / sums[head]
        grad_q[head] = jnp.zeros(grad_q.shape[1:], jnp.float32)

    def terms(keys, values, head, span, masked):
        queries = q[head][:, span]
        low = grad[head][:, span]
        probs = jnp.exp(dims_tn(keys, queries) * scale) * share[head][:, span]
        if masked:
            allowed = lax.broadcasted_iota(jnp.int32, probs.shape, 1) >= lax.broadcasted_iota(
                jnp.int32, probs.shape, 0
            )
            probs = jnp.where(allowed, probs, 0.0)
        grad_scores = (probs * (dims_tn(values, low) - delta[head][:, span])).astype(jnp.bfloat16)
        grad_q[head, :, span] += (
            jnp.dot(keys, grad_scores, preferred_element_type=jnp.float32) * scale
        )
        return (
            dims_nt(queries, grad_scores) * scale,
            dims_nt(low, probs.astype(jnp.bfloat16)),
        )

    def over_groups(keys, values, h, span, masked):
        grad_keys, grad_values = terms(keys, values, h * groups, span, masked)
        for g in range(1, groups):
            more_keys, more_values = terms(keys, values, h * groups + g, span, masked)
            grad_keys, grad_values = grad_keys + more_keys, grad_values + more_values
        return grad_keys, grad_values

    for t in range(1, max(count, chips)):
        if t >= count:
            hop(t)
            continue
        there = lax.rem(here + t, count)

        @pl.when(there < here)
        def _():
            @pl.loop(0, key_heads, unroll=2)
            def _(h):
                keys = kv_all[there, h][:, front]
                values = kv_all[there, key_heads + h][:, front]
                grad_keys, grad_values = over_groups(keys, values, h, every, False)
                zeros = jnp.zeros((keys.shape[0], rows - block), jnp.bfloat16)
                send_buf[t, h, :, front] = grad_keys.astype(jnp.bfloat16)
                send_buf[t, key_heads + h, :, front] = grad_values.astype(jnp.bfloat16)
                send_buf[t, h, :, back] = zeros
                send_buf[t, key_heads + h, :, back] = zeros

        @pl.when(there > here)
        def _():
            @pl.loop(0, key_heads, unroll=2)
            def _(h):
                keys = kv_all[there, h]
                values = kv_all[there, key_heads + h]
                grad_keys, grad_values = over_groups(keys, values, h, back, False)
                send_buf[t, h] = grad_keys.astype(jnp.bfloat16)
                send_buf[t, key_heads + h] = grad_values.astype(jnp.bfloat16)

        copy(t).start()
        if t < chips:
            hop(t)

    @pl.loop(0, key_heads, unroll=2)
    def _(h):
        keys = kv_all[here, h]
        values = kv_all[here, key_heads + h]
        grad_keys, grad_values = over_groups(keys[:, front], values[:, front], h, every, True)
        grad_kv[h, :, front] = grad_keys
        grad_kv[key_heads + h, :, front] = grad_values
        grad_keys, grad_values = over_groups(keys[:, back], values[:, back], h, back, True)
        grad_kv[h, :, back] = grad_keys
        grad_kv[key_heads + h, :, back] = grad_values

    for t in range(1, count):
        copy(t).wait_recv()

        @pl.loop(0, 2 * key_heads)
        def _(h):
            grad_kv[h] += recv_buf[t, h].astype(jnp.float32)

    value = term(0)
    ring_copy(chips - 2).wait_recv()
    result[...] = value + in_sum[chips - 2].astype(jnp.float32)
    for t in range(1, count):
        copy(t).wait_send()
    for n in range(chips):
        near_copy(n).wait_send()
    for k in range(chips - 1):
        ring_copy(k).wait_send()


def attend_back_call(ident, q, kv_all, grad, att, sums, outs):
    count = lax.axis_size("ctx")
    heads, size, rows = q.shape
    kv_shape = kv_all.shape[1:]
    chips = outs.shape[0] // 2
    block = outs.shape[1:]
    groups = heads // (kv_shape[0] // 2)
    vmem = pl.BlockSpec(memory_space=pltpu.VMEM)
    dma = pltpu.SemaphoreType.DMA
    return pl.pallas_call(
        partial(attend_back_kernel, chips, count, groups),
        out_shape=[
            jax.ShapeDtypeStruct(q.shape, jnp.float32),
            jax.ShapeDtypeStruct(kv_shape, jnp.float32),
            jax.ShapeDtypeStruct(block, jnp.float32),
        ],
        in_specs=[vmem] * 5 + [pl.BlockSpec(memory_space=pl.ANY)],
        out_specs=[vmem] * 3,
        scratch_shapes=[
            pltpu.VMEM(sums.shape, jnp.float32),
            pltpu.VMEM(sums.shape, jnp.float32),
            pltpu.VMEM(kv_all.shape, jnp.bfloat16),
            pltpu.VMEM(kv_all.shape, jnp.bfloat16),
            pltpu.VMEM((chips,) + block, jnp.bfloat16),
            pltpu.VMEM((chips,) + block, jnp.bfloat16),
            pltpu.VMEM((chips - 1,) + block, jnp.bfloat16),
            pltpu.VMEM((chips - 1,) + block, jnp.bfloat16),
            dma((count,)),
            dma((count,)),
            dma((chips,)),
            dma((chips,)),
            dma((chips,)),
            dma((chips,)),
            dma((chips,)),
        ],
        compiler_params=pltpu.CompilerParams(
            collective_id=ident, has_side_effects=True, vmem_limit_bytes=40 * 2**20
        ),
        cost_estimate=pl.CostEstimate(flops=1, bytes_accessed=1, transcendentals=0),
    )(q, kv_all, grad, att, sums, outs)


def local(
    hidden_in,
    cotangent,
    norm_mix,
    in_proj,
    conv_kernel,
    out_proj,
    norm_ff1,
    gate1,
    up1,
    down1,
    norm_attn,
    q_proj,
    key_projection,
    value_projection,
    q_norm,
    k_norm,
    o_proj,
    norm_ff2,
    gate2,
    up2,
    down2,
):
    narrow_dtype = jnp.bfloat16
    start = hidden_in[0].astype(jnp.float32)
    token_rows = start.shape[0]
    block = token_rows // 2
    margin = KW - 1
    ctx_count = lax.axis_size("ctx")
    ctx_place = lax.axis_index("ctx")
    is_last = ctx_place == ctx_count - 1
    query_places = dealt_places(
        ctx_place * token_rows + jnp.arange(token_rows, dtype=jnp.int32), block, ctx_count
    )
    freqs = THETA ** (-jnp.arange(HEAD_SIZE // 2, dtype=jnp.float32) * 2.0 / HEAD_SIZE)
    angles = freqs[:, None] * query_places.astype(jnp.float32)[None, :]
    vectors = (
        norm_mix, norm_ff1, norm_attn, norm_ff2, q_norm, k_norm, conv_kernel.reshape(-1)
    )
    lengths = [one.shape[0] for one in vectors]
    vector = jnp.concatenate(vectors)
    vector = jnp.pad(vector, (0, 2048 - sum(lengths))).reshape(16, 128)
    attn_shard = jnp.concatenate([q_proj, key_projection, value_projection, o_proj], axis=0)
    attn_rows = attn_shard.shape[0]
    attn_slice = pick(attn_shard.reshape(ctx_count, -1, MODEL_WIDTH), ctx_place, 0)
    attn_slices = lax.all_gather(attn_slice, "fsdp", axis=0)
    tails = jnp.concatenate(
        [
            hidden_in[0, block - margin : block],
            hidden_in[0, token_rows - margin :],
            jnp.zeros((16 - 2 * margin, MODEL_WIDTH), narrow_dtype),
        ],
        axis=0,
    )
    mix_in, mix_out, given, gathered_vectors, edges = head_call(
        4, in_proj, out_proj, cotangent[0], vector, tails
    )
    edge_rows = jnp.concatenate(
        [
            jnp.where(ctx_place == 0, 0.0, edges[1, :margin]).astype(narrow_dtype),
            jnp.where(is_last, tails[:margin], edges[-1, margin : 2 * margin]),
            tails[2 * margin :],
        ],
        axis=0,
    )
    attn_slices, mix_in = lax.optimization_barrier((attn_slices, mix_in))
    attn_wholes = lax.all_gather(attn_slices, "ctx", axis=1)
    attn_wholes = attn_wholes.reshape(-1, attn_rows, MODEL_WIDTH)
    gathered_vectors = gathered_vectors.reshape(-1, 2048)
    wholes = []
    at = 0
    for one in lengths:
        wholes.append(gathered_vectors[:, at : at + one].reshape(-1))
        at += one
    mix_norm, ff_norm_one, attn_norm, ff_norm_two, query_gain, key_gain, mix_kernel = wholes
    mix_kernel = mix_kernel.reshape(-1, KW)
    kernel = mix_kernel.astype(jnp.float32)
    gain_one = mix_norm.astype(jnp.float32)
    normed_one, norm_back_one = jax.vjp(rms_scale, start, gain_one)
    normed_one_low = normed_one.astype(narrow_dtype)
    edges_low = rms_scale(edge_rows.astype(jnp.float32), gain_one).astype(narrow_dtype)
    projected_all = dot_rows(jnp.concatenate([normed_one_low, edges_low], axis=0), mix_in)
    projected = projected_all[:token_rows]
    edge_mixed = (
        projected_all[token_rows:, :MODEL_WIDTH] * projected_all[token_rows:, 2 * MODEL_WIDTH :]
    ).astype(narrow_dtype)
    b_part = projected[:, :MODEL_WIDTH]
    c_part = projected[:, MODEL_WIDTH : 2 * MODEL_WIDTH]
    x_part = projected[:, 2 * MODEL_WIDTH :]
    mixed_low = (b_part * x_part).astype(narrow_dtype)
    before_front = edge_mixed[:margin]
    before_back = edge_mixed[margin : 2 * margin]
    front_ext = jnp.concatenate([before_front, mixed_low[:block]], axis=0).astype(jnp.float32)
    back_ext = jnp.concatenate([before_back, mixed_low[block:]], axis=0).astype(jnp.float32)
    conv_out = jnp.concatenate(
        [conv_apply(front_ext, kernel), conv_apply(back_ext, kernel)], axis=0
    )
    gated_low = (c_part * conv_out).astype(narrow_dtype)
    first = start + dot_rows(gated_low, mix_out)
    normed_two, norm_back_two = jax.vjp(rms_scale, first, ff_norm_one.astype(jnp.float32))
    ff_out_one, inputs_one = ff_call(
        "forward", 1, normed_two.astype(narrow_dtype), gate1, up1, down1
    )
    one_low, ff_out_one = lax.optimization_barrier((normed_one_low, ff_out_one))
    one_blocks = lax.all_gather(one_low, "fsdp", axis=0)
    second = first + ff_out_one
    attn_parts = []
    at = 0
    for one in (q_proj, key_projection, value_projection, o_proj):
        attn_parts.append(attn_wholes[:, at : at + one.shape[0]].reshape(-1, MODEL_WIDTH))
        at += one.shape[0]
    w_query, w_key, w_value, w_output = attn_parts
    normed_three, norm_back_three = jax.vjp(rms_scale, second, attn_norm.astype(jnp.float32))
    three_low = normed_three.astype(narrow_dtype)
    query_raw = dot_rows(w_query, three_low)
    key_raw = dot_rows(w_key, three_low)
    value_raw = dot_rows(w_value, three_low)
    query_heads, query_back = jax.vjp(
        partial(head_prep, angles=angles), query_raw, query_gain.astype(jnp.float32)
    )
    key_heads, key_back = jax.vjp(
        partial(head_prep, angles=angles), key_raw, key_gain.astype(jnp.float32)
    )
    query_narrow = query_heads.astype(narrow_dtype)
    key_value = jnp.concatenate(
        [key_heads, value_raw.reshape(key_heads.shape)], axis=0
    ).astype(narrow_dtype)
    attended_low, exp_sums, key_value_all = attend_call(6, query_narrow, key_value)
    attended_flat = attended_low.reshape(-1, token_rows)
    third = second + lax.dot_general(
        attended_flat, w_output, (((0,), (1,)), ((), ())), preferred_element_type=jnp.float32
    )
    normed_four, norm_back_four = jax.vjp(rms_scale, third, ff_norm_two.astype(jnp.float32))
    four_low, one_blocks = lax.optimization_barrier((normed_four.astype(narrow_dtype), one_blocks))
    grad_four, two_grads, outs_two = ff_call("both", 2, four_low, gate2, up2, down2, given)
    shards = lax.axis_size("fsdp")
    ff_two = lax.psum(two_grads, "ctx")
    grad_final = cotangent[0].astype(jnp.float32)
    grad_third_part, grad_ff_norm_two = norm_back_four(grad_four)
    grad_third = grad_final + grad_third_part
    output_low = grad_third.astype(narrow_dtype)
    attended_gradient = lax.dot_general(
        w_output, output_low, (((0,), (1,)), ((), ())), preferred_element_type=jnp.float32
    )
    grad_w_output = (
        lax.dot_general(
            output_low, attended_flat, (((0,), (1,)), ((), ())), preferred_element_type=jnp.float32
        )
        .astype(narrow_dtype)
        .reshape(lax.axis_size("fsdp"), -1, MODEL_WIDTH)
    )
    grad_query, grad_key_value, ff_out_two = attend_back_call(
        7,
        query_narrow,
        key_value_all,
        attended_gradient.astype(narrow_dtype).reshape(query_narrow.shape),
        attended_low,
        exp_sums,
        outs_two,
    )
    final = third + ff_out_two
    key_count = grad_key_value.shape[0] // 2
    grad_query_raw, grad_query_gain = query_back(grad_query)
    raw_key_gradient, key_gain_gradient = key_back(grad_key_value[:key_count])
    query_grad_low = grad_query_raw.astype(narrow_dtype)
    key_grad_low = raw_key_gradient.astype(narrow_dtype)
    value_grad_low = grad_key_value[key_count:].astype(narrow_dtype).reshape(key_grad_low.shape)
    grad_three = (
        dot_cols(query_grad_low, w_query)
        + dot_cols(key_grad_low, w_key)
        + dot_cols(value_grad_low, w_value)
    )
    grad_rows = [
        one.reshape(shards, -1, token_rows) for one in (query_grad_low, key_grad_low, value_grad_low)
    ]
    widths = [one.shape[1] for one in grad_rows]
    grad_rows = jnp.concatenate(grad_rows, axis=1).reshape(-1, token_rows)
    grad_w_qkv = (
        dot_plain(grad_rows, three_low).astype(narrow_dtype).reshape(shards, sum(widths), -1)
    )
    grad_second_part, grad_attn_norm = norm_back_three(grad_three)
    grad_second = grad_third + grad_second_part
    grad_two, one_grads = ff_call(
        "backward", 3, grad_second.astype(narrow_dtype), gate1, up1, down1, inputs_one
    )
    grad_two, one_grads, ff_two = lax.optimization_barrier((grad_two, one_grads, ff_two))
    ff_one = lax.psum(one_grads, "ctx")
    ff_one, ff_two = [
        [
            one[at : at + gate1.shape[0]].astype(jnp.float32)
            for at in range(0, one.shape[0], gate1.shape[0])
        ]
        for one in (ff_one, ff_two)
    ]
    grad_first_part, grad_ff_norm_one = norm_back_two(grad_two)
    grad_first = grad_second + grad_first_part
    first_low = grad_first.astype(narrow_dtype)
    grad_gated = dot_plain(first_low, mix_out)
    grad_mix_out = (
        dot_cols(first_low, gated_low).astype(narrow_dtype).reshape(shards, -1, MODEL_WIDTH)
    )
    grad_c_part = grad_gated * conv_out
    grad_conv = grad_gated * c_part
    grad_front_ext = conv_input_grad(grad_conv[:block], kernel)
    grad_back_ext = conv_input_grad(grad_conv[block:], kernel)
    back_before = grad_back_ext[:margin]
    outgoing = jnp.concatenate(
        [grad_front_ext[:margin], jnp.where(is_last, 0.0, back_before)], axis=0
    )
    returned = extended_2(outgoing, (("ctx", 0),), margin)
    from_prev = returned[:margin]
    from_next = returned[returned.shape[0] - margin :]
    own_edge = jnp.where(is_last, back_before, 0.0)
    front_grad = grad_front_ext[margin:]
    back_grad = grad_back_ext[margin:]
    front_grad = jnp.concatenate(
        [front_grad[: block - margin], front_grad[block - margin :] + from_next + own_edge], axis=0
    )
    back_grad = jnp.concatenate(
        [back_grad[: block - margin], back_grad[block - margin :] + from_prev], axis=0
    )
    grad_mixed = jnp.concatenate([front_grad, back_grad], axis=0)
    grad_kernel = kernel_grad(front_ext, grad_conv[:block]) + kernel_grad(
        back_ext, grad_conv[block:]
    )
    grad_projected = jnp.concatenate(
        [grad_mixed * x_part, grad_c_part, grad_mixed * b_part], axis=-1
    ).astype(narrow_dtype)
    grad_one = dot_plain(grad_projected, mix_in)
    grad_start_part, grad_mix_norm = norm_back_one(grad_one)
    grad_start = grad_first + grad_start_part
    smalls = (
        grad_mix_norm,
        grad_kernel.reshape(-1),
        grad_ff_norm_one,
        grad_attn_norm,
        grad_query_gain,
        key_gain_gradient,
        grad_ff_norm_two,
    )
    pieces = [one.reshape(shards, -1) for one in smalls]
    sizes = [one.shape[1] for one in pieces]
    small = jnp.concatenate(pieces + [jnp.zeros((shards, 2048 - sum(sizes)), jnp.float32)], axis=1)
    grad_w_qkv, grad_w_output, grad_mix_out, grad_mix_in, small_sum = tail_call(
        5, [grad_w_qkv, grad_w_output, grad_mix_out], grad_projected, one_blocks,
        small.reshape(shards, 16, 128),
    )
    grad_w_query = grad_w_qkv[: widths[0]]
    grad_w_key = grad_w_qkv[widths[0] : widths[0] + widths[1]]
    grad_w_value = grad_w_qkv[widths[0] + widths[1] :]
    small_out = []
    at = 0
    for one in sizes:
        small_out.append(small_sum[at : at + one])
        at += one
    return (
        final.astype(narrow_dtype)[None],
        grad_start[None],
        small_out[0],
        grad_mix_in,
        small_out[1].reshape(-1, KW),
        grad_mix_out,
        small_out[2],
        ff_one[0],
        ff_one[1],
        ff_one[2],
        small_out[3],
        grad_w_query,
        grad_w_key,
        grad_w_value,
        small_out[4],
        small_out[5],
        grad_w_output,
        small_out[6],
        ff_two[0],
        ff_two[1],
        ff_two[2],
    )


def solution(mesh):
    in_specs = (
        P("fsdp", "ctx", None),
        P("fsdp", "ctx", None),
        P("fsdp"),
        P("fsdp", None),
        P("fsdp", None),
        P("fsdp", None),
        P("fsdp"),
        P("fsdp", None),
        P("fsdp", None),
        P("fsdp", None),
        P("fsdp"),
        P("fsdp", None),
        P("fsdp", None),
        P("fsdp", None),
        P("fsdp"),
        P("fsdp"),
        P("fsdp", None),
        P("fsdp"),
        P("fsdp", None),
        P("fsdp", None),
        P("fsdp", None),
    )
    out_specs = (
        P("fsdp", "ctx", None),
        P("fsdp", "ctx", None),
        P("fsdp"),
        P("fsdp", None),
        P("fsdp", None),
        P("fsdp", None),
        P("fsdp"),
        P("fsdp", None),
        P("fsdp", None),
        P("fsdp", None),
        P("fsdp"),
        P("fsdp", None),
        P("fsdp", None),
        P("fsdp", None),
        P("fsdp"),
        P("fsdp"),
        P("fsdp", None),
        P("fsdp"),
        P("fsdp", None),
        P("fsdp", None),
        P("fsdp", None),
    )
    return jax.shard_map(local, mesh=mesh, in_specs=in_specs, out_specs=out_specs, check_vma=False)
```

```python
from functools import partial

import jax
import jax.numpy as jnp
from jax import lax
from jax.experimental import pallas as pl
from jax.experimental.pallas import tpu as pltpu
from jax.sharding import PartitionSpec as P

MODEL_WIDTH = 1536
QUERY_HEADS = 24
KEY_VALUE_HEADS = 8
HEAD_SIZE = 64
KW = 3


EPS = 1e-05
THETA = 1000000.0
NEG = -1e30


def extended_2(array, sides, width):
    for axis, dim in sides:
        size, length = (lax.axis_size(axis), array.shape[dim])
        up = [(i, (i + 1) % size) for i in range(size - 1)]
        down = [(j, i) for i, j in up]
        last = lax.slice_in_dim(array, length - width, length, axis=dim)
        first = lax.slice_in_dim(array, 0, width, axis=dim)
        before = lax.ppermute(last, axis, up)
        after = lax.ppermute(first, axis, down)
        array = jnp.concatenate([before, array, after], axis=dim)
    return array


def rms_scale(value, gain):
    return value * lax.rsqrt(jnp.mean(value * value, axis=-1, keepdims=True) + EPS) * gain


def rotate(value, angles):
    half_dim = value.shape[1] // 2
    cosine = jnp.cos(angles)
    sine = jnp.sin(angles)
    first = value[:, :half_dim]
    second = value[:, half_dim:]
    return jnp.concatenate(
        [first * cosine - second * sine, second * cosine + first * sine], axis=1
    )


def head_prep(raw, gain, angles):
    heads = raw.reshape(-1, gain.shape[0], raw.shape[1])
    mean = jnp.mean(heads * heads, axis=1, keepdims=True)
    return rotate(heads * lax.rsqrt(mean + EPS) * gain[:, None], angles)


def dot_rows(left, right):
    return lax.dot_general(
        left, right, (((1,), (1,)), ((), ())), preferred_element_type=jnp.float32
    )


def dot_cols(left, right):
    return lax.dot_general(
        left, right, (((0,), (0,)), ((), ())), preferred_element_type=jnp.float32
    )


def dot_plain(left, right):
    return jnp.dot(left, right, preferred_element_type=jnp.float32)


def swish_product(gate_val, up_val):
    return jax.nn.silu(gate_val) * up_val


def dealt_places(index, block, ctx_count):
    device = index // (2 * block)
    within = index % (2 * block)
    which = jnp.where(within < block, device, 2 * ctx_count - 1 - device)
    return which * block + within % block


def conv_apply(extended, kernel):
    sequence_length = extended.shape[0] - KW + 1
    total = extended[0:sequence_length] * kernel[:, 0]
    for place in range(1, KW):
        total = total + extended[place : place + sequence_length] * kernel[:, place]
    return total


def conv_input_grad(grad_conv, kernel):
    sequence_length = grad_conv.shape[0] + KW - 1
    padded = jnp.pad(grad_conv, ((KW - 1, KW - 1), (0, 0)))
    total = padded[KW - 1 : KW - 1 + sequence_length] * kernel[:, 0]
    for place in range(1, KW):
        total = total + padded[KW - 1 - place : KW - 1 - place + sequence_length] * kernel[:, place]
    return total


def kernel_grad(extended, grad_conv):
    sequence_length = grad_conv.shape[0]
    columns = [
        jnp.sum(grad_conv * extended[place : place + sequence_length], axis=0)
        for place in range(KW)
    ]
    return jnp.stack(columns, axis=1)


def pick(value, index, axis):
    return lax.dynamic_index_in_dim(value, index, axis, keepdims=False)


MESH = pl.DeviceIdType.MESH


def dims_nt(left, right):
    return lax.dot_general(
        left, right, (((1,), (1,)), ((), ())), preferred_element_type=jnp.float32
    )


def dims_tn(left, right):
    return lax.dot_general(
        left, right, (((0,), (0,)), ((), ())), preferred_element_type=jnp.float32
    )


def ff_call(mode, ident, x, gate, up_w, down, given=None):
    size = lax.axis_size("fsdp")
    chips = size // 2
    rows, width = x.shape
    units = gate.shape[0]
    forward = mode == "forward"
    bf16 = jnp.bfloat16
    blocks = jax.ShapeDtypeStruct((size, rows, width), bf16)
    vmem = pl.BlockSpec(memory_space=pltpu.VMEM)
    anywhere = pl.BlockSpec(memory_space=pl.ANY)
    outs = [jax.ShapeDtypeStruct((rows, width), jnp.float32)] + [blocks] * forward
    out_specs = [vmem] * len(outs)
    args = [x, gate, up_w, down]
    specs = [vmem] + [anywhere] * 3
    dma = pltpu.SemaphoreType.DMA
    scratch = [] if forward else [pltpu.VMEM(blocks.shape, bf16)]
    scratch += [pltpu.VMEM(gate.shape, bf16)] * 3 + [dma((3,))]
    scratch += [pltpu.VMEM((rows, width), jnp.float32)]
    scratch += [pltpu.VMEM((chips, rows, width), bf16)] * 3
    scratch += [pltpu.VMEM((chips + 1, rows, width), bf16)]
    scratch += [dma((chips,))] * 8 + [dma((chips, 8 if forward else 4))] * 4
    if not forward:
        outs.append(jax.ShapeDtypeStruct((3 * units, width), bf16))
        out_specs.append(anywhere)
        if mode == "both":
            outs.append(blocks)
            out_specs.append(anywhere)
        args.insert(1, given)
        specs.insert(1, anywhere)
        scratch += [pltpu.VMEM(blocks.shape, bf16)]
        scratch += [pltpu.VMEM((units, size * rows), bf16)] * 3
        scratch += [pltpu.VMEM((2, units, 256), bf16), dma((size,)), dma((2,))]
        if mode == "both":
            scratch += [pltpu.VMEM((2, rows, width), bf16), dma((2,))]
    products = 3 if forward else 9
    return pl.pallas_call(
        partial(ff_kernel, chips, mode),
        out_shape=outs,
        in_specs=specs,
        out_specs=out_specs,
        scratch_shapes=scratch,
        compiler_params=pltpu.CompilerParams(
            collective_id=ident, has_side_effects=True, vmem_limit_bytes=61 * 2**20
        ),
        cost_estimate=pl.CostEstimate(
            flops=1 if mode == "backward" else 2 * products * size * rows * units * width,
            bytes_accessed=1 if mode == "backward" else 4 * size * rows * width,
            transcendentals=0 if mode == "backward" else size * rows * units,
        ),
    )(*args)


def places():
    count = lax.axis_size("fsdp") // 2
    place = lax.axis_index("fsdp")
    chip = place // 2
    core = place % 2
    after = lax.rem(chip + 1, count) * 2 + core
    before = lax.rem(chip + count - 1, count) * 2 + core
    return place, chip, core, after, before, chip * 2 + 1 - core


def greet(targets):
    barrier = pltpu.get_barrier_semaphore()
    for target in targets:
        pl.semaphore_signal(barrier, inc=1, device_id=target, device_id_type=MESH)
    pl.semaphore_wait(barrier, len(targets))


def push(src, dst, send, recv, target):
    return pltpu.make_async_remote_copy(
        src_ref=src, dst_ref=dst, send_sem=send, recv_sem=recv,
        device_id=target, device_id_type=MESH,
    )


def ff_kernel(chips, mode, *refs):
    forward = mode == "forward"
    if forward:
        x_ref, gate, up_w, down, out, xall = refs[:6]
        rest = refs[6:]
    elif mode == "both":
        x_ref, y_hbm, gate, up_w, down, out, weight_grads, result, xall = refs[:9]
        rest = refs[9:]
    else:
        x_ref, y_hbm, gate, up_w, down, out, weight_grads, xall = refs[:8]
        rest = refs[8:]
    weights = (gate, up_w, down)
    gate, up_w, down, weight_m, part, term, other_send, other_recv, in_sum = rest[:9]
    (up_s, up_r, down_s, down_r, core_s, core_r, ps_s, ps_r, ups_s, ups_r, downs_s, downs_r) = rest[9:21]
    if not forward:
        yall, hid, dgate, dup, stage, ysem, stage_sem = rest[21:28]
        if mode == "both":
            out_stage, out_sem = rest[28:]
    rows, width = x_ref.shape
    units = gate.shape[0]
    place, chip, core, _, _, peer = places()
    low_side = chip > 0
    high_side = chip < chips - 1
    below = {"fsdp": lax.rem(place + 2 * chips - 2, 2 * chips)}
    above = {"fsdp": lax.rem(place + 2, 2 * chips)}
    pieces = ups_s.shape[1]
    piece = rows // pieces
    loads = [
        pltpu.make_async_copy(one, into, weight_m.at[n])
        for n, (one, into) in enumerate(zip(weights, (gate, up_w, down)))
    ]
    for one in loads:
        one.start()
    greet([below, above, {"fsdp": peer}])

    def up_rows(d):
        block = xall.at[2 * d + core]
        return push(block, block, up_s.at[d], up_r.at[d], above)

    def down_rows(d):
        block = xall.at[2 * d + core]
        return push(block, block, down_s.at[d], down_r.at[d], below)

    def core_copy(d):
        block = xall.at[2 * d + core]
        return push(block, block, core_s.at[d], core_r.at[d], {"fsdp": peer})

    def core_in(d):
        block = xall.at[2 * d + 1 - core]
        return push(block, block, core_s.at[d], core_r.at[d], {"fsdp": peer})

    def part_copy(d):
        return push(other_send.at[d], other_recv.at[d], ps_s.at[d], ps_r.at[d], {"fsdp": peer})

    def span(b):
        return pl.ds(pl.multiple_of(b * piece, piece), piece)

    def up_sum(d, b):
        return push(
            term.at[d, span(b)], in_sum.at[d + 1, span(b)], ups_s.at[d, b], ups_r.at[d, b], above
        )

    def down_sum(d, b):
        return push(
            term.at[d, span(b)], in_sum.at[d, span(b)], downs_s.at[d, b], downs_r.at[d, b], below
        )

    def y_copy(s):
        return pltpu.make_async_copy(y_hbm.at[s], yall.at[s], ysem.at[s])

    def across(s):
        return pl.ds(pl.multiple_of(s * rows, rows), rows)

    def block(s):
        x = xall[s]
        if forward:
            gate_val = dims_nt(gate[...], x)
            up_val = dims_nt(up_w[...], x)
            hidden = (gate_val / (1.0 + jnp.exp(-gate_val)) * up_val).astype(jnp.bfloat16)
            return dims_tn(hidden, down[...])
        y_copy(s).wait()
        y = yall[s]
        a, g = (x, y) if mode == "both" else (y, x)
        gate_val = dims_nt(gate[...], a)
        up_val = dims_nt(up_w[...], a)
        grad_hidden = dims_nt(down[...], g)
        sig = 1.0 / (1.0 + jnp.exp(-gate_val))
        act = gate_val * sig
        grad_up = (grad_hidden * act).astype(jnp.bfloat16)
        grad_gate = (
            grad_hidden * up_val * (sig * (1.0 + gate_val * (1.0 - sig)))
        ).astype(jnp.bfloat16)
        hid[:, across(s)] = (act * up_val).astype(jnp.bfloat16)
        dup[:, across(s)] = grad_up
        dgate[:, across(s)] = grad_gate
        return dims_tn(grad_gate, gate[...]) + dims_tn(grad_up, up_w[...])

    xall[place] = x_ref[...]
    if not forward:
        @pl.loop(0, 2 * chips)
        def _(s):
            y_copy(s).start()

    @pl.when(high_side)
    def _():
        up_rows(chip).start()

    @pl.when(low_side)
    def _():
        down_rows(chip).start()

    inside = low_side & high_side
    reach = jnp.minimum(chip, chips - 1 - chip)

    def turn(r):
        far = jnp.where(r <= 2 * reach, (r + 1) // 2, r - reach)
        downward = jnp.where(r <= 2 * reach, r % 2 == 1, chip > chips - 1 - chip)
        return jnp.where(downward, chip - far, chip + far)

    def receive(r):
        d = turn(r)

        @pl.when(d < chip)
        def _():
            up_rows(d).wait_recv()

            @pl.when(high_side)
            def _():
                up_rows(d).start()

        @pl.when(d > chip)
        def _():
            down_rows(d).wait_recv()

            @pl.when(low_side)
            def _():
                down_rows(d).start()

        core_copy(d).start()

    core_copy(chip).start()

    @pl.loop(0, chips)
    def _(r):
        @pl.when((r == 1) | ((r > 1) & ~inside))
        def _():
            receive(r)

        @pl.when((r >= 1) & (r < chips - 1) & inside)
        def _():
            receive(r + 1)

        d = turn(r)

        @pl.when(r == 0)
        def _():
            for one in loads:
                one.wait()

        @pl.loop(0, 2)
        def _(o):
            @pl.when(o == 1)
            def _():
                core_in(d).wait_recv()

            value = block(2 * d + (core + o) % 2)

            @pl.when(o == 0)
            def _():
                part[...] = value

            @pl.when(o == 1)
            def _():
                other_send[d] = value.astype(jnp.bfloat16)
                part_copy(d).start()

        part_copy(d).wait_recv()

        @pl.when(d == chip)
        def _():
            out[...] = part[...] + other_recv[d].astype(jnp.float32)

        @pl.when(d != chip)
        def _():
            term[d] = (part[...] + other_recv[d].astype(jnp.float32)).astype(jnp.bfloat16)

        @pl.when((d > chip) & (chip == 0))
        def _():
            for b in range(pieces):
                up_sum(d, b).start()

        @pl.when((d < chip) & (chip == chips - 1))
        def _():
            for b in range(pieces):
                down_sum(d, b).start()

    lag = 2
    items = (chips - 2) * pieces
    relays = items + lag * max(chips - 3, 0)

    def relay(n):
        rise = n - lag * (chip - 1)
        fall = n - lag * (chips - 2 - chip)
        high = jnp.maximum(rise, 0) // pieces + 2
        low = chips - 3 - jnp.maximum(fall, 0) // pieces

        @pl.when((rise >= 0) & (rise < items) & (high > chip) & low_side)
        def _():
            b = rise % pieces
            up_sum(high, b).wait_recv()
            term[high, span(b)] = (
                term[high, span(b)].astype(jnp.float32)
                + in_sum[high + 1, span(b)].astype(jnp.float32)
            ).astype(jnp.bfloat16)
            up_sum(high, b).start()

        @pl.when((fall >= 0) & (fall < items) & (low < chip) & high_side)
        def _():
            b = fall % pieces
            down_sum(low, b).wait_recv()
            term[low, span(b)] = (
                term[low, span(b)].astype(jnp.float32) + in_sum[low, span(b)].astype(jnp.float32)
            ).astype(jnp.bfloat16)
            down_sum(low, b).start()

    if forward:
        @pl.loop(0, relays)
        def _(n):
            relay(n)
    else:
        step = stage.shape[2]
        steps = width // step
        gate_right, hid_right = (xall, yall) if mode == "both" else (yall, xall)
        pairs = ((dgate, gate_right), (dup, gate_right), (hid, hid_right))

        def stage_copy(n, j):
            there = weight_grads.at[
                pl.ds(n * units, units), pl.ds(pl.multiple_of(j * step, step), step)
            ]
            return pltpu.make_async_copy(stage.at[j % 2], there, stage_sem.at[j % 2])

        @pl.loop(0, max(2 * relays, 3 * steps))
        def _(m):
            @pl.when((m % 2 == 0) & (m < 2 * relays))
            def _():
                relay(m // 2)

            j = m % steps
            for n, (left, right) in enumerate(pairs):
                @pl.when(m // steps == n)
                def _():
                    @pl.when(m >= 2)
                    def _():
                        stage_copy(n, j).wait()

                    at = pl.ds(pl.multiple_of(j * step, step), step)
                    sums = jnp.dot(
                        left[...],
                        right[:, :, at].reshape(2 * chips * rows, step),
                        preferred_element_type=jnp.float32,
                    )
                    stage[j % 2] = sums.astype(jnp.bfloat16)
                    stage_copy(n, j).start()

        for j in range(2):
            stage_copy(2, j).wait()
        if mode == "both":
            def result_copy(s):
                return pltpu.make_async_copy(out_stage.at[s % 2], result.at[s], out_sem.at[s % 2])

            @pl.loop(0, 2 * chips)
            def _(s):
                @pl.when(s >= 2)
                def _():
                    result_copy(s).wait()

                out_stage[s % 2] = dims_tn(hid[:, across(s)], down[...]).astype(jnp.bfloat16)
                result_copy(s).start()

            for s in range(2):
                result_copy(s).wait()

    @pl.when(low_side)
    def _():
        for b in range(pieces):
            up_sum(chip, b).wait_recv()
        out[...] += in_sum[chip + 1].astype(jnp.float32)

    @pl.when(high_side)
    def _():
        for b in range(pieces):
            down_sum(chip, b).wait_recv()
        out[...] += in_sum[chip].astype(jnp.float32)

    @pl.loop(0, chips)
    def _(d):
        core_copy(d).wait_send()
        part_copy(d).wait_send()

        @pl.when((d <= chip) & high_side)
        def _():
            up_rows(d).wait_send()

        @pl.when((d >= chip) & low_side)
        def _():
            down_rows(d).wait_send()

        @pl.when(d > chip)
        def _():
            for b in range(pieces):
                up_sum(d, b).wait_send()

        @pl.when(d < chip)
        def _():
            for b in range(pieces):
                down_sum(d, b).wait_send()


def head_kernel(chips, count, *refs):
    shards = refs[:2]
    block, vector, edge = refs[2:5]
    wholes = refs[5:7]
    blocks, vectors, edges = refs[7:10]
    local, near_s, near_r, hop_s, hop_r, side_s, side_r, pass_s, pass_r, edge_s, edge_r = refs[10:]
    place, chip, core, after, before, peer = places()
    here = lax.axis_index("ctx")
    others = [{"ctx": lax.rem(here + t, count)} for t in range(1, count)]
    greet([{"fsdp": before}, {"fsdp": peer}] + others)
    started = []

    def go(copy):
        copy.start()
        started.append(copy)

    def shard_of(k):
        return lax.rem(chip + chips - k, chips) * 2 + core

    def hop(k, n):
        owner = shard_of(k)
        if n < 2:
            src = shards[n].at[here] if k == 0 else wholes[n].at[owner, here]
            dst = wholes[n].at[owner, here]
        elif n == 2:
            src = block if k == 0 else blocks.at[owner]
            dst = blocks.at[owner]
        else:
            src = vector if k == 0 else vectors.at[owner]
            dst = vectors.at[owner]
        return push(src, dst, hop_s.at[n, k], hop_r.at[n, k], {"fsdp": after})

    def side(k, t, n):
        piece = wholes[n].at[shard_of(k), here]
        return push(piece, piece, side_s.at[n, k, t], side_r.at[n, k, t], others[t - 1])

    def side_in(k, t, n):
        piece = wholes[n].at[shard_of(k), lax.rem(here + count - t, count)]
        return piece, push(piece, piece, side_s.at[n, k, t], side_r.at[n, k, t], others[t - 1])

    def across(k, t, n):
        if n == 2:
            src = dst = blocks.at[shard_of(k)]
        elif n == 3:
            src = dst = vectors.at[shard_of(k)]
        else:
            src = dst = wholes[n].at[shard_of(k), lax.rem(here + count - t, count)]
        return push(src, dst, pass_s.at[n, k, t], pass_r.at[n, k, t], {"fsdp": peer})

    def across_in(k, t, n):
        owner = lax.rem(chip + chips - k, chips) * 2 + 1 - core
        if n == 2:
            dst = blocks.at[owner]
        elif n == 3:
            dst = vectors.at[owner]
        else:
            dst = wholes[n].at[owner, lax.rem(here + count - t, count)]
        return push(dst, dst, pass_s.at[n, k, t], pass_r.at[n, k, t], {"fsdp": peer})

    homes = [one.at[place] for one in (*wholes, blocks, vectors)]
    came = [one.at[peer] for one in (*wholes, blocks, vectors)]
    sources = [shards[0], shards[1], block, vector]
    order = (3, 0, 1, 2)

    def edge_copy(t):
        return push(edge, edges.at[t], edge_s.at[t], edge_r.at[t], others[t - 1])

    for t in range(1, count):
        go(edge_copy(t))
    first = pltpu.make_async_copy(edge, edges.at[0], edge_s.at[0])
    first.start()
    for n in order:
        go(hop(0, n))
    keeps = [pltpu.make_async_copy(sources[n], homes[n], local.at[n]) for n in order]
    for one in keeps:
        one.start()
    for n in order:
        go(push(sources[n], homes[n], near_s.at[n], near_r.at[n], {"fsdp": peer}))
    for k in range(1, chips):
        for n in order:
            hop(k - 1, n).wait_recv()
            if k < chips - 1:
                go(hop(k, n))
            if n < 2:
                for t in range(1, count):
                    go(side(k, t, n))
            go(across(k, 0, n))
        if k > 1:
            for n in range(2):
                for t in range(1, count):
                    side_in(k - 1, t, n)[1].wait_recv()
                    go(across(k - 1, t, n))
    for n in range(2):
        for t in range(1, count):
            side_in(chips - 1, t, n)[1].wait_recv()
            go(across(chips - 1, t, n))
    for n in order:
        push(came[n], came[n], near_s.at[n], near_r.at[n], {"fsdp": peer}).wait_recv()
        for k in range(1, chips):
            for t in range(count if n < 2 else 1):
                across_in(k, t, n).wait_recv()
    for t in range(1, count):
        edge_copy(t).wait_recv()
    first.wait()
    for one in keeps:
        one.wait()
    for one in started:
        one.wait_send()


def head_call(ident, shard_a, shard_b, block, vector, edge):
    size = lax.axis_size("fsdp")
    count = lax.axis_size("ctx")
    chips = size // 2
    width = shard_a.shape[1]
    shards = [one.reshape(count, -1, width) for one in (shard_a, shard_b)]
    outs = [jax.ShapeDtypeStruct((size,) + one.shape, jnp.bfloat16) for one in shards]
    outs.append(jax.ShapeDtypeStruct((size,) + block.shape, jnp.bfloat16))
    outs.append(jax.ShapeDtypeStruct((size,) + vector.shape, jnp.bfloat16))
    outs.append(jax.ShapeDtypeStruct((count,) + edge.shape, jnp.bfloat16))
    anywhere = pl.BlockSpec(memory_space=pl.ANY)
    dma = pltpu.SemaphoreType.DMA
    whole_a, whole_b, blocks, vectors, edges = pl.pallas_call(
        partial(head_kernel, chips, count),
        out_shape=outs,
        in_specs=[anywhere] * 5,
        out_specs=[anywhere] * 5,
        scratch_shapes=[
            dma((4,)), dma((4,)), dma((4,)),
            dma((4, chips)), dma((4, chips)),
            dma((2, chips, count)), dma((2, chips, count)),
            dma((4, chips, count)), dma((4, chips, count)),
            dma((count,)), dma((count,)),
        ],
        compiler_params=pltpu.CompilerParams(collective_id=ident, has_side_effects=True),
        cost_estimate=pl.CostEstimate(
            flops=0, bytes_accessed=2 * size * (shard_a.size + shard_b.size) * 2, transcendentals=0
        ),
    )(*shards, block, vector, edge)
    return whole_a.reshape(-1, width), whole_b.reshape(-1, width), blocks, vectors, edges


def tail_kernel(chips, count, pieces, *refs):
    number = len(pieces)
    grads = refs[:number]
    factor, inputs, small = refs[number : number + 3]
    total, total_in, small_total = refs[number + 3 : number + 6]
    rest = refs[number + 6 :]
    own, near, line, in_sum, fin, rc, fs, held, fin_in, rc_in, fs_in, small_in, small_sums = rest[:13]
    (own_m, near_s, near_r, up_s, up_r, down_s, down_r, sc_s, sc_r, ag_s, ag_r, fac_m, fac_s, fac_r,
     sci_s, sci_r, agi_s, agi_r, sm_s, sm_r, smc_s, smc_r) = rest[13:]
    place, chip, core, after, before, peer = places()
    here = lax.axis_index("ctx")
    size = 2 * chips
    chunks = sum(pieces)
    ctx_others = [{"ctx": lax.rem(here + t, count)} for t in range(1, count)]
    shard_others = [{"fsdp": lax.rem(place + t, size)} for t in range(1, size)]
    greet(ctx_others + shard_others)

    def factor_copy(t):
        there = lax.rem(place + t, size)
        return push(factor.at[there], held.at[place], fac_s.at[t], fac_r.at[t], {"fsdp": there})

    def small_copy(t):
        there = lax.rem(place + t, size)
        return push(small.at[there], small_in.at[t], sm_s.at[t], sm_r.at[t], {"fsdp": there})

    def small_share(t):
        return push(
            small_sums.at[0], small_sums.at[t], smc_s.at[t], smc_r.at[t], ctx_others[t - 1]
        )

    for t in range(1, size):
        small_copy(t).start()
        factor_copy(t).start()
    keep = pltpu.make_async_copy(factor.at[place], held.at[place], fac_m)
    keep.start()

    bases = [sum(pieces[:n]) for n in range(number)]

    def near_copy(n, j):
        at = bases[n] + j
        return push(
            grads[n].at[:, 1 - core, j], near.at[at], near_s.at[at], near_r.at[at], {"fsdp": peer}
        )

    def own_copy(n, j):
        at = bases[n] + j
        return pltpu.make_async_copy(grads[n].at[:, core, j], own.at[at], own_m.at[at])

    for n in range(number):
        @pl.loop(0, pieces[n])
        def _(j):
            near_copy(n, j).start()
            own_copy(n, j).start()

    def up_copy(d, j):
        there = {"fsdp": lax.rem(place + 2, size)}
        return push(own.at[j, d], in_sum.at[d + 1, j], up_s.at[d, j], up_r.at[d, j], there)

    def down_copy(d, j):
        there = {"fsdp": lax.rem(place + size - 2, size)}
        return push(own.at[j, d], in_sum.at[d, j], down_s.at[d, j], down_r.at[d, j], there)

    def near_in(j):
        return push(near.at[j], near.at[j], near_s.at[j], near_r.at[j], {"fsdp": peer})

    def own_in(j):
        return pltpu.make_async_copy(own.at[j], own.at[j], own_m.at[j])

    def term(j, owner):
        return own[j, owner].astype(jnp.float32) + near[j, owner].astype(jnp.float32)

    def scatter_copy(j, t):
        there = lax.rem(here + t, count)
        return push(fin.at[j, there], rc.at[j, t], sc_s.at[j, t], sc_r.at[j, t], {"ctx": there})

    def gather_copy(j, t):
        return push(
            fs.at[j], total.at[j, here], ag_s.at[j, t], ag_r.at[j, t], ctx_others[t - 1]
        )

    def gather_in(j, t):
        there = total.at[j, lax.rem(here + count - t, count)]
        return push(there, there, ag_s.at[j, t], ag_r.at[j, t], ctx_others[t - 1])

    def scatter_in_copy(t):
        there = lax.rem(here + t, count)
        return push(fin_in.at[there], rc_in.at[t], sci_s.at[t], sci_r.at[t], {"ctx": there})

    def gather_in_copy(t):
        return push(fs_in, total_in.at[here], agi_s.at[t], agi_r.at[t], ctx_others[t - 1])

    def gather_in_wait(t):
        there = total_in.at[lax.rem(here + count - t, count)]
        return push(there, there, agi_s.at[t], agi_r.at[t], ctx_others[t - 1])

    def products():
        for t in range(1, size):
            src = held.at[lax.rem(place + size - t, size)]
            push(src, src, fac_s.at[t], fac_r.at[t], {"fsdp": peer}).wait_recv()
        keep.wait()

        tall = held.shape[2]
        joined = 1 if tall % 16 else count
        step = 256

        @pl.loop(0, count // joined)
        def _(c):
            @pl.loop(0, inputs.shape[2] // step)
            def _(n):
                at = pl.ds(pl.multiple_of(n * step, step), step)
                sums = 0.0
                for s in range(size):
                    left = held[s].reshape(count * tall, -1) if joined > 1 else held[s, c]
                    sums = sums + jnp.dot(
                        left, inputs[s, :, at], preferred_element_type=jnp.float32
                    )
                sums = sums.astype(jnp.bfloat16)
                if joined > 1:
                    fin_in[:, :, at] = sums.reshape(count, tall, step)
                else:
                    fin_in[c, :, at] = sums

        for t in range(1, count):
            scatter_in_copy(t).start()
        sums = small[place]
        for t in range(1, size):
            small_copy(t).wait_recv()
            sums = sums + small_in[t]
        small_sums[0] = sums
        for t in range(1, count):
            small_share(t).start()

    def products_sum():
        sums = fin_in[here].astype(jnp.float32)
        for t in range(1, count):
            scatter_in_copy(t).wait_recv()
            sums = sums + rc_in[t].astype(jnp.float32)
        fs_in[...] = sums.astype(jnp.bfloat16)
        for t in range(1, count):
            gather_in_copy(t).start()
        total_in[here] = fs_in[...]
        sums = small_sums[0]
        for t in range(1, count):
            small_share(t).wait_recv()
            sums = sums + small_sums[t]
        small_total[...] = sums

    def relay(d, j, arrives, arrived, slot, leave):
        line[...] = term(j, d)

        @pl.when(arrives)
        def _():
            arrived(d, j).wait_recv()
            line[...] += in_sum[slot, j].astype(jnp.float32)

        own[j, d] = line[...].astype(jnp.bfloat16)
        leave(d, j).start()

    lag = 2
    items = (chips - 1) * chunks

    @pl.loop(0, items + lag * (chips - 1))
    def _(i):
        @pl.when(i < chunks)
        def _():
            own_in(i).wait()
            near_in(i).wait_recv()

        rise = i - lag * chip
        upward = chips - 1 - jnp.maximum(rise, 0) // chunks

        @pl.when((rise >= 0) & (rise < items) & (upward > chip))
        def _():
            relay(upward, rise % chunks, chip > 0, up_copy, upward + 1, up_copy)

        fall = i - lag * (chips - 1 - chip)
        downward = jnp.maximum(fall, 0) // chunks

        @pl.when((fall >= 0) & (fall < items) & (downward < chip))
        def _():
            relay(downward, fall % chunks, chip < chips - 1, down_copy, downward, down_copy)

        @pl.when(i == items // 2)
        def _():
            products()

    def reduce_chunk(j):
        sums = fin[j, here].astype(jnp.float32)
        for t in range(1, count):
            scatter_copy(j, t).wait_recv()
            sums = sums + rc[j, t].astype(jnp.float32)
        fs[j] = sums.astype(jnp.bfloat16)
        for t in range(1, count):
            gather_copy(j, t).start()
        total[j, here] = fs[j]

    @pl.loop(0, chunks)
    def _(j):
        line[...] = term(j, chip)

        @pl.when(chip > 0)
        def _():
            up_copy(chip, j).wait_recv()
            line[...] += in_sum[chip + 1, j].astype(jnp.float32)

        @pl.when(chip < chips - 1)
        def _():
            down_copy(chip, j).wait_recv()
            line[...] += in_sum[chip, j].astype(jnp.float32)

        fin[j] = line[...].astype(jnp.bfloat16)
        for t in range(1, count):
            scatter_copy(j, t).start()

        @pl.when(j >= 2)
        def _():
            reduce_chunk(j - 2)

        @pl.when(j == chunks // 2)
        def _():
            products_sum()

    @pl.loop(chunks - 2, chunks)
    def _(j):
        reduce_chunk(j)

    @pl.loop(0, chunks)
    def _(j):
        for t in range(1, count):
            gather_in(j, t).wait_recv()
            gather_copy(j, t).wait_send()
            scatter_copy(j, t).wait_send()

        near_in(j).wait_send()

        @pl.loop(0, chips)
        def _(d):
            @pl.when(d > chip)
            def _():
                up_copy(d, j).wait_send()

            @pl.when(d < chip)
            def _():
                down_copy(d, j).wait_send()

    for t in range(1, count):
        gather_in_wait(t).wait_recv()
        gather_in_copy(t).wait_send()
        scatter_in_copy(t).wait_send()
        small_share(t).wait_send()
    for t in range(1, size):
        small_copy(t).wait_send()
        factor_copy(t).wait_send()


def tail_call(ident, grads, factor, inputs, small):
    size = lax.axis_size("fsdp")
    count = lax.axis_size("ctx")
    chips = size // 2
    width = inputs.shape[2]
    rows = inputs.shape[1]
    unit = min(one.shape[1] for one in grads) // 3
    pieces = [one.shape[1] // unit for one in grads]
    chunks = sum(pieces)
    part = unit // count
    views = [
        one.reshape(chips, 2, n, count, part, width) for one, n in zip(grads, pieces)
    ]
    factor = factor.T.reshape(size, count, -1, rows)
    mine = factor.shape[2]
    bf16 = jnp.bfloat16
    anywhere = pl.BlockSpec(memory_space=pl.ANY)
    vmem = pl.BlockSpec(memory_space=pltpu.VMEM)
    dma = pltpu.SemaphoreType.DMA
    total, total_in, small_total = pl.pallas_call(
        partial(tail_kernel, chips, count, pieces),
        out_shape=[
            jax.ShapeDtypeStruct((chunks, count, part, width), bf16),
            jax.ShapeDtypeStruct((count, mine, width), bf16),
            jax.ShapeDtypeStruct(small.shape[1:], jnp.float32),
        ],
        in_specs=[anywhere] * (len(views) + 1) + [vmem] * 2,
        out_specs=[vmem] * 3,
        scratch_shapes=[
            pltpu.VMEM((chunks, chips, count, part, width), bf16),
            pltpu.VMEM((chunks, chips, count, part, width), bf16),
            pltpu.VMEM((count, part, width), jnp.float32),
            pltpu.VMEM((chips + 1, chunks, count, part, width), bf16),
            pltpu.VMEM((chunks, count, part, width), bf16),
            pltpu.VMEM((chunks, count, part, width), bf16),
            pltpu.VMEM((chunks, part, width), bf16),
            pltpu.VMEM((size, count, mine, rows), bf16),
            pltpu.VMEM((count, mine, width), bf16),
            pltpu.VMEM((count, mine, width), bf16),
            pltpu.VMEM((mine, width), bf16),
            pltpu.VMEM(small.shape, jnp.float32),
            pltpu.VMEM((count,) + small.shape[1:], jnp.float32),
            dma((chunks,)), dma((chunks,)), dma((chunks,)),
            dma((chips, chunks)), dma((chips, chunks)), dma((chips, chunks)), dma((chips, chunks)),
            dma((chunks, count)), dma((chunks, count)), dma((chunks, count)), dma((chunks, count)),
            dma, dma((size,)), dma((size,)),
            dma((count,)), dma((count,)), dma((count,)), dma((count,)),
            dma((size,)), dma((size,)), dma((count,)), dma((count,)),
        ],
        compiler_params=pltpu.CompilerParams(
            collective_id=ident, has_side_effects=True, vmem_limit_bytes=61 * 2**20
        ),
        cost_estimate=pl.CostEstimate(
            flops=2 * size * rows * width * count * mine,
            bytes_accessed=4 * size * chunks * unit * width,
            transcendentals=0,
        ),
    )(*views, factor, inputs, small)
    total = total.reshape(-1, width).astype(jnp.float32)
    outs = []
    at = 0
    for one in grads:
        outs.append(total[at : at + one.shape[1]])
        at += one.shape[1]
    return outs + [total_in.reshape(-1, width).astype(jnp.float32), small_total.reshape(-1)]


def attend_kernel(count, groups, q, kv, att, sums, kv_all, acc, send, recv):
    here = lax.axis_index("ctx")
    others = [{"ctx": lax.rem(here + t, count)} for t in range(1, count)]
    greet(others)
    key_heads = kv.shape[0] // 2
    rows = kv.shape[2]
    block = rows // 2
    scale = HEAD_SIZE ** (-0.5)

    def out_copy(t):
        return push(kv, kv_all.at[here], send.at[t], recv.at[t], others[t - 1])

    def in_copy(t):
        there = kv_all.at[lax.rem(here + count - t, count)]
        return push(there, there, send.at[t], recv.at[t], others[t - 1])

    for t in range(1, count):
        out_copy(t).start()
    kv_all[here] = kv[...]

    def weights(keys, queries, masked):
        value = jnp.exp(dims_tn(keys, queries) * scale)
        if masked:
            allowed = lax.broadcasted_iota(jnp.int32, value.shape, 1) >= lax.broadcasted_iota(
                jnp.int32, value.shape, 0
            )
            value = jnp.where(allowed, value, 0.0)
        return value

    def apply(values, part):
        return jnp.dot(values, part.astype(jnp.bfloat16), preferred_element_type=jnp.float32)

    @pl.loop(0, key_heads, unroll=2)
    def _(h):
        keys = kv[h]
        values = kv[key_heads + h]
        for g in range(groups):
            head = h * groups + g
            queries = q[head]
            part = weights(keys[:, :block], queries, True)
            acc[head] = apply(values[:, :block], part)
            sums[head] = jnp.sum(part, axis=0, keepdims=True)
            part = weights(keys[:, block:], queries[:, block:], True)
            acc[head, :, block:] += apply(values[:, block:], part)
            sums[head, :, block:] += jnp.sum(part, axis=0, keepdims=True)

    for t in range(1, count):
        there = lax.rem(here + count - t, count)
        in_copy(t).wait_recv()

        @pl.when(there < here)
        def _():
            @pl.loop(0, key_heads, unroll=2)
            def _(h):
                keys = kv_all[there, h]
                values = kv_all[there, key_heads + h]
                for g in range(groups):
                    head = h * groups + g
                    part = weights(keys[:, :block], q[head], False)
                    acc[head] += apply(values[:, :block], part)
                    sums[head] += jnp.sum(part, axis=0, keepdims=True)

        @pl.when(there > here)
        def _():
            @pl.loop(0, key_heads, unroll=2)
            def _(h):
                keys = kv_all[there, h]
                values = kv_all[there, key_heads + h]
                for g in range(groups):
                    head = h * groups + g
                    part = weights(keys, q[head][:, block:], False)
                    acc[head, :, block:] += apply(values, part)
                    sums[head, :, block:] += jnp.sum(part, axis=0, keepdims=True)

    @pl.loop(0, key_heads * groups)
    def _(head):
        att[head] = (acc[head] / sums[head]).astype(jnp.bfloat16)

    for t in range(1, count):
        out_copy(t).wait_send()


def attend_call(ident, q, kv):
    count = lax.axis_size("ctx")
    heads, size, rows = q.shape
    groups = heads // (kv.shape[0] // 2)
    vmem = pl.BlockSpec(memory_space=pltpu.VMEM)
    dma = pltpu.SemaphoreType.DMA
    return pl.pallas_call(
        partial(attend_kernel, count, groups),
        out_shape=[
            jax.ShapeDtypeStruct(q.shape, jnp.bfloat16),
            jax.ShapeDtypeStruct((heads, 1, rows), jnp.float32),
            jax.ShapeDtypeStruct((count,) + kv.shape, jnp.bfloat16),
        ],
        in_specs=[vmem] * 2,
        out_specs=[vmem] * 3,
        scratch_shapes=[pltpu.VMEM(q.shape, jnp.float32), dma((count,)), dma((count,))],
        compiler_params=pltpu.CompilerParams(
            collective_id=ident, has_side_effects=True, vmem_limit_bytes=40 * 2**20
        ),
        cost_estimate=pl.CostEstimate(
            flops=4 * heads * size * rows * rows * count,
            bytes_accessed=4 * (q.size + kv.size * count),
            transcendentals=heads * rows * rows * count,
        ),
    )(q, kv)


def attend_back_kernel(
    chips, count, groups, q, kv_all, grad, att, sums, outs, grad_q, grad_kv, result,
    delta, share, send_buf, recv_buf, own, near, out_sum, in_sum,
    send, recv, own_m, near_s, near_r, ring_s, ring_r
):
    place, chip, core, after, before, peer = places()
    here = lax.axis_index("ctx")
    others = [{"ctx": lax.rem(here + t, count)} for t in range(1, count)]
    greet([{"fsdp": before}, {"fsdp": peer}] + others)

    def near_copy(n):
        return push(
            outs.at[2 * n + 1 - core], near.at[n], near_s.at[n], near_r.at[n], {"fsdp": peer}
        )

    def own_copy(n):
        return pltpu.make_async_copy(outs.at[2 * n + core], own.at[n], own_m.at[n])

    def ring_copy(k):
        return push(out_sum.at[k], in_sum.at[k], ring_s.at[k], ring_r.at[k], {"fsdp": after})

    def term(k):
        owner = lax.rem(chip + chips - k, chips)
        own_copy(owner).wait()
        near_copy(owner).wait_recv()
        return own[owner].astype(jnp.float32) + near[owner].astype(jnp.float32)

    def hop(k):
        value = term(k)
        if k > 1:
            ring_copy(k - 2).wait_recv()
            value = value + in_sum[k - 2].astype(jnp.float32)
        out_sum[k - 1] = value.astype(jnp.bfloat16)
        ring_copy(k - 1).start()

    for n in range(chips):
        near_copy(n).start()
        own_copy(n).start()
    key_heads = kv_all.shape[1] // 2
    rows = q.shape[2]
    block = rows // 2
    scale = HEAD_SIZE ** (-0.5)
    every = slice(0, rows)
    front = slice(0, block)
    back = slice(block, rows)

    def copy(t):
        return push(send_buf.at[t], recv_buf.at[t], send.at[t], recv.at[t], others[t - 1])

    @pl.loop(0, key_heads * groups)
    def _(head):
        delta[head] = jnp.sum(
            grad[head].astype(jnp.float32) * att[head].astype(jnp.float32), axis=0, keepdims=True
        )
        share[head] = 1.0 / sums[head]
        grad_q[head] = jnp.zeros(grad_q.shape[1:], jnp.float32)

    def terms(keys, values, head, span, masked):
        queries = q[head][:, span]
        low = grad[head][:, span]
        probs = jnp.exp(dims_tn(keys, queries) * scale) * share[head][:, span]
        if masked:
            allowed = lax.broadcasted_iota(jnp.int32, probs.shape, 1) >= lax.broadcasted_iota(
                jnp.int32, probs.shape, 0
            )
            probs = jnp.where(allowed, probs, 0.0)
        grad_scores = (probs * (dims_tn(values, low) - delta[head][:, span])).astype(jnp.bfloat16)
        grad_q[head, :, span] += (
            jnp.dot(keys, grad_scores, preferred_element_type=jnp.float32) * scale
        )
        return (
            dims_nt(queries, grad_scores) * scale,
            dims_nt(low, probs.astype(jnp.bfloat16)),
        )

    def over_groups(keys, values, h, span, masked):
        grad_keys, grad_values = terms(keys, values, h * groups, span, masked)
        for g in range(1, groups):
            more_keys, more_values = terms(keys, values, h * groups + g, span, masked)
            grad_keys, grad_values = grad_keys + more_keys, grad_values + more_values
        return grad_keys, grad_values

    for t in range(1, max(count, chips)):
        if t >= count:
            hop(t)
            continue
        there = lax.rem(here + t, count)

        @pl.when(there < here)
        def _():
            @pl.loop(0, key_heads, unroll=2)
            def _(h):
                keys = kv_all[there, h][:, front]
                values = kv_all[there, key_heads + h][:, front]
                grad_keys, grad_values = over_groups(keys, values, h, every, False)
                zeros = jnp.zeros((keys.shape[0], rows - block), jnp.bfloat16)
                send_buf[t, h, :, front] = grad_keys.astype(jnp.bfloat16)
                send_buf[t, key_heads + h, :, front] = grad_values.astype(jnp.bfloat16)
                send_buf[t, h, :, back] = zeros
                send_buf[t, key_heads + h, :, back] = zeros

        @pl.when(there > here)
        def _():
            @pl.loop(0, key_heads, unroll=2)
            def _(h):
                keys = kv_all[there, h]
                values = kv_all[there, key_heads + h]
                grad_keys, grad_values = over_groups(keys, values, h, back, False)
                send_buf[t, h] = grad_keys.astype(jnp.bfloat16)
                send_buf[t, key_heads + h] = grad_values.astype(jnp.bfloat16)

        copy(t).start()
        if t < chips:
            hop(t)

    @pl.loop(0, key_heads, unroll=2)
    def _(h):
        keys = kv_all[here, h]
        values = kv_all[here, key_heads + h]
        grad_keys, grad_values = over_groups(keys[:, front], values[:, front], h, every, True)
        grad_kv[h, :, front] = grad_keys
        grad_kv[key_heads + h, :, front] = grad_values
        grad_keys, grad_values = over_groups(keys[:, back], values[:, back], h, back, True)
        grad_kv[h, :, back] = grad_keys
        grad_kv[key_heads + h, :, back] = grad_values

    for t in range(1, count):
        copy(t).wait_recv()

        @pl.loop(0, 2 * key_heads)
        def _(h):
            grad_kv[h] += recv_buf[t, h].astype(jnp.float32)

    value = term(0)
    ring_copy(chips - 2).wait_recv()
    result[...] = value + in_sum[chips - 2].astype(jnp.float32)
    for t in range(1, count):
        copy(t).wait_send()
    for n in range(chips):
        near_copy(n).wait_send()
    for k in range(chips - 1):
        ring_copy(k).wait_send()


def attend_back_call(ident, q, kv_all, grad, att, sums, outs):
    count = lax.axis_size("ctx")
    heads, size, rows = q.shape
    kv_shape = kv_all.shape[1:]
    chips = outs.shape[0] // 2
    block = outs.shape[1:]
    groups = heads // (kv_shape[0] // 2)
    vmem = pl.BlockSpec(memory_space=pltpu.VMEM)
    dma = pltpu.SemaphoreType.DMA
    return pl.pallas_call(
        partial(attend_back_kernel, chips, count, groups),
        out_shape=[
            jax.ShapeDtypeStruct(q.shape, jnp.float32),
            jax.ShapeDtypeStruct(kv_shape, jnp.float32),
            jax.ShapeDtypeStruct(block, jnp.float32),
        ],
        in_specs=[vmem] * 5 + [pl.BlockSpec(memory_space=pl.ANY)],
        out_specs=[vmem] * 3,
        scratch_shapes=[
            pltpu.VMEM(sums.shape, jnp.float32),
            pltpu.VMEM(sums.shape, jnp.float32),
            pltpu.VMEM(kv_all.shape, jnp.bfloat16),
            pltpu.VMEM(kv_all.shape, jnp.bfloat16),
            pltpu.VMEM((chips,) + block, jnp.bfloat16),
            pltpu.VMEM((chips,) + block, jnp.bfloat16),
            pltpu.VMEM((chips - 1,) + block, jnp.bfloat16),
            pltpu.VMEM((chips - 1,) + block, jnp.bfloat16),
            dma((count,)),
            dma((count,)),
            dma((chips,)),
            dma((chips,)),
            dma((chips,)),
            dma((chips,)),
            dma((chips,)),
        ],
        compiler_params=pltpu.CompilerParams(
            collective_id=ident, has_side_effects=True, vmem_limit_bytes=40 * 2**20
        ),
        cost_estimate=pl.CostEstimate(flops=1, bytes_accessed=1, transcendentals=0),
    )(q, kv_all, grad, att, sums, outs)


def local(
    hidden_in,
    cotangent,
    norm_mix,
    in_proj,
    conv_kernel,
    out_proj,
    norm_ff1,
    gate1,
    up1,
    down1,
    norm_attn,
    q_proj,
    key_projection,
    value_projection,
    q_norm,
    k_norm,
    o_proj,
    norm_ff2,
    gate2,
    up2,
    down2,
):
    narrow_dtype = jnp.bfloat16
    start = hidden_in[0].astype(jnp.float32)
    token_rows = start.shape[0]
    block = token_rows // 2
    margin = KW - 1
    ctx_count = lax.axis_size("ctx")
    ctx_place = lax.axis_index("ctx")
    is_last = ctx_place == ctx_count - 1
    query_places = dealt_places(
        ctx_place * token_rows + jnp.arange(token_rows, dtype=jnp.int32), block, ctx_count
    )
    freqs = THETA ** (-jnp.arange(HEAD_SIZE // 2, dtype=jnp.float32) * 2.0 / HEAD_SIZE)
    angles = freqs[:, None] * query_places.astype(jnp.float32)[None, :]
    vectors = (
        norm_mix, norm_ff1, norm_attn, norm_ff2, q_norm, k_norm, conv_kernel.reshape(-1)
    )
    lengths = [one.shape[0] for one in vectors]
    vector = jnp.concatenate(vectors)
    vector = jnp.pad(vector, (0, 2048 - sum(lengths))).reshape(16, 128)
    attn_shard = jnp.concatenate([q_proj, key_projection, value_projection, o_proj], axis=0)
    attn_rows = attn_shard.shape[0]
    attn_slice = pick(attn_shard.reshape(ctx_count, -1, MODEL_WIDTH), ctx_place, 0)
    attn_slices = lax.all_gather(attn_slice, "fsdp", axis=0)
    tails = jnp.concatenate(
        [
            hidden_in[0, block - margin : block],
            hidden_in[0, token_rows - margin :],
            jnp.zeros((16 - 2 * margin, MODEL_WIDTH), narrow_dtype),
        ],
        axis=0,
    )
    mix_in, mix_out, given, gathered_vectors, edges = head_call(
        4, in_proj, out_proj, cotangent[0], vector, tails
    )
    edge_rows = jnp.concatenate(
        [
            jnp.where(ctx_place == 0, 0.0, edges[1, :margin]).astype(narrow_dtype),
            jnp.where(is_last, tails[:margin], edges[-1, margin : 2 * margin]),
            tails[2 * margin :],
        ],
        axis=0,
    )
    attn_slices, mix_in = lax.optimization_barrier((attn_slices, mix_in))
    attn_wholes = lax.all_gather(attn_slices, "ctx", axis=1)
    attn_wholes = attn_wholes.reshape(-1, attn_rows, MODEL_WIDTH)
    gathered_vectors = gathered_vectors.reshape(-1, 2048)
    wholes = []
    at = 0
    for one in lengths:
        wholes.append(gathered_vectors[:, at : at + one].reshape(-1))
        at += one
    mix_norm, ff_norm_one, attn_norm, ff_norm_two, query_gain, key_gain, mix_kernel = wholes
    mix_kernel = mix_kernel.reshape(-1, KW)
    kernel = mix_kernel.astype(jnp.float32)
    gain_one = mix_norm.astype(jnp.float32)
    normed_one, norm_back_one = jax.vjp(rms_scale, start, gain_one)
    normed_one_low = normed_one.astype(narrow_dtype)
    edges_low = rms_scale(edge_rows.astype(jnp.float32), gain_one).astype(narrow_dtype)
    projected_all = dot_rows(jnp.concatenate([normed_one_low, edges_low], axis=0), mix_in)
    projected = projected_all[:token_rows]
    edge_mixed = (
        projected_all[token_rows:, :MODEL_WIDTH] * projected_all[token_rows:, 2 * MODEL_WIDTH :]
    ).astype(narrow_dtype)
    b_part = projected[:, :MODEL_WIDTH]
    c_part = projected[:, MODEL_WIDTH : 2 * MODEL_WIDTH]
    x_part = projected[:, 2 * MODEL_WIDTH :]
    mixed_low = (b_part * x_part).astype(narrow_dtype)
    before_front = edge_mixed[:margin]
    before_back = edge_mixed[margin : 2 * margin]
    front_ext = jnp.concatenate([before_front, mixed_low[:block]], axis=0).astype(jnp.float32)
    back_ext = jnp.concatenate([before_back, mixed_low[block:]], axis=0).astype(jnp.float32)
    conv_out = jnp.concatenate(
        [conv_apply(front_ext, kernel), conv_apply(back_ext, kernel)], axis=0
    )
    gated_low = (c_part * conv_out).astype(narrow_dtype)
    first = start + dot_rows(gated_low, mix_out)
    normed_two, norm_back_two = jax.vjp(rms_scale, first, ff_norm_one.astype(jnp.float32))
    ff_out_one, inputs_one = ff_call(
        "forward", 1, normed_two.astype(narrow_dtype), gate1, up1, down1
    )
    one_low, ff_out_one = lax.optimization_barrier((normed_one_low, ff_out_one))
    one_blocks = lax.all_gather(one_low, "fsdp", axis=0)
    second = first + ff_out_one
    attn_parts = []
    at = 0
    for one in (q_proj, key_projection, value_projection, o_proj):
        attn_parts.append(attn_wholes[:, at : at + one.shape[0]].reshape(-1, MODEL_WIDTH))
        at += one.shape[0]
    w_query, w_key, w_value, w_output = attn_parts
    normed_three, norm_back_three = jax.vjp(rms_scale, second, attn_norm.astype(jnp.float32))
    three_low = normed_three.astype(narrow_dtype)
    query_raw = dot_rows(w_query, three_low)
    key_raw = dot_rows(w_key, three_low)
    value_raw = dot_rows(w_value, three_low)
    query_heads, query_back = jax.vjp(
        partial(head_prep, angles=angles), query_raw, query_gain.astype(jnp.float32)
    )
    key_heads, key_back = jax.vjp(
        partial(head_prep, angles=angles), key_raw, key_gain.astype(jnp.float32)
    )
    query_narrow = query_heads.astype(narrow_dtype)
    key_value = jnp.concatenate(
        [key_heads, value_raw.reshape(key_heads.shape)], axis=0
    ).astype(narrow_dtype)
    attended_low, exp_sums, key_value_all = attend_call(6, query_narrow, key_value)
    attended_flat = attended_low.reshape(-1, token_rows)
    third = second + lax.dot_general(
        attended_flat, w_output, (((0,), (1,)), ((), ())), preferred_element_type=jnp.float32
    )
    normed_four, norm_back_four = jax.vjp(rms_scale, third, ff_norm_two.astype(jnp.float32))
    four_low, one_blocks = lax.optimization_barrier((normed_four.astype(narrow_dtype), one_blocks))
    grad_four, two_grads, outs_two = ff_call("both", 2, four_low, gate2, up2, down2, given)
    shards = lax.axis_size("fsdp")
    ff_two = lax.psum(two_grads, "ctx")
    grad_final = cotangent[0].astype(jnp.float32)
    grad_third_part, grad_ff_norm_two = norm_back_four(grad_four)
    grad_third = grad_final + grad_third_part
    output_low = grad_third.astype(narrow_dtype)
    attended_gradient = lax.dot_general(
        w_output, output_low, (((0,), (1,)), ((), ())), preferred_element_type=jnp.float32
    )
    grad_w_output = (
        lax.dot_general(
            output_low, attended_flat, (((0,), (1,)), ((), ())), preferred_element_type=jnp.float32
        )
        .astype(narrow_dtype)
        .reshape(lax.axis_size("fsdp"), -1, MODEL_WIDTH)
    )
    grad_query, grad_key_value, ff_out_two = attend_back_call(
        7,
        query_narrow,
        key_value_all,
        attended_gradient.astype(narrow_dtype).reshape(query_narrow.shape),
        attended_low,
        exp_sums,
        outs_two,
    )
    final = third + ff_out_two
    key_count = grad_key_value.shape[0] // 2
    grad_query_raw, grad_query_gain = query_back(grad_query)
    raw_key_gradient, key_gain_gradient = key_back(grad_key_value[:key_count])
    query_grad_low = grad_query_raw.astype(narrow_dtype)
    key_grad_low = raw_key_gradient.astype(narrow_dtype)
    value_grad_low = grad_key_value[key_count:].astype(narrow_dtype).reshape(key_grad_low.shape)
    grad_three = (
        dot_cols(query_grad_low, w_query)
        + dot_cols(key_grad_low, w_key)
        + dot_cols(value_grad_low, w_value)
    )
    grad_rows = [
        one.reshape(shards, -1, token_rows) for one in (query_grad_low, key_grad_low, value_grad_low)
    ]
    widths = [one.shape[1] for one in grad_rows]
    grad_rows = jnp.concatenate(grad_rows, axis=1).reshape(-1, token_rows)
    grad_w_qkv = (
        dot_plain(grad_rows, three_low).astype(narrow_dtype).reshape(shards, sum(widths), -1)
    )
    grad_second_part, grad_attn_norm = norm_back_three(grad_three)
    grad_second = grad_third + grad_second_part
    grad_two, one_grads = ff_call(
        "backward", 3, grad_second.astype(narrow_dtype), gate1, up1, down1, inputs_one
    )
    grad_two, one_grads, ff_two = lax.optimization_barrier((grad_two, one_grads, ff_two))
    ff_one = lax.psum(one_grads, "ctx")
    ff_one, ff_two = [
        [
            one[at : at + gate1.shape[0]].astype(jnp.float32)
            for at in range(0, one.shape[0], gate1.shape[0])
        ]
        for one in (ff_one, ff_two)
    ]
    grad_first_part, grad_ff_norm_one = norm_back_two(grad_two)
    grad_first = grad_second + grad_first_part
    first_low = grad_first.astype(narrow_dtype)
    grad_gated = dot_plain(first_low, mix_out)
    grad_mix_out = (
        dot_cols(first_low, gated_low).astype(narrow_dtype).reshape(shards, -1, MODEL_WIDTH)
    )
    grad_c_part = grad_gated * conv_out
    grad_conv = grad_gated * c_part
    grad_front_ext = conv_input_grad(grad_conv[:block], kernel)
    grad_back_ext = conv_input_grad(grad_conv[block:], kernel)
    back_before = grad_back_ext[:margin]
    outgoing = jnp.concatenate(
        [grad_front_ext[:margin], jnp.where(is_last, 0.0, back_before)], axis=0
    )
    returned = extended_2(outgoing, (("ctx", 0),), margin)
    from_prev = returned[:margin]
    from_next = returned[returned.shape[0] - margin :]
    own_edge = jnp.where(is_last, back_before, 0.0)
    front_grad = grad_front_ext[margin:]
    back_grad = grad_back_ext[margin:]
    front_grad = jnp.concatenate(
        [front_grad[: block - margin], front_grad[block - margin :] + from_next + own_edge], axis=0
    )
    back_grad = jnp.concatenate(
        [back_grad[: block - margin], back_grad[block - margin :] + from_prev], axis=0
    )
    grad_mixed = jnp.concatenate([front_grad, back_grad], axis=0)
    grad_kernel = kernel_grad(front_ext, grad_conv[:block]) + kernel_grad(
        back_ext, grad_conv[block:]
    )
    grad_projected = jnp.concatenate(
        [grad_mixed * x_part, grad_c_part, grad_mixed * b_part], axis=-1
    ).astype(narrow_dtype)
    grad_one = dot_plain(grad_projected, mix_in)
    grad_start_part, grad_mix_norm = norm_back_one(grad_one)
    grad_start = grad_first + grad_start_part
    smalls = (
        grad_mix_norm,
        grad_kernel.reshape(-1),
        grad_ff_norm_one,
        grad_attn_norm,
        grad_query_gain,
        key_gain_gradient,
        grad_ff_norm_two,
    )
    pieces = [one.reshape(shards, -1) for one in smalls]
    sizes = [one.shape[1] for one in pieces]
    small = jnp.concatenate(pieces + [jnp.zeros((shards, 2048 - sum(sizes)), jnp.float32)], axis=1)
    grad_w_qkv, grad_w_output, grad_mix_out, grad_mix_in, small_sum = tail_call(
        5, [grad_w_qkv, grad_w_output, grad_mix_out], grad_projected, one_blocks,
        small.reshape(shards, 16, 128),
    )
    grad_w_query = grad_w_qkv[: widths[0]]
    grad_w_key = grad_w_qkv[widths[0] : widths[0] + widths[1]]
    grad_w_value = grad_w_qkv[widths[0] + widths[1] :]
    small_out = []
    at = 0
    for one in sizes:
        small_out.append(small_sum[at : at + one])
        at += one
    return (
        final.astype(narrow_dtype)[None],
        grad_start[None],
        small_out[0],
        grad_mix_in,
        small_out[1].reshape(-1, KW),
        grad_mix_out,
        small_out[2],
        ff_one[0],
        ff_one[1],
        ff_one[2],
        small_out[3],
        grad_w_query,
        grad_w_key,
        grad_w_value,
        small_out[4],
        small_out[5],
        grad_w_output,
        small_out[6],
        ff_two[0],
        ff_two[1],
        ff_two[2],
    )


def solution(mesh):
    in_specs = (
        P("fsdp", "ctx", None),
        P("fsdp", "ctx", None),
        P("fsdp"),
        P("fsdp", None),
        P("fsdp", None),
        P("fsdp", None),
        P("fsdp"),
        P("fsdp", None),
        P("fsdp", None),
        P("fsdp", None),
        P("fsdp"),
        P("fsdp", None),
        P("fsdp", None),
        P("fsdp", None),
        P("fsdp"),
        P("fsdp"),
        P("fsdp", None),
        P("fsdp"),
        P("fsdp", None),
        P("fsdp", None),
        P("fsdp", None),
    )
    out_specs = (
        P("fsdp", "ctx", None),
        P("fsdp", "ctx", None),
        P("fsdp"),
        P("fsdp", None),
        P("fsdp", None),
        P("fsdp", None),
        P("fsdp"),
        P("fsdp", None),
        P("fsdp", None),
        P("fsdp", None),
        P("fsdp"),
        P("fsdp", None),
        P("fsdp", None),
        P("fsdp", None),
        P("fsdp"),
        P("fsdp"),
        P("fsdp", None),
        P("fsdp"),
        P("fsdp", None),
        P("fsdp", None),
        P("fsdp", None),
    )
    return jax.shard_map(local, mesh=mesh, in_specs=in_specs, out_specs=out_specs, check_vma=False)
```
